128 devices in a mesh: section: 2 (over core), fsdp: 8 (over y, x_lo), ctx: 4 (over z), tp: 2 (over x_hi).
Axes of the slice: x: 4 (x_hi: 2, x_lo: 2; x = x_hi * 2 + x_lo), y: 4, z: 4, core: 2. Of those that a mesh axis runs over, the one named last changes fastest.
Arguments:
- layer_input: bfloat16 [2, 3072, 896], P(None, ('fsdp', 'ctx')), may hold values from -6 to 6
- cotangent: bfloat16 [2, 3072, 896], P(None, ('fsdp', 'ctx')), may hold values from -6 to 6
- doc_lengths: int32 [2, 8, 4], P(None, 'fsdp'), may hold values from 1 to 381, as said below
- attn_gain: bfloat16 [2, 896], P('section', 'fsdp'), may hold values from 0.5 to 1.5
- w_qkv: bfloat16 [2, 896, 2, 576], P('section', 'fsdp', 'tp'), may hold values from -0.1875 to 0.1875
- b_qkv: bfloat16 [2, 2, 576], P('section', 'tp', 'fsdp'), may hold values from -3 to 3
- w_out: bfloat16 [2, 896, 896], P('section', 'tp', 'fsdp'), may hold values from -1 to 1
- mlp_gain: bfloat16 [2, 896], P('section', 'fsdp'), may hold values from 0.5 to 1.5
- w_gate_up: bfloat16 [2, 896, 2, 4864], P('section', 'fsdp', None, 'tp'), may hold values from -0.1875 to 0.1875
- w_down: bfloat16 [2, 4864, 896], P('section', 'tp', 'fsdp'), may hold values from -0.15625 to 0.15625
Outputs:
- hidden_states: bfloat16 [2, 2, 3072, 896], P('section', None, ('fsdp', 'ctx'))
- input_grads: bfloat16 [2, 2, 3072, 896], P('section', None, ('fsdp', 'ctx'))
- grad_attn_gain: float32 [2, 896], P('section', 'fsdp')
- grad_w_qkv: float32 [2, 896, 2, 576], P('section', 'fsdp', 'tp')
- grad_b_qkv: float32 [2, 2, 512], P('section', 'tp', 'fsdp')
- grad_b_value: float32 [2, 2, 64], P('section', 'tp', 'fsdp')
- grad_w_out: float32 [2, 896, 896], P('section', 'tp', 'fsdp')
- grad_mlp_gain: float32 [2, 896], P('section', 'fsdp')
- grad_w_gate_up: float32 [2, 896, 2, 4864], P('section', 'fsdp', None, 'tp')
- grad_w_down: float32 [2, 4864, 896], P('section', 'tp', 'fsdp')
The draws below stay inside these ranges and needn't reach their ends.
Inputs may be any that keep to these rules, and one draw needn't show every extreme that they name: `doc_lengths`: in each pack the 4 lengths sum to 384, and one document of each pack holds more than 288 positions.
All inputs are finite; a program needn't handle non-finite values.
Results may differ from the reference program's by a relative error of at most 0.035.
Values may be sent and summed in bfloat16 or wider, within the bound.
No kernel may reach another device: no remote copies, remote signals or barrier semaphores. Data moves between devices by JAX's collectives and lax.ppermute only.
A program may use at most 192 MiB of HBM per device.

```python
import jax
import jax.numpy as jnp
from jax import lax

D = 896
HEADS = 14
KV = 2
HD = 64
FF = 4864
CTX_TOK = 96
M = 2
DOCS = 4
PACK = 384
PACKS = 8
TOKENS = 3072
GQ = 576


def draw_doc_lengths(key, part):
    key = jax.random.fold_in(key, 11)
    key_rest, key_share, key_slot, key_pick = jax.random.split(key, 4)
    cells = M * PACKS
    remaining = jax.random.randint(key_rest, (cells,), DOCS - 1, CTX_TOK)
    chosen = jax.random.randint(key_pick, (), 0, cells)
    remaining = jnp.where(jnp.arange(cells) == chosen, DOCS - 1, remaining)
    shares = jax.random.randint(key_share, (cells, DOCS - 1), 1, 65)
    spare = remaining - (DOCS - 1)
    pieces = 1 + spare[:, None] * shares // jnp.sum(shares, axis=1, keepdims=True)
    leftover = remaining - jnp.sum(pieces, axis=1)
    pieces = jnp.concatenate([pieces[:, :-1], pieces[:, -1:] + leftover[:, None]], axis=1)
    slot = jax.random.randint(key_slot, (cells,), 0, DOCS)
    longest = PACK - remaining
    columns = []
    for document in range(DOCS):
        shifted = jnp.clip(document - (document > slot).astype(jnp.int32), 0, DOCS - 2)
        shorter = jnp.take_along_axis(pieces, shifted[:, None], axis=1)[:, 0]
        columns.append(jnp.where(slot == document, longest, shorter))
    return jnp.stack(columns, axis=1).reshape(M, PACKS, DOCS).astype(jnp.int32)


def level_of(own_key, shape, cuts, smallest, high):
    loudness, own = 1.0, jax.random.fold_in(own_key, 6)
    for axis_at, shards_of in cuts:
        draws = jnp.exp(jax.random.uniform(jax.random.fold_in(own, axis_at), (shards_of,), jnp.float32, smallest / len(cuts), high / len(cuts)))
        loudness = loudness * jnp.repeat(draws, shape[axis_at] // shards_of).reshape([-1 if axis == axis_at else 1 for axis in range(len(shape))])
    return loudness


def gaussian(key, extent, width, reach, cuts=(), kind=jnp.bfloat16):
    loudness = level_of(key, extent, cuts, -0.22, 0.18) if cuts else 1.0
    result = jax.random.normal(key, extent, jnp.float32) * width * loudness
    return jnp.minimum(jnp.maximum(result, -reach), reach).astype(kind)


def setup_inputs(seed: int = 0) -> dict:
    arg_keys = jax.random.split(jax.random.key(seed), 11)
    layer_input = gaussian(arg_keys[0], (M, TOKENS, D), 1.0, 6.0, ((1, 32),))
    cotangent = gaussian(arg_keys[1], (M, TOKENS, D), 1.0, 6.0, ((1, 32),))
    doc_lengths = draw_doc_lengths(jax.random.fold_in(arg_keys[10], 71), 0)
    attn_gain = jnp.clip(1.0 + 0.1 * jax.random.normal(arg_keys[3], (2, D), jnp.float32), 0.5, 1.5).astype(jnp.bfloat16)
    w_qkv = gaussian(arg_keys[4], (2, D, KV, GQ), D ** -0.5, 0.1875, ((0, 2), (1, 8), (2, 2)))
    b_qkv = gaussian(arg_keys[5], (2, KV, GQ), 0.5, 3.0, ((0, 2), (1, 2), (2, 8)))
    w_out = gaussian(arg_keys[6], (2, HEADS * HD, D), (HD // 2) ** -0.5, 1.0, ((0, 2), (1, 2), (2, 8)))
    mlp_gain = jnp.clip(1.0 + 0.1 * jax.random.normal(arg_keys[7], (2, D), jnp.float32), 0.5, 1.5).astype(jnp.bfloat16)
    w_gate_up = gaussian(arg_keys[8], (2, D, 2, FF), D ** -0.5, 0.1875, ((0, 2), (1, 8), (3, 2)))
    w_down = gaussian(arg_keys[9], (2, FF, D), (FF // 3) ** -0.5, 0.15625, ((0, 2), (1, 2), (2, 8)))
    return {"layer_input": layer_input, "cotangent": cotangent, "doc_lengths": doc_lengths, "attn_gain": attn_gain, "w_qkv": w_qkv, "b_qkv": b_qkv, "w_out": w_out, "mlp_gain": mlp_gain, "w_gate_up": w_gate_up, "w_down": w_down}


@jax.custom_vjp
def low(v):
    return lax.optimization_barrier(v.astype(jnp.bfloat16)).astype(jnp.float32)

@jax.custom_vjp
def low_back(v):
    return v

def low_keep(v):
    return (low(v), None)

def low_pass(kept, grad):
    return (grad,)

def back_keep(v):
    return (v, None)

def back_low(kept, grad):
    return (low(grad),)
low.defvjp(low_keep, low_pass)
low_back.defvjp(back_keep, back_low)
epsilon = 1e-06
rope_base = 1000000.0
masked_score = -1000000000.0
highest = lax.Precision.HIGHEST

def pack_tables(lengths):
    doc_ends = jnp.cumsum(lengths, axis=-1).astype(jnp.int32)
    places = jnp.arange(PACK, dtype=jnp.int32)
    passed = places[:, None] >= doc_ends[..., None, :]
    segment = lax.optimization_barrier(jnp.sum(passed.astype(jnp.int32), axis=-1)).astype(jnp.int32)
    doc_start = lax.optimization_barrier(jnp.sum(jnp.where(passed, lengths[..., None, :], 0), axis=-1)).astype(jnp.int32)
    return (segment, places - doc_start)

def rotary_tables(position):
    inverse = rope_base ** (-jnp.arange(0, HD, 2, dtype=jnp.float32) / HD)
    angles = position.astype(jnp.float32)[..., None] * inverse
    angles = jnp.concatenate([angles, angles], axis=-1)
    return (jnp.cos(angles), jnp.sin(angles))

def rotate(values, cosine, sine):
    half_width = values.shape[-1] // 2
    turned = jnp.concatenate([-values[..., half_width:], values[..., :half_width]], axis=-1)
    return values * cosine + turned * sine

def rms_normed(resid, gain):
    return resid * lax.rsqrt(lax.optimization_barrier(jnp.mean(resid * resid, axis=-1, keepdims=True)) + epsilon) * gain

def attend_pack(pieces):
    pack_queries, pack_keys, pack_values, pack_segment = pieces
    scores = jnp.einsum('qkgd,tkd->kgqt', pack_queries, pack_keys, precision=highest) * 0.125
    scores = low_back(scores)
    places = jnp.arange(PACK, dtype=jnp.int32)
    allowed = (pack_segment[:, None] == pack_segment[None, :]) & (places[:, None] >= places[None, :])
    scores = jnp.where(allowed, scores, masked_score)
    probs_low = low(jax.nn.softmax(scores, axis=-1))
    return jnp.einsum('kgqt,tkd->qkgd', probs_low, pack_values, precision=highest)

def block_layer(resid, weights, segment, cosine, sine):
    attn_gain, w_qkv, b_qkv, w_out, mlp_gain, w_gate_up, w_down = weights
    row_count = resid.shape[0]
    group_size = HEADS // KV
    query_width = group_size * HD
    normed_in = low(rms_normed(resid, attn_gain))
    projected = low_back(jnp.einsum('rd,dkc->rkc', normed_in, w_qkv, precision=highest) + b_qkv)
    queries = rotate(projected[..., :query_width].reshape(row_count, KV, group_size, HD), cosine[:, None, None, :], sine[:, None, None, :])
    key_heads = rotate(projected[..., query_width:query_width + HD], cosine[:, None, :], sine[:, None, :])
    value_heads = projected[..., query_width + HD:]
    queries = low(queries)
    key_heads = low(key_heads)
    value_heads = low(value_heads)
    pack_count = row_count // PACK
    mixed = lax.map(jax.checkpoint(attend_pack), (queries.reshape(pack_count, PACK, KV, group_size, HD), key_heads.reshape(pack_count, PACK, KV, HD), value_heads.reshape(pack_count, PACK, KV, HD), segment))
    mixed = low_back(low(mixed.reshape(row_count, HEADS * HD)))
    middle = resid + low_back(jnp.dot(mixed, w_out, precision=highest))
    normed_mid = low(rms_normed(middle, mlp_gain))
    gate_up = low_back(jnp.einsum('rd,dcf->rcf', normed_mid, w_gate_up, precision=highest))
    hidden = low(jax.nn.silu(gate_up[:, 0]) * gate_up[:, 1])
    return middle + low_back(jnp.dot(hidden, w_down, precision=highest))

def reference(layer_input, cotangent, doc_lengths, attn_gain, w_qkv, b_qkv, w_out, mlp_gain, w_gate_up, w_down):
    total_rows = M * TOKENS
    segment, position = pack_tables(doc_lengths)
    segment = segment.reshape(M * PACKS, PACK)
    cosine, sine = rotary_tables(position.reshape(total_rows))
    params = (attn_gain, w_qkv, b_qkv, w_out, mlp_gain, w_gate_up, w_down)
    lower_weights = tuple((param[0].astype(jnp.float32) for param in params))
    upper_weights = tuple((param[1].astype(jnp.float32) for param in params))

    def apply_layer(resid, *weights):
        return block_layer(resid, weights, segment, cosine, sine)
    start_rows = layer_input.reshape(total_rows, D).astype(jnp.float32)
    first_out, lower_back = jax.vjp(apply_layer, start_rows, *lower_weights)
    first_out = low(first_out)
    second_out, upper_back = jax.vjp(apply_layer, first_out, *upper_weights)
    upper_grads = upper_back(cotangent.reshape(total_rows, D).astype(jnp.float32))
    middle_grad = low(upper_grads[0])
    lower_grads = lower_back(middle_grad)
    hidden_states = jnp.stack([first_out, second_out]).reshape(2, M, TOKENS, D).astype(jnp.bfloat16)
    input_grads = jnp.stack([lower_grads[0], middle_grad]).reshape(2, M, TOKENS, D).astype(jnp.bfloat16)
    stacked = [jnp.stack([former, latter]) for former, latter in zip(lower_grads[1:], upper_grads[1:])]
    bias_grad = stacked[2]
    return (hidden_states, input_grads, stacked[0], stacked[1], bias_grad[..., :GQ - HD], bias_grad[..., GQ - HD:], stacked[3], stacked[4], stacked[5], stacked[6])
```

```python
import jax
import jax.numpy as jnp
from jax import lax
from jax.sharding import PartitionSpec as P

HD = 64
UNITS = 640

epsilon = 1e-06
rope_base = 1000000.0
masked_score = -1000000000.0
low_type = jnp.bfloat16
wide = jnp.float32


def contract(left, right, left_dim, right_dim):
    return lax.dot_general(
        left, right, (((left_dim,), (right_dim,)), ((), ())), preferred_element_type=wide
    )


def turn(value, axis, steps):
    count = lax.axis_size(axis)
    return lax.ppermute(value, axis, [(place, (place + steps) % count) for place in range(count)])


def turn_y(value, steps):
    count = lax.axis_size("fsdp")
    return lax.ppermute(
        value, "fsdp", [(place, (place + 2 * steps) % count) for place in range(count)]
    )


def flip_x(value):
    count = lax.axis_size("fsdp")
    return lax.ppermute(value, "fsdp", [(place, place ^ 1) for place in range(count)])


def turn_in_section(value, section, axis, steps):
    count = lax.axis_size(axis)
    base = section * count
    return lax.ppermute(
        value,
        ("section", axis),
        [(base + place, base + (place + steps) % count) for place in range(count)],
    )


def spread(block, axis):
    count = lax.axis_size(axis)
    order = [1, count - 1] + list(range(2, count - 1))
    moved = {steps: turn(block, axis, steps) for steps in order}
    return [block] + [moved[steps] for steps in range(1, count)]


def collect(blocks, axis):
    count = lax.axis_size(axis)
    order = [1, count - 1] + list(range(2, count - 1))
    total = blocks[0].astype(wide)
    for steps in order:
        total = total + turn(blocks[steps], axis, -steps).astype(wide)
    return total


def tensor_sum(partial_value):
    own = lax.optimization_barrier(partial_value.astype(low_type))
    return own.astype(wide) + turn(own, "tp", 1).astype(wide)


def gather_rows(block, row_place, column_place):
    rows, columns = block.shape
    pair = jnp.zeros((2, rows, columns), block.dtype)
    pair = lax.dynamic_update_slice(pair, block[None], (column_place, 0, 0))
    pair = lax.dynamic_update_slice(pair, flip_x(block)[None], (1 - column_place, 0, 0))
    whole = jnp.zeros((4, 2, rows, columns), block.dtype)
    whole = lax.dynamic_update_slice(whole, pair[None], (row_place, 0, 0, 0))
    for steps in (1, 3, 2):
        whole = lax.dynamic_update_slice(
            whole, turn_y(pair, steps)[None], ((row_place - steps) % 4, 0, 0, 0)
        )
    return whole


def both_layers(own, section_place):
    other = turn(own, "section", 1)
    first = section_place == 0
    return jnp.where(first, own, other), jnp.where(first, other, own)


def rotary_tables(position):
    inverse = rope_base ** (-jnp.arange(0, HD, 2, dtype=wide) / HD)
    angles = position.astype(wide)[..., None] * inverse
    angles = jnp.concatenate([angles, angles], axis=-1)
    return (jnp.cos(angles), jnp.sin(angles))


def rotate(values, cosine, sine):
    half_width = values.shape[-1] // 2
    turned = jnp.concatenate([-values[..., half_width:], values[..., :half_width]], axis=-1)
    return values * cosine + turned * sine


def rotate_back(grads, cosine, sine):
    half_width = grads.shape[-1] // 2
    scaled = grads * sine
    turned = jnp.concatenate([scaled[..., half_width:], -scaled[..., :half_width]], axis=-1)
    return grads * cosine + turned


def norm_backward(grad_normed, resid, scale, gain):
    grad_gain = jnp.sum(grad_normed * resid * scale, axis=0)
    inner = grad_normed * gain
    grad_resid = scale * inner - resid * (scale * scale * scale) * jnp.mean(
        inner * resid, axis=-1, keepdims=True
    )
    return (grad_gain, grad_resid)


def mask_tables(lengths, ctx_place, row_count, ctx_count):
    doc_ends = jnp.cumsum(lengths, axis=-1)
    blocks = (ctx_place - jnp.arange(ctx_count, dtype=jnp.int32)) % ctx_count
    places = (blocks[:, None] * row_count + jnp.arange(row_count, dtype=jnp.int32)).reshape(-1)
    passed = places[:, None] >= doc_ends[None, :]
    segment = jnp.sum(passed.astype(jnp.int32), axis=-1)
    doc_start = jnp.sum(jnp.where(passed, lengths[None, :], 0), axis=-1)
    position = places - doc_start
    cosine, sine = rotary_tables(position[:row_count])
    allowed = (segment[:row_count, None] == segment[None, :]) & (
        places[:row_count, None] >= places[None, :]
    )
    return (allowed, cosine, sine)


def forward_layer(layer_in, weights, tables):
    attn_gain, mlp_gain, bias, w_attn, w_mlp = weights
    allowed, cosine, sine = tables
    row_count, width = layer_in.shape
    resid = layer_in.astype(wide)
    scale_one = lax.rsqrt(jnp.mean(resid * resid, axis=-1, keepdims=True) + epsilon)
    normed_in = (resid * scale_one * attn_gain).astype(low_type)
    projected = jnp.dot(normed_in, w_attn[:, :640], preferred_element_type=wide) + bias
    queries = rotate(
        projected[:, :448].reshape(row_count, 7, HD), cosine[:, None, :], sine[:, None, :]
    ).astype(low_type)
    key_own = rotate(projected[:, 448:512], cosine, sine).astype(low_type)
    value_own = projected[:, 512:576].astype(low_type)
    key_value = jnp.concatenate(
        spread(jnp.concatenate([key_own, value_own], axis=1), "ctx"), axis=0
    )
    key_all, value_all = key_value[:, :HD], key_value[:, HD:]
    scores = jnp.einsum("qgd,td->gqt", queries, key_all, preferred_element_type=wide) * 0.125
    scores = jnp.where(allowed[None], scores, masked_score)
    largest = jnp.max(scores, axis=-1, keepdims=True)
    raised = jnp.exp(scores - largest)
    totals = jnp.sum(raised, axis=-1, keepdims=True)
    log_total = largest + jnp.log(totals)
    probs = (raised / totals).astype(low_type)
    mixed = jnp.einsum("gqt,td->qgd", probs, value_all, preferred_element_type=wide)
    mixed = jnp.pad(mixed.reshape(row_count, 448).astype(low_type), ((0, 0), (64, 0)))
    middle = resid + tensor_sum(contract(mixed, w_attn[:, 512:], 1, 1))
    scale_two = lax.rsqrt(jnp.mean(middle * middle, axis=-1, keepdims=True) + epsilon)
    normed_mid = jnp.concatenate(
        spread((middle * scale_two * mlp_gain).astype(low_type), "ctx"), axis=0
    )
    gate_up = jnp.dot(normed_mid, w_mlp[:, : 2 * UNITS], preferred_element_type=wide)
    hidden = (jax.nn.silu(gate_up[:, :UNITS]) * gate_up[:, UNITS:]).astype(low_type)
    branch = contract(hidden, w_mlp[:, 2 * UNITS :], 1, 1).astype(low_type)
    branch = branch.reshape(-1, row_count, width)
    layer_out = middle + tensor_sum(collect(list(branch), "ctx"))
    kept = (
        resid,
        scale_one,
        normed_in,
        queries,
        key_all,
        value_all,
        log_total,
        mixed,
        middle,
        scale_two,
        normed_mid,
        gate_up,
        hidden,
    )
    return (layer_out.astype(low_type), kept)


def backward_layer(grad_out, kept, weights, tables):
    attn_gain, mlp_gain, bias, w_attn, w_mlp = weights
    allowed, cosine, sine = tables
    (
        resid,
        scale_one,
        normed_in,
        queries,
        key_all,
        value_all,
        log_total,
        mixed,
        middle,
        scale_two,
        normed_mid,
        gate_up,
        hidden,
    ) = kept
    row_count, width = resid.shape
    grad_all = jnp.concatenate(spread(grad_out, "ctx"), axis=0)
    grad_hidden = jnp.dot(grad_all, w_mlp[:, 2 * UNITS :], preferred_element_type=wide)
    gate = gate_up[:, :UNITS]
    upward = gate_up[:, UNITS:]
    sigmoid = jax.nn.sigmoid(gate)
    grad_gate = grad_hidden * upward * sigmoid * (1.0 + gate * (1.0 - sigmoid))
    grad_upward = grad_hidden * gate * sigmoid
    grad_gate_up = jnp.concatenate([grad_gate, grad_upward], axis=1).astype(low_type)
    branch = contract(grad_gate_up, w_mlp[:, : 2 * UNITS], 1, 1).astype(low_type)
    branch = branch.reshape(-1, row_count, width)
    grad_normed_mid = tensor_sum(collect(list(branch), "ctx"))
    grad_mlp = jnp.concatenate(
        [
            contract(normed_mid, grad_gate_up, 0, 0).astype(low_type),
            contract(grad_all, hidden, 0, 0).astype(low_type),
        ],
        axis=1,
    )
    grad_mlp_gain, grad_middle = norm_backward(grad_normed_mid, middle, scale_two, mlp_gain)
    grad_middle = grad_middle + grad_out.astype(wide)
    grad_branch = grad_middle.astype(low_type)
    grad_mixed = jnp.dot(grad_branch, w_attn[:, 512:], preferred_element_type=wide)
    grad_mixed = grad_mixed[:, 64:].astype(low_type).reshape(queries.shape)
    scores = jnp.einsum("qgd,td->gqt", queries, key_all, preferred_element_type=wide) * 0.125
    probs = jnp.where(allowed[None], jnp.exp(scores - log_total), 0.0)
    grad_probs = jnp.einsum("qgd,td->gqt", grad_mixed, value_all, preferred_element_type=wide)
    grad_value_all = jnp.einsum(
        "gqt,qgd->td", probs.astype(low_type), grad_mixed, preferred_element_type=wide
    )
    row_delta = jnp.sum(grad_probs * probs, axis=-1, keepdims=True)
    grad_scores = (probs * (grad_probs - row_delta)).astype(low_type)
    grad_queries = (
        jnp.einsum("gqt,td->qgd", grad_scores, key_all, preferred_element_type=wide) * 0.125
    )
    grad_key_all = (
        jnp.einsum("gqt,qgd->td", grad_scores, queries, preferred_element_type=wide) * 0.125
    )
    grad_key_value = jnp.concatenate([grad_key_all, grad_value_all], axis=1).astype(low_type)
    grad_key_value = collect(list(grad_key_value.reshape(-1, row_count, 2 * HD)), "ctx")
    grad_projected = jnp.concatenate(
        [
            rotate_back(grad_queries, cosine[:, None, :], sine[:, None, :]).reshape(row_count, 448),
            rotate_back(grad_key_value[:, :HD], cosine, sine),
            grad_key_value[:, HD:],
            jnp.zeros((row_count, HD), wide),
        ],
        axis=1,
    ).astype(low_type)
    grad_normed_in = tensor_sum(contract(grad_projected, w_attn[:, :640], 1, 1))
    grad_attn_gain, grad_resid = norm_backward(grad_normed_in, resid, scale_one, attn_gain)
    grad_bias = jnp.sum(grad_projected.astype(wide), axis=0)
    grad_attn = jnp.concatenate(
        [
            contract(normed_in, grad_projected[:, :576], 0, 0).astype(low_type),
            contract(grad_branch, mixed[:, 64:], 0, 0).astype(low_type),
        ],
        axis=1,
    )
    small = (grad_attn_gain, grad_mlp_gain, grad_bias)
    return ((grad_resid + grad_middle).astype(low_type), grad_mlp, grad_attn, small)


def pick(array, place, axis):
    return lax.dynamic_index_in_dim(array, place, axis, keepdims=False)


def halve(blocks, section_place):
    sent = turn(pick(blocks, 1 - section_place, 1), "section", 1)
    return (pick(blocks, section_place, 1).astype(wide) + sent.astype(wide)).astype(low_type)


def sum_rows(blocks, row_place):
    total = pick(blocks, row_place, 0).astype(wide)
    for steps in (1, 3, 2):
        total = total + turn_y(pick(blocks, (row_place + steps) % 4, 0), steps).astype(wide)
    return total.astype(low_type)


def sum_columns(block, layer, column_place):
    hops = []
    for row in range(4):
        hops.append((8 + 2 * row, 8 + 2 * row + 1))
        hops.append((2 * row + 1, 2 * row))
    total = block.astype(wide) + lax.ppermute(block, ("section", "fsdp"), hops).astype(wide)
    total = total.astype(low_type)
    other = 1 - layer
    hops = [(8 * other + 2 * row + other, 8 * layer + 2 * row + other) for row in range(4)]
    return jnp.where(
        column_place == layer, total, lax.ppermute(total, ("section", "fsdp"), hops)
    )


def spread_in_section(block, layer, ctx_place):
    whole = jnp.zeros((4,) + block.shape, block.dtype)
    start = (0,) * block.ndim
    whole = lax.dynamic_update_slice(whole, block[None], (ctx_place,) + start)
    for steps in (1, 3, 2):
        whole = lax.dynamic_update_slice(
            whole,
            turn_in_section(block, layer, "ctx", steps)[None],
            ((ctx_place - steps) % 4,) + start,
        )
    return whole


def reduce_mlp(grad, layer, places):
    section_place, row_place, column_place, ctx_place = places
    blocks = halve(grad.reshape(4, 2, 112, 3 * UNITS), section_place)
    block = sum_columns(sum_rows(blocks, row_place), layer, column_place)
    return spread_in_section(block, layer, ctx_place)


def reduce_attn(grad, small, layer, places):
    section_place, row_place, column_place, ctx_place = places
    grad_attn_gain, grad_mlp_gain, grad_bias = small
    lines = jnp.concatenate(
        [
            jnp.pad(grad_attn_gain.reshape(8, 112), ((0, 0), (0, 16))),
            jnp.pad(grad_mlp_gain.reshape(8, 112), ((0, 0), (0, 16))),
            jnp.pad(grad_bias[:512].reshape(8, 64), ((0, 0), (0, 64))),
            jnp.pad(grad_bias[512:576].reshape(8, 8), ((0, 0), (0, 632))),
        ],
        axis=1,
    ).astype(low_type)
    lines = jnp.pad(lines[:, None], ((0, 0), (0, 15), (0, 0)))
    blocks = jnp.concatenate([grad.reshape(8, 112, 1024), lines], axis=1)
    blocks = halve(blocks.reshape(4, 2, 128, 1024), section_place)
    quarter = lambda place: lax.dynamic_slice_in_dim(blocks, place * 256, 256, 2)
    blocks = collect([quarter((ctx_place - steps) % 4) for steps in range(4)], "ctx")
    block = sum_columns(sum_rows(blocks.astype(low_type), row_place), layer, column_place)
    return spread_in_section(block, layer, ctx_place)


def per_device(
    layer_input, cotangent, doc_lengths, attn_gain, w_qkv, b_qkv, w_out, mlp_gain, w_gate_up, w_down
):
    section_place = lax.axis_index("section")
    fsdp_place = lax.axis_index("fsdp")
    row_place, column_place = fsdp_place // 2, fsdp_place % 2
    ctx_place = lax.axis_index("ctx")
    places = (section_place, row_place, column_place, ctx_place)
    row_count, width = layer_input.shape[1:]
    units_all = w_down.shape[1]

    line = jnp.concatenate(
        [
            jnp.pad(attn_gain, ((0, 0), (0, 16))),
            jnp.pad(mlp_gain, ((0, 0), (0, 16))),
            jnp.pad(b_qkv[0], ((0, 0), (0, 696))),
        ],
        axis=1,
    )
    attn_block = jnp.concatenate(
        [
            jnp.concatenate([w_qkv[0, :, 0], w_out[0].T], axis=1),
            jnp.pad(line, ((0, 15), (0, 0))),
        ],
        axis=0,
    )
    past = 4 * UNITS - units_all
    mlp_block = jnp.concatenate(
        [
            jnp.pad(w_gate_up[0], ((0, 0), (0, 0), (0, past))),
            jnp.pad(w_down[0].T, ((0, 0), (0, past)))[:, None],
        ],
        axis=1,
    )
    mlp_block = lax.dynamic_slice_in_dim(mlp_block, ctx_place * UNITS, UNITS, 2)
    mlp_block = mlp_block.reshape(112, 3 * UNITS)

    attn_whole = gather_rows(attn_block, row_place, column_place).reshape(8, 128, 1024)
    w_mlp = gather_rows(mlp_block, row_place, column_place).reshape(width, 3 * UNITS)
    attn_pair = both_layers(attn_whole, section_place)
    mlp_pair = both_layers(w_mlp, section_place)
    weights = []
    for attn, mlp in zip(attn_pair, mlp_pair):
        lines = attn[:, 112].astype(wide)
        weights.append(
            (
                lines[:, :112].reshape(width),
                lines[:, 128:240].reshape(width),
                jnp.pad(lines[:, 256:328].reshape(576), (0, 64)),
                attn[:, :112].reshape(width, 1024),
                mlp,
            )
        )

    tables = mask_tables(pick(doc_lengths, section_place, 0)[0], ctx_place, row_count, 4)
    rows = pick(layer_input, section_place, 0)
    outputs, kept_all = [], []
    for layer in range(2):
        rows, kept = forward_layer(rows, weights[layer], tables)
        outputs.append(rows)
        kept_all.append(kept)
    grads = pick(cotangent, section_place, 0)
    grads_back, mlp_grads, attn_grads = [None, None], [None, None], [None, None]
    for layer in (1, 0):
        grads, grad_mlp, grad_attn, small = backward_layer(
            grads, kept_all[layer], weights[layer], tables
        )
        grads_back[layer] = grads
        mlp_grads[layer] = reduce_mlp(grad_mlp, layer, places)
        attn_grads[layer] = reduce_attn(grad_attn, small, layer, places)

    first = section_place == 0

    def by_layer(values):
        own = jnp.where(first, values[0], values[1])
        other = turn(jnp.where(first, values[1], values[0]), "section", 1)
        return jnp.where(first, jnp.stack([own, other]), jnp.stack([other, own]))[None]

    hidden_states = by_layer(outputs)
    input_grads = by_layer(grads_back)
    mlp = jnp.where(first, mlp_grads[0], mlp_grads[1]).reshape(4, 112, 3, UNITS)
    attn = jnp.where(first, attn_grads[0], attn_grads[1])
    attn = attn.transpose(1, 0, 2).reshape(128, 1024).astype(wide)
    gate_up = mlp[:, :, :2].transpose(1, 2, 0, 3).reshape(112, 2, 4 * UNITS)[:, :, :units_all]
    down = mlp[:, :, 2].transpose(0, 2, 1).reshape(4 * UNITS, 112)[:units_all]
    lines = attn[112:113]
    return (
        hidden_states,
        input_grads,
        lines[:, :112],
        attn[None, :112, None, :576],
        lines[None, :, 256:320],
        lines[None, :, 384:392],
        attn[:112, 576:].T[None],
        lines[:, 128:240],
        gate_up.astype(wide)[None],
        down.astype(wide)[None],
    )


def solution(mesh):
    return jax.shard_map(
        per_device,
        mesh=mesh,
        in_specs=(
            P(None, ("fsdp", "ctx"), None),
            P(None, ("fsdp", "ctx"), None),
            P(None, "fsdp", None),
            P("section", "fsdp"),
            P("section", "fsdp", "tp", None),
            P("section", "tp", "fsdp"),
            P("section", "tp", "fsdp"),
            P("section", "fsdp"),
            P("section", "fsdp", None, "tp"),
            P("section", "tp", "fsdp"),
        ),
        out_specs=(
            P("section", None, ("fsdp", "ctx"), None),
            P("section", None, ("fsdp", "ctx"), None),
            P("section", "fsdp"),
            P("section", "fsdp", "tp", None),
            P("section", "tp", "fsdp"),
            P("section", "tp", "fsdp"),
            P("section", "tp", "fsdp"),
            P("section", "fsdp"),
            P("section", "fsdp", None, "tp"),
            P("section", "tp", "fsdp"),
        ),
        check_vma=False,
    )
```

```python
import jax
import jax.numpy as jnp
from jax import lax
from jax.sharding import PartitionSpec as P

HD = 64
UNITS = 640

epsilon = 1e-06
rope_base = 1000000.0
masked_score = -1000000000.0
low_type = jnp.bfloat16
wide = jnp.float32


def contract(left, right, left_dim, right_dim):
    return lax.dot_general(
        left, right, (((left_dim,), (right_dim,)), ((), ())), preferred_element_type=wide
    )


def turn(value, axis, steps):
    count = lax.axis_size(axis)
    return lax.ppermute(value, axis, [(place, (place + steps) % count) for place in range(count)])


def turn_y(value, steps):
    count = lax.axis_size("fsdp")
    return lax.ppermute(
        value, "fsdp", [(place, (place + 2 * steps) % count) for place in range(count)]
    )


def flip_x(value):
    count = lax.axis_size("fsdp")
    return lax.ppermute(value, "fsdp", [(place, place ^ 1) for place in range(count)])


def spread(block, axis):
    count = lax.axis_size(axis)
    order = [1, count - 1] + list(range(2, count - 1))
    moved = {steps: turn(block, axis, steps) for steps in order}
    return [block] + [moved[steps] for steps in range(1, count)]


def collect(blocks, axis):
    count = lax.axis_size(axis)
    order = [1, count - 1] + list(range(2, count - 1))
    total = blocks[0].astype(wide)
    for steps in order:
        total = total + turn(blocks[steps], axis, -steps).astype(wide)
    return total


def tensor_sum(partial_value):
    own = lax.optimization_barrier(partial_value.astype(low_type))
    return own.astype(wide) + turn(own, "tp", 1).astype(wide)


def after(value, *others):
    tied = lax.optimization_barrier((value,) + others)
    return tied[0] if not others else tied


def gather_halves(half, row_place, column_place, section_place):
    rows, columns = half.shape
    pair = jnp.zeros((2, rows, columns), half.dtype)
    pair = lax.dynamic_update_slice(pair, half[None], (column_place, 0, 0))
    pair = lax.dynamic_update_slice(pair, flip_x(half)[None], (1 - column_place, 0, 0))
    part = jnp.zeros((4, 2, rows, columns), half.dtype)
    part = lax.dynamic_update_slice(part, pair[None], (row_place, 0, 0, 0))
    for steps in (1, 3, 2):
        part = lax.dynamic_update_slice(
            part, turn_y(pair, steps)[None], ((row_place - steps) % 4, 0, 0, 0)
        )
    part = part.reshape(8, rows, columns)
    other = turn(part, "section", 1)
    first = section_place == 0
    return jnp.concatenate([jnp.where(first, part, other), jnp.where(first, other, part)], axis=2)


def halves_by_layer(block, section_place):
    columns = block.shape[1] // 2
    kept = lax.dynamic_slice_in_dim(block, section_place * columns, columns, 1)
    sent = lax.dynamic_slice_in_dim(block, (1 - section_place) * columns, columns, 1)
    received = turn(sent, "section", 1)
    first = section_place == 0
    return jnp.where(first, kept, received), jnp.where(first, received, kept)


def rotary_tables(position):
    inverse = rope_base ** (-jnp.arange(0, HD, 2, dtype=wide) / HD)
    angles = position.astype(wide)[..., None] * inverse
    angles = jnp.concatenate([angles, angles], axis=-1)
    return (jnp.cos(angles), jnp.sin(angles))


def rotate(values, cosine, sine):
    half_width = values.shape[-1] // 2
    turned = jnp.concatenate([-values[..., half_width:], values[..., :half_width]], axis=-1)
    return values * cosine + turned * sine


def rotate_back(grads, cosine, sine):
    half_width = grads.shape[-1] // 2
    scaled = grads * sine
    turned = jnp.concatenate([scaled[..., half_width:], -scaled[..., :half_width]], axis=-1)
    return grads * cosine + turned


def norm_backward(grad_normed, resid, scale, gain):
    grad_gain = jnp.sum(grad_normed * resid * scale, axis=0)
    inner = grad_normed * gain
    grad_resid = scale * inner - resid * (scale * scale * scale) * jnp.mean(
        inner * resid, axis=-1, keepdims=True
    )
    return (grad_gain, grad_resid)


def mask_tables(lengths, ctx_place, row_count, ctx_count):
    doc_ends = jnp.cumsum(lengths, axis=-1)
    blocks = (ctx_place - jnp.arange(ctx_count, dtype=jnp.int32)) % ctx_count
    places = (blocks[:, None] * row_count + jnp.arange(row_count, dtype=jnp.int32)).reshape(-1)
    passed = places[:, None] >= doc_ends[None, :]
    segment = jnp.sum(passed.astype(jnp.int32), axis=-1)
    doc_start = jnp.sum(jnp.where(passed, lengths[None, :], 0), axis=-1)
    position = places - doc_start
    cosine, sine = rotary_tables(position[:row_count])
    allowed = (segment[:row_count, None] == segment[None, :]) & (
        places[:row_count, None] >= places[None, :]
    )
    return (allowed, cosine, sine)


def forward_layer(layer_in, weights, tables):
    attn_gain, mlp_gain, bias, w_attn, w_mlp = weights
    allowed, cosine, sine = tables
    row_count, width = layer_in.shape
    resid = layer_in.astype(wide)
    scale_one = lax.rsqrt(jnp.mean(resid * resid, axis=-1, keepdims=True) + epsilon)
    normed_in = (resid * scale_one * attn_gain).astype(low_type)
    projected = jnp.dot(normed_in, w_attn[:, :640], preferred_element_type=wide) + bias
    queries = rotate(
        projected[:, :448].reshape(row_count, 7, HD), cosine[:, None, :], sine[:, None, :]
    ).astype(low_type)
    key_own = rotate(projected[:, 448:512], cosine, sine).astype(low_type)
    value_own = projected[:, 512:576].astype(low_type)
    key_value = jnp.concatenate(
        spread(jnp.concatenate([key_own, value_own], axis=1), "ctx"), axis=0
    )
    key_all, value_all = key_value[:, :HD], key_value[:, HD:]
    scores = jnp.einsum("qgd,td->gqt", queries, key_all, preferred_element_type=wide) * 0.125
    scores = jnp.where(allowed[None], scores, masked_score)
    largest = jnp.max(scores, axis=-1, keepdims=True)
    raised = jnp.exp(scores - largest)
    totals = jnp.sum(raised, axis=-1, keepdims=True)
    log_total = largest + jnp.log(totals)
    probs = (raised / totals).astype(low_type)
    mixed = jnp.einsum("gqt,td->qgd", probs, value_all, preferred_element_type=wide)
    mixed = jnp.pad(mixed.reshape(row_count, 448).astype(low_type), ((0, 0), (64, 0)))
    middle = resid + tensor_sum(contract(mixed, w_attn[:, 512:], 1, 1))
    scale_two = lax.rsqrt(jnp.mean(middle * middle, axis=-1, keepdims=True) + epsilon)
    normed_mid = jnp.concatenate(
        spread((middle * scale_two * mlp_gain).astype(low_type), "ctx"), axis=0
    )
    gate_up = jnp.dot(normed_mid, w_mlp[:, : 2 * UNITS], preferred_element_type=wide)
    hidden = (jax.nn.silu(gate_up[:, :UNITS]) * gate_up[:, UNITS:]).astype(low_type)
    branch = contract(hidden, w_mlp[:, 2 * UNITS : 3 * UNITS], 1, 1).astype(low_type)
    branch = branch.reshape(-1, row_count, width)
    layer_out = middle + tensor_sum(collect(list(branch), "ctx"))
    kept = (
        resid,
        scale_one,
        normed_in,
        queries,
        key_all,
        value_all,
        log_total,
        mixed,
        middle,
        scale_two,
        normed_mid,
        gate_up,
        hidden,
    )
    return (layer_out.astype(low_type), kept)


def backward_mlp(grad_out, kept, weights):
    attn_gain, mlp_gain, bias, w_attn, w_mlp = weights
    middle, scale_two, normed_mid, gate_up, hidden = kept[8:]
    row_count, width = middle.shape
    grad_all = jnp.concatenate(spread(grad_out, "ctx"), axis=0)
    grad_hidden = jnp.dot(grad_all, w_mlp[:, 2 * UNITS : 3 * UNITS], preferred_element_type=wide)
    gate = gate_up[:, :UNITS]
    upward = gate_up[:, UNITS:]
    sigmoid = jax.nn.sigmoid(gate)
    grad_gate = grad_hidden * upward * sigmoid * (1.0 + gate * (1.0 - sigmoid))
    grad_upward = grad_hidden * gate * sigmoid
    grad_gate_up = jnp.concatenate([grad_gate, grad_upward], axis=1).astype(low_type)
    branch = contract(grad_gate_up, w_mlp[:, : 2 * UNITS], 1, 1).astype(low_type)
    branch = branch.reshape(-1, row_count, width)
    grad_normed_mid = tensor_sum(collect(list(branch), "ctx"))
    grad_mlp = jnp.concatenate(
        [
            contract(normed_mid, grad_gate_up, 0, 0).astype(low_type),
            contract(grad_all, hidden, 0, 0).astype(low_type),
        ],
        axis=1,
    )
    grad_mlp_gain, grad_middle = norm_backward(grad_normed_mid, middle, scale_two, mlp_gain)
    return (grad_middle + grad_out.astype(wide), grad_mlp, grad_mlp_gain)


def backward_attn(grad_middle, kept, weights, tables):
    attn_gain, mlp_gain, bias, w_attn, w_mlp = weights
    allowed, cosine, sine = tables
    resid, scale_one, normed_in, queries, key_all, value_all, log_total, mixed = kept[:8]
    row_count, width = resid.shape
    grad_branch = grad_middle.astype(low_type)
    grad_mixed = jnp.dot(grad_branch, w_attn[:, 512:], preferred_element_type=wide)
    grad_mixed = grad_mixed[:, 64:].astype(low_type).reshape(queries.shape)
    scores = jnp.einsum("qgd,td->gqt", queries, key_all, preferred_element_type=wide) * 0.125
    probs = jnp.where(allowed[None], jnp.exp(scores - log_total), 0.0)
    grad_probs = jnp.einsum("qgd,td->gqt", grad_mixed, value_all, preferred_element_type=wide)
    grad_value_all = jnp.einsum(
        "gqt,qgd->td", probs.astype(low_type), grad_mixed, preferred_element_type=wide
    )
    row_delta = jnp.sum(grad_probs * probs, axis=-1, keepdims=True)
    grad_scores = (probs * (grad_probs - row_delta)).astype(low_type)
    grad_queries = (
        jnp.einsum("gqt,td->qgd", grad_scores, key_all, preferred_element_type=wide) * 0.125
    )
    grad_key_all = (
        jnp.einsum("gqt,qgd->td", grad_scores, queries, preferred_element_type=wide) * 0.125
    )
    grad_key_value = jnp.concatenate([grad_key_all, grad_value_all], axis=1).astype(low_type)
    grad_key_value = collect(list(grad_key_value.reshape(-1, row_count, 2 * HD)), "ctx")
    grad_projected = jnp.concatenate(
        [
            rotate_back(grad_queries, cosine[:, None, :], sine[:, None, :]).reshape(row_count, 448),
            rotate_back(grad_key_value[:, :HD], cosine, sine),
            grad_key_value[:, HD:],
            jnp.zeros((row_count, HD), wide),
        ],
        axis=1,
    ).astype(low_type)
    grad_normed_in = tensor_sum(contract(grad_projected, w_attn[:, :640], 1, 1))
    grad_attn_gain, grad_resid = norm_backward(grad_normed_in, resid, scale_one, attn_gain)
    grad_bias = jnp.sum(grad_projected.astype(wide), axis=0)
    grad_attn = jnp.concatenate(
        [
            contract(normed_in, grad_projected[:, :576], 0, 0).astype(low_type),
            contract(grad_branch, mixed[:, 64:], 0, 0).astype(low_type),
        ],
        axis=1,
    )
    return ((grad_resid + grad_middle).astype(low_type), grad_attn, grad_attn_gain, grad_bias)


def pick(array, place, axis):
    return lax.dynamic_index_in_dim(array, place, axis, keepdims=False)


def halve(blocks, section_place):
    sent = turn(pick(blocks, 1 - section_place, 1), "section", 1)
    return (pick(blocks, section_place, 1).astype(wide) + sent.astype(wide)).astype(low_type)


def sum_rows(blocks, row_place, axis):
    total = pick(blocks, row_place, axis).astype(wide)
    for steps in (1, 3, 2):
        total = total + turn_y(pick(blocks, (row_place + steps) % 4, axis), steps).astype(wide)
    return total.astype(low_type)


def sum_columns(block):
    hops = []
    for row in range(4):
        hops.append((8 + 2 * row, 8 + 2 * row + 1))
        hops.append((2 * row + 1, 2 * row))
    total = block.astype(wide) + lax.ppermute(block, ("section", "fsdp"), hops).astype(wide)
    return total.astype(low_type)


def own_layer(block_zero, block_one, section_place, column_place):
    first = section_place == 0
    hops = []
    for row in range(4):
        hops.append((2 * row, 8 + 2 * row))
        hops.append((8 + 2 * row + 1, 2 * row + 1))
    own = jnp.where(first, block_zero, block_one)
    sent = jnp.where(first, block_one, block_zero)
    received = lax.ppermute(sent, ("section", "fsdp"), hops)
    return jnp.where(section_place == column_place, own, received)


def spread_in_order(block, ctx_place):
    whole = jnp.zeros((4,) + block.shape, block.dtype)
    start = (0,) * block.ndim
    whole = lax.dynamic_update_slice(whole, block[None], (ctx_place,) + start)
    for steps in (1, 3, 2):
        whole = lax.dynamic_update_slice(
            whole, turn(block, "ctx", steps)[None], ((ctx_place - steps) % 4,) + start
        )
    return whole


def halve_mlp(grad, section_place):
    return halve(grad.reshape(4, 2, 112, 3 * UNITS), section_place)


def halve_attn(grad, small, section_place):
    grad_attn_gain, grad_mlp_gain, grad_bias = small
    lines = jnp.concatenate(
        [
            jnp.pad(grad_attn_gain.reshape(8, 112), ((0, 0), (0, 16))),
            jnp.pad(grad_mlp_gain.reshape(8, 112), ((0, 0), (0, 16))),
            jnp.pad(grad_bias[:512].reshape(8, 64), ((0, 0), (0, 64))),
            jnp.pad(grad_bias[512:576].reshape(8, 8), ((0, 0), (0, 632))),
        ],
        axis=1,
    ).astype(low_type)
    lines = jnp.pad(lines[:, None], ((0, 0), (0, 15), (0, 0)))
    blocks = jnp.concatenate([grad.reshape(8, 112, 1024), lines], axis=1)
    return halve(blocks.reshape(4, 2, 128, 1024), section_place)


def sum_ctx(blocks, ctx_place):
    quarter = lambda place: lax.dynamic_slice_in_dim(blocks, place * 256, 256, 2)
    total = collect([quarter((ctx_place - steps) % 4) for steps in range(4)], "ctx")
    return total.astype(low_type)


def per_device(
    layer_input, cotangent, doc_lengths, attn_gain, w_qkv, b_qkv, w_out, mlp_gain, w_gate_up, w_down
):
    section_place = lax.axis_index("section")
    fsdp_place = lax.axis_index("fsdp")
    row_place, column_place = fsdp_place // 2, fsdp_place % 2
    ctx_place = lax.axis_index("ctx")
    places = (section_place, row_place, column_place, ctx_place)
    row_count, width = layer_input.shape[1:]
    units_all = w_down.shape[1]

    line = jnp.concatenate(
        [
            jnp.pad(attn_gain, ((0, 0), (0, 16))),
            jnp.pad(mlp_gain, ((0, 0), (0, 16))),
            jnp.pad(b_qkv[0], ((0, 0), (0, 696))),
        ],
        axis=1,
    )
    attn_block = jnp.concatenate(
        [
            jnp.concatenate([w_qkv[0, :, 0], w_out[0].T], axis=1),
            jnp.pad(line, ((0, 15), (0, 0))),
        ],
        axis=0,
    )
    past = 4 * UNITS - units_all
    mlp_block = jnp.concatenate(
        [
            jnp.pad(w_gate_up[0], ((0, 0), (0, 0), (0, past))),
            jnp.pad(w_down[0].T, ((0, 0), (0, past)))[:, None],
        ],
        axis=1,
    )
    mlp_block = lax.dynamic_slice_in_dim(mlp_block, ctx_place * UNITS, UNITS, 2)
    mlp_block = jnp.pad(mlp_block.reshape(112, 3 * UNITS), ((0, 0), (0, 128)))

    attn_halves = halves_by_layer(attn_block, section_place)
    mlp_halves = halves_by_layer(mlp_block, section_place)
    attn_zero = gather_halves(attn_halves[0], row_place, column_place, section_place)
    mlp_zero = gather_halves(mlp_halves[0], row_place, column_place, section_place)
    mlp_zero, half_attn, half_mlp = after(mlp_zero, attn_halves[1], mlp_halves[1])
    attn_one = gather_halves(half_attn, row_place, column_place, section_place)
    mlp_one = gather_halves(half_mlp, row_place, column_place, section_place)
    attn_pair = (attn_zero, attn_one)
    mlp_pair = (mlp_zero.reshape(width, 2048), mlp_one.reshape(width, 2048))
    weights = []
    for attn, mlp in zip(attn_pair, mlp_pair):
        lines = attn[:, 112].astype(wide)
        weights.append(
            (
                lines[:, :112].reshape(width),
                lines[:, 128:240].reshape(width),
                jnp.pad(lines[:, 256:328].reshape(576), (0, 64)),
                attn[:, :112].reshape(width, 1024),
                mlp,
            )
        )

    tables = mask_tables(pick(doc_lengths, section_place, 0)[0], ctx_place, row_count, 4)
    rows = pick(layer_input, section_place, 0)
    outputs, kept_all = [], []
    for layer in range(2):
        rows, kept = forward_layer(rows, weights[layer], tables)
        outputs.append(rows)
        kept_all.append(kept)
    grads_last = pick(cotangent, section_place, 0)

    middle_one, mlp_one, gain_one = backward_mlp(grads_last, kept_all[1], weights[1])
    mlp_one = sum_rows(halve_mlp(mlp_one, section_place), row_place, 0)
    grads_one, attn_one, *small = backward_attn(middle_one, kept_all[1], weights[1], tables)
    grads_one, mlp_one = after(grads_one, mlp_one)
    attn_one = halve_attn(attn_one, (small[0], gain_one, small[1]), section_place)

    middle_zero, mlp_zero, gain_zero = backward_mlp(grads_one, kept_all[0], weights[0])
    mlp_one = sum_columns(mlp_one)
    middle_zero, mlp_one, attn_one = after(middle_zero, mlp_one, attn_one)
    mlp_zero = sum_rows(halve_mlp(mlp_zero, section_place), row_place, 0)
    attn_one = sum_ctx(attn_one, ctx_place)
    grads_zero, attn_zero, *small = backward_attn(middle_zero, kept_all[0], weights[0], tables)
    grads_zero, attn_zero, mlp_zero, attn_one = after(grads_zero, attn_zero, mlp_zero, attn_one)

    attn_zero = halve_attn(attn_zero, (small[0], gain_zero, small[1]), section_place)
    attn_zero = sum_ctx(attn_zero, ctx_place)
    attn_both = sum_columns(sum_rows(jnp.stack([attn_zero, attn_one]), row_place, 1))
    mlp = own_layer(sum_columns(mlp_zero), mlp_one, section_place, column_place)
    attn = own_layer(attn_both[0], attn_both[1], section_place, column_place)
    mlp = spread_in_order(mlp, ctx_place).reshape(4, 112, 3, UNITS)
    attn = spread_in_order(attn, ctx_place)

    first = section_place == 0

    def by_layer(values):
        own = jnp.where(first, values[0], values[1])
        other = turn(jnp.where(first, values[1], values[0]), "section", 1)
        return jnp.where(first, jnp.stack([own, other]), jnp.stack([other, own]))[None]

    hidden_states = by_layer(outputs)
    input_grads = by_layer([grads_zero, grads_one])
    attn = attn.transpose(1, 0, 2).reshape(128, 1024).astype(wide)
    gate_up = mlp[:, :, :2].transpose(1, 2, 0, 3).reshape(112, 2, 4 * UNITS)[:, :, :units_all]
    down = mlp[:, :, 2].transpose(0, 2, 1).reshape(4 * UNITS, 112)[:units_all]
    lines = attn[112:113]
    return (
        hidden_states,
        input_grads,
        lines[:, :112],
        attn[None, :112, None, :576],
        lines[None, :, 256:320],
        lines[None, :, 384:392],
        attn[:112, 576:].T[None],
        lines[:, 128:240],
        gate_up.astype(wide)[None],
        down.astype(wide)[None],
    )


def solution(mesh):
    return jax.shard_map(
        per_device,
        mesh=mesh,
        in_specs=(
            P(None, ("fsdp", "ctx"), None),
            P(None, ("fsdp", "ctx"), None),
            P(None, "fsdp", None),
            P("section", "fsdp"),
            P("section", "fsdp", "tp", None),
            P("section", "tp", "fsdp"),
            P("section", "tp", "fsdp"),
            P("section", "fsdp"),
            P("section", "fsdp", None, "tp"),
            P("section", "tp", "fsdp"),
        ),
        out_specs=(
            P("section", None, ("fsdp", "ctx"), None),
            P("section", None, ("fsdp", "ctx"), None),
            P("section", "fsdp"),
            P("section", "fsdp", "tp", None),
            P("section", "tp", "fsdp"),
            P("section", "tp", "fsdp"),
            P("section", "tp", "fsdp"),
            P("section", "fsdp"),
            P("section", "fsdp", None, "tp"),
            P("section", "tp", "fsdp"),
        ),
        check_vma=False,
    )
```

```python
import jax
import jax.numpy as jnp
from jax import lax
from jax.sharding import PartitionSpec as P

HD = 64
UNITS = 640

epsilon = 1e-06
rope_base = 1000000.0
masked_score = -1000000000.0
low_type = jnp.bfloat16
wide = jnp.float32


def contract(left, right, left_dim, right_dim):
    return lax.dot_general(
        left, right, (((left_dim,), (right_dim,)), ((), ())), preferred_element_type=wide
    )


def turn(value, axis, steps):
    count = lax.axis_size(axis)
    return lax.ppermute(value, axis, [(place, (place + steps) % count) for place in range(count)])


def turn_y(value, steps):
    count = lax.axis_size("fsdp")
    return lax.ppermute(
        value, "fsdp", [(place, (place + 2 * steps) % count) for place in range(count)]
    )


def flip_x(value):
    count = lax.axis_size("fsdp")
    return lax.ppermute(value, "fsdp", [(place, place ^ 1) for place in range(count)])


def spread(block, axis):
    count = lax.axis_size(axis)
    order = [1, count - 1] + list(range(2, count - 1))
    moved = {steps: turn(block, axis, steps) for steps in order}
    return [block] + [moved[steps] for steps in range(1, count)]


def collect(blocks, axis):
    count = lax.axis_size(axis)
    order = [1, count - 1] + list(range(2, count - 1))
    total = blocks[0].astype(wide)
    for steps in order:
        total = total + turn(blocks[steps], axis, -steps).astype(wide)
    return total


def tensor_sum(partial_value):
    own = lax.optimization_barrier(partial_value.astype(low_type))
    return own.astype(wide) + turn(own, "tp", 1).astype(wide)


def after(value, *others):
    tied = lax.optimization_barrier((value,) + others)
    return tied[0] if not others else tied


def with_column(half, received, column_place):
    pair = jnp.zeros((2,) + half.shape, half.dtype)
    pair = lax.dynamic_update_slice(pair, half[None], (column_place, 0, 0))
    return lax.dynamic_update_slice(pair, received[None], (1 - column_place, 0, 0))


def with_rows(pair, moved, row_place):
    part = jnp.zeros((4,) + pair.shape, pair.dtype)
    part = lax.dynamic_update_slice(part, pair[None], (row_place, 0, 0, 0))
    for steps, piece in zip((1, 3, 2), moved):
        part = lax.dynamic_update_slice(part, piece[None], ((row_place - steps) % 4, 0, 0, 0))
    return part.reshape((8,) + pair.shape[1:])


def turn_rows(pair):
    return [turn_y(pair, steps) for steps in (1, 3, 2)]


def with_halves(part, other, section_place):
    first = section_place == 0
    return jnp.concatenate([jnp.where(first, part, other), jnp.where(first, other, part)], axis=2)


def split_attn(attn):
    width = 8 * 112
    lines = attn[:, 112].astype(wide)
    return (
        lines[:, :112].reshape(width),
        lines[:, 128:240].reshape(width),
        jnp.pad(lines[:, 256:328].reshape(576), (0, 64)),
        attn[:, :112].reshape(width, 1024),
    )


def halves_by_layer(block, section_place):
    columns = block.shape[1] // 2
    kept = lax.dynamic_slice_in_dim(block, section_place * columns, columns, 1)
    sent = lax.dynamic_slice_in_dim(block, (1 - section_place) * columns, columns, 1)
    received = turn(sent, "section", 1)
    first = section_place == 0
    return jnp.where(first, kept, received), jnp.where(first, received, kept)


def rotary_tables(position):
    inverse = rope_base ** (-jnp.arange(0, HD, 2, dtype=wide) / HD)
    angles = position.astype(wide)[..., None] * inverse
    angles = jnp.concatenate([angles, angles], axis=-1)
    return (jnp.cos(angles), jnp.sin(angles))


def rotate(values, cosine, sine):
    half_width = values.shape[-1] // 2
    turned = jnp.concatenate([-values[..., half_width:], values[..., :half_width]], axis=-1)
    return values * cosine + turned * sine


def rotate_back(grads, cosine, sine):
    half_width = grads.shape[-1] // 2
    scaled = grads * sine
    turned = jnp.concatenate([scaled[..., half_width:], -scaled[..., :half_width]], axis=-1)
    return grads * cosine + turned


def norm_backward(grad_normed, resid, scale, gain):
    grad_gain = jnp.sum(grad_normed * resid * scale, axis=0)
    inner = grad_normed * gain
    grad_resid = scale * inner - resid * (scale * scale * scale) * jnp.mean(
        inner * resid, axis=-1, keepdims=True
    )
    return (grad_gain, grad_resid)


def mask_tables(lengths, ctx_place, row_count, ctx_count):
    doc_ends = jnp.cumsum(lengths, axis=-1)
    blocks = (ctx_place - jnp.arange(ctx_count, dtype=jnp.int32)) % ctx_count
    places = (blocks[:, None] * row_count + jnp.arange(row_count, dtype=jnp.int32)).reshape(-1)
    passed = places[:, None] >= doc_ends[None, :]
    segment = jnp.sum(passed.astype(jnp.int32), axis=-1)
    doc_start = jnp.sum(jnp.where(passed, lengths[None, :], 0), axis=-1)
    position = places - doc_start
    cosine, sine = rotary_tables(position[:row_count])
    allowed = (segment[:row_count, None] == segment[None, :]) & (
        places[:row_count, None] >= places[None, :]
    )
    return (allowed, cosine, sine)


def forward_attn(layer_in, weights, tables):
    attn_gain, mlp_gain, bias, w_attn = weights
    allowed, cosine, sine = tables
    row_count, width = layer_in.shape
    resid = layer_in.astype(wide)
    scale_one = lax.rsqrt(jnp.mean(resid * resid, axis=-1, keepdims=True) + epsilon)
    normed_in = (resid * scale_one * attn_gain).astype(low_type)
    projected = jnp.dot(normed_in, w_attn[:, :640], preferred_element_type=wide) + bias
    queries = rotate(
        projected[:, :448].reshape(row_count, 7, HD), cosine[:, None, :], sine[:, None, :]
    ).astype(low_type)
    key_own = rotate(projected[:, 448:512], cosine, sine).astype(low_type)
    value_own = projected[:, 512:576].astype(low_type)
    key_value = jnp.concatenate(
        spread(jnp.concatenate([key_own, value_own], axis=1), "ctx"), axis=0
    )
    key_all, value_all = key_value[:, :HD], key_value[:, HD:]
    scores = jnp.einsum("qgd,td->gqt", queries, key_all, preferred_element_type=wide) * 0.125
    scores = jnp.where(allowed[None], scores, masked_score)
    largest = jnp.max(scores, axis=-1, keepdims=True)
    raised = jnp.exp(scores - largest)
    totals = jnp.sum(raised, axis=-1, keepdims=True)
    log_total = largest + jnp.log(totals)
    probs = (raised / totals).astype(low_type)
    mixed = jnp.einsum("gqt,td->qgd", probs, value_all, preferred_element_type=wide)
    mixed = jnp.pad(mixed.reshape(row_count, 448).astype(low_type), ((0, 0), (64, 0)))
    kept = (resid, scale_one, normed_in, queries, key_all, value_all, log_total, mixed)
    return contract(mixed, w_attn[:, 512:], 1, 1), kept


def forward_mid(branch, resid, mlp_gain):
    middle = resid + tensor_sum(branch)
    scale_two = lax.rsqrt(jnp.mean(middle * middle, axis=-1, keepdims=True) + epsilon)
    return middle, scale_two, (middle * scale_two * mlp_gain).astype(low_type)


def forward_mlp(middle, scale_two, normed_mid, w_mlp):
    row_count, width = middle.shape
    normed_mid = jnp.concatenate(spread(normed_mid, "ctx"), axis=0)
    gate_up = jnp.dot(normed_mid, w_mlp[:, : 2 * UNITS], preferred_element_type=wide)
    hidden = (jax.nn.silu(gate_up[:, :UNITS]) * gate_up[:, UNITS:]).astype(low_type)
    branch = contract(hidden, w_mlp[:, 2 * UNITS : 3 * UNITS], 1, 1).astype(low_type)
    branch = branch.reshape(-1, row_count, width)
    layer_out = middle + tensor_sum(collect(list(branch), "ctx"))
    return layer_out.astype(low_type), (middle, scale_two, normed_mid, gate_up, hidden)


def backward_mlp(grad_out, kept, w_mlp):
    middle, scale_two, normed_mid, gate_up, hidden = kept
    row_count, width = middle.shape
    grad_all = jnp.concatenate(spread(grad_out, "ctx"), axis=0)
    grad_hidden = jnp.dot(grad_all, w_mlp[:, 2 * UNITS : 3 * UNITS], preferred_element_type=wide)
    gate = gate_up[:, :UNITS]
    upward = gate_up[:, UNITS:]
    sigmoid = jax.nn.sigmoid(gate)
    grad_gate = grad_hidden * upward * sigmoid * (1.0 + gate * (1.0 - sigmoid))
    grad_upward = grad_hidden * gate * sigmoid
    grad_gate_up = jnp.concatenate([grad_gate, grad_upward], axis=1).astype(low_type)
    branch = contract(grad_gate_up, w_mlp[:, : 2 * UNITS], 1, 1).astype(low_type)
    branch = branch.reshape(-1, row_count, width)
    branch = collect(list(branch), "ctx")
    grad_mlp = jnp.concatenate(
        [
            contract(normed_mid, grad_gate_up, 0, 0).astype(low_type),
            contract(grad_all, hidden, 0, 0).astype(low_type),
        ],
        axis=1,
    )
    return branch, grad_mlp


def backward_mid(branch, grad_out, kept, mlp_gain):
    middle, scale_two = kept[:2]
    grad_normed_mid = tensor_sum(branch)
    grad_mlp_gain, grad_middle = norm_backward(grad_normed_mid, middle, scale_two, mlp_gain)
    return grad_middle + grad_out.astype(wide), grad_mlp_gain


def backward_attn(grad_middle, kept, weights, tables):
    attn_gain, mlp_gain, bias, w_attn = weights
    allowed, cosine, sine = tables
    resid, scale_one, normed_in, queries, key_all, value_all, log_total, mixed = kept
    row_count, width = resid.shape
    grad_branch = grad_middle.astype(low_type)
    grad_mixed = jnp.dot(grad_branch, w_attn[:, 512:], preferred_element_type=wide)
    grad_mixed = grad_mixed[:, 64:].astype(low_type).reshape(queries.shape)
    scores = jnp.einsum("qgd,td->gqt", queries, key_all, preferred_element_type=wide) * 0.125
    probs = jnp.where(allowed[None], jnp.exp(scores - log_total), 0.0)
    grad_probs = jnp.einsum("qgd,td->gqt", grad_mixed, value_all, preferred_element_type=wide)
    grad_value_all = jnp.einsum(
        "gqt,qgd->td", probs.astype(low_type), grad_mixed, preferred_element_type=wide
    )
    row_delta = jnp.sum(grad_probs * probs, axis=-1, keepdims=True)
    grad_scores = (probs * (grad_probs - row_delta)).astype(low_type)
    grad_queries = (
        jnp.einsum("gqt,td->qgd", grad_scores, key_all, preferred_element_type=wide) * 0.125
    )
    grad_key_all = (
        jnp.einsum("gqt,qgd->td", grad_scores, queries, preferred_element_type=wide) * 0.125
    )
    grad_key_value = jnp.concatenate([grad_key_all, grad_value_all], axis=1).astype(low_type)
    grad_key_value = collect(list(grad_key_value.reshape(-1, row_count, 2 * HD)), "ctx")
    grad_projected = jnp.concatenate(
        [
            rotate_back(grad_queries, cosine[:, None, :], sine[:, None, :]).reshape(row_count, 448),
            rotate_back(grad_key_value[:, :HD], cosine, sine),
            grad_key_value[:, HD:],
            jnp.zeros((row_count, HD), wide),
        ],
        axis=1,
    ).astype(low_type)
    return grad_branch, grad_projected


def backward_in(grad_projected, grad_middle, kept, weights):
    attn_gain, mlp_gain, bias, w_attn = weights
    resid, scale_one = kept[:2]
    grad_normed_in = tensor_sum(contract(grad_projected, w_attn[:, :640], 1, 1))
    grad_attn_gain, grad_resid = norm_backward(grad_normed_in, resid, scale_one, attn_gain)
    return (grad_resid + grad_middle).astype(low_type), grad_attn_gain


def attn_weight_grads(grad_branch, grad_projected, kept):
    normed_in, mixed = kept[2], kept[7]
    grad_bias = jnp.sum(grad_projected.astype(wide), axis=0)
    projection = contract(normed_in, grad_projected, 0, 0)
    output = contract(grad_branch, mixed, 0, 0)
    latter = jnp.pad(projection[:, 512:], ((0, 0), (0, 384))) + output
    return jnp.concatenate([projection[:, :512], latter], axis=1).astype(low_type), grad_bias


def pick(array, place, axis):
    return lax.dynamic_index_in_dim(array, place, axis, keepdims=False)


def row_blocks(blocks, row_place, axis):
    return [pick(blocks, (row_place + steps) % 4, axis) for steps in (0, 1, 3, 2)]


def sum_rows(pieces):
    total = pieces[0].astype(wide)
    for steps, piece in zip((1, 3, 2), pieces[1:]):
        total = total + turn_y(piece, steps).astype(wide)
    return total.astype(low_type)


def split_columns(blocks, section_place):
    return pick(blocks, section_place, 1), pick(blocks, 1 - section_place, 1)


def halve(kept, sent):
    return (kept.astype(wide) + turn(sent, "section", 1).astype(wide)).astype(low_type)


def sum_columns(block):
    hops = []
    for row in range(4):
        hops.append((8 + 2 * row, 8 + 2 * row + 1))
        hops.append((2 * row + 1, 2 * row))
    total = block.astype(wide) + lax.ppermute(block, ("section", "fsdp"), hops).astype(wide)
    return total.astype(low_type)


def own_layer(block_zero, block_one, section_place, column_place):
    first = section_place == 0
    hops = []
    for row in range(4):
        hops.append((2 * row, 8 + 2 * row))
        hops.append((8 + 2 * row + 1, 2 * row + 1))
    own = jnp.where(first, block_zero, block_one)
    sent = jnp.where(first, block_one, block_zero)
    received = lax.ppermute(sent, ("section", "fsdp"), hops)
    return jnp.where(section_place == column_place, own, received)


def spread_in_order(block, ctx_place):
    pieces = jnp.stack(spread(block, "ctx"))
    return jnp.stack([pick(pieces, (ctx_place - place) % 4, 0) for place in range(4)])


def pack_lines(small):
    grad_attn_gain, grad_mlp_gain, grad_bias = small
    lines = jnp.concatenate(
        [
            jnp.pad(grad_attn_gain.reshape(8, 112), ((0, 0), (0, 16))),
            jnp.pad(grad_mlp_gain.reshape(8, 112), ((0, 0), (0, 16))),
            jnp.pad(grad_bias[:512].reshape(8, 64), ((0, 0), (0, 64))),
            jnp.pad(grad_bias[512:576].reshape(8, 8), ((0, 0), (0, 632))),
        ],
        axis=1,
    ).astype(low_type)
    return jnp.pad(lines[:, None], ((0, 0), (0, 15), (0, 0))).reshape(4, 2, 16, 1024)


def ctx_blocks(blocks, lines, ctx_place):
    quarters = []
    for steps in range(4):
        start = (ctx_place - steps) % 4 * 256
        quarters.append(
            jnp.concatenate(
                [
                    lax.dynamic_slice_in_dim(blocks, start, 256, 2),
                    lax.dynamic_slice_in_dim(lines, start, 256, 2),
                ],
                axis=1,
            )
        )
    return quarters


def per_device(
    layer_input, cotangent, doc_lengths, attn_gain, w_qkv, b_qkv, w_out, mlp_gain, w_gate_up, w_down
):
    section_place = lax.axis_index("section")
    fsdp_place = lax.axis_index("fsdp")
    row_place, column_place = fsdp_place // 2, fsdp_place % 2
    ctx_place = lax.axis_index("ctx")
    places = (section_place, row_place, column_place, ctx_place)
    row_count, width = layer_input.shape[1:]
    units_all = w_down.shape[1]

    line = jnp.concatenate(
        [
            jnp.pad(attn_gain, ((0, 0), (0, 16))),
            jnp.pad(mlp_gain, ((0, 0), (0, 16))),
            jnp.pad(b_qkv[0], ((0, 0), (0, 696))),
        ],
        axis=1,
    )
    attn_block = jnp.concatenate(
        [
            jnp.concatenate([w_qkv[0, :, 0], w_out[0].T], axis=1),
            jnp.pad(line, ((0, 15), (0, 0))),
        ],
        axis=0,
    )
    past = 4 * UNITS - units_all
    mlp_block = jnp.concatenate(
        [
            jnp.pad(w_gate_up[0], ((0, 0), (0, 0), (0, past))),
            jnp.pad(w_down[0].T, ((0, 0), (0, past)))[:, None],
        ],
        axis=1,
    )
    mlp_block = lax.dynamic_slice_in_dim(mlp_block, ctx_place * UNITS, UNITS, 2)
    mlp_block = jnp.pad(mlp_block.reshape(112, 3 * UNITS), ((0, 0), (0, 128)))

    half_attn, late_attn = halves_by_layer(attn_block, section_place)
    half_mlp, late_mlp = halves_by_layer(mlp_block, section_place)
    pair_attn = with_column(half_attn, flip_x(half_attn), column_place)
    pair_mlp = with_column(half_mlp, flip_x(half_mlp), column_place)
    rows_attn = turn_rows(pair_attn)
    rows_mlp = turn_rows(pair_mlp)
    part = with_rows(pair_attn, rows_attn, row_place)
    weights_zero = split_attn(with_halves(part, turn(part, "section", 1), section_place))

    tables = mask_tables(pick(doc_lengths, section_place, 0)[0], ctx_place, row_count, 4)
    layer_in = pick(layer_input, section_place, 0)
    branch, kept_attn_zero = forward_attn(layer_in, weights_zero, tables)
    branch, pair_mlp, late_attn, late_mlp, *rows_mlp = after(
        branch, pair_mlp, late_attn, late_mlp, *rows_mlp
    )
    part = with_rows(pair_mlp, rows_mlp, row_place)
    mlp_other = turn(part, "section", 1)
    late_attn_other, late_mlp_other = flip_x(late_attn), flip_x(late_mlp)
    middle, scale_two, normed_mid = forward_mid(branch, kept_attn_zero[0], weights_zero[1])
    pair_attn = with_column(late_attn, late_attn_other, column_place)
    normed_mid, pair_attn = after(normed_mid, pair_attn)
    rows_attn = turn_rows(pair_attn)
    w_mlp_zero = with_halves(part, mlp_other, section_place).reshape(width, 2048)
    pair_mlp = with_column(late_mlp, late_mlp_other, column_place)
    w_mlp_zero, pair_mlp = after(w_mlp_zero, pair_mlp)
    rows_mlp = turn_rows(pair_mlp)
    out_zero, kept_mlp_zero = forward_mlp(middle, scale_two, normed_mid, w_mlp_zero)
    out_zero, pair_attn, *rows_attn = after(out_zero, pair_attn, *rows_attn)
    part = with_rows(pair_attn, rows_attn, row_place)
    weights_one = split_attn(with_halves(part, turn(part, "section", 1), section_place))

    branch, kept_attn_one = forward_attn(out_zero, weights_one, tables)
    branch, pair_mlp, *rows_mlp = after(branch, pair_mlp, *rows_mlp)
    part = with_rows(pair_mlp, rows_mlp, row_place)
    mlp_other = turn(part, "section", 1)
    middle, scale_two, normed_mid = forward_mid(branch, kept_attn_one[0], weights_one[1])
    w_mlp_one = with_halves(part, mlp_other, section_place).reshape(width, 2048)
    out_one, kept_mlp_one = forward_mlp(middle, scale_two, normed_mid, w_mlp_one)
    outputs = [out_zero, out_one]
    grads_last = pick(cotangent, section_place, 0)

    mlp_shape = (4, 2, 112, 3 * UNITS)
    attn_shape = (4, 2, 112, 1024)
    branch, mlp_one = backward_mlp(grads_last, kept_mlp_one, w_mlp_one)
    branch, *mlp_one = after(branch, *split_columns(mlp_one.reshape(mlp_shape), section_place))
    middle_one, gain_one = backward_mid(branch, grads_last, kept_mlp_one, weights_one[1])
    middle_one, *mlp_one = after(middle_one, *row_blocks(halve(*mlp_one), row_place, 0))
    branch_one, projected_one = backward_attn(middle_one, kept_attn_one, weights_one, tables)
    grads_one, attn_gain_one = backward_in(projected_one, middle_one, kept_attn_one, weights_one)
    grads_one, mlp_one = after(grads_one, sum_rows(mlp_one))
    attn_one, bias_one = attn_weight_grads(branch_one, projected_one, kept_attn_one)
    lines_one = pack_lines((attn_gain_one, gain_one, bias_one))

    branch, mlp_zero = backward_mlp(grads_one, kept_mlp_zero, w_mlp_zero)
    branch, mlp_keep, mlp_sent, attn_keep, attn_sent, lines_keep, lines_sent, mlp_one = after(
        branch,
        *split_columns(mlp_zero.reshape(mlp_shape), section_place),
        *split_columns(attn_one.reshape(attn_shape), section_place),
        *split_columns(lines_one, section_place),
        sum_columns(mlp_one),
    )
    middle_zero, gain_zero = backward_mid(branch, grads_one, kept_mlp_zero, weights_zero[1])
    middle_zero, *pieces = after(
        middle_zero,
        *row_blocks(halve(mlp_keep, mlp_sent), row_place, 0),
        *ctx_blocks(halve(attn_keep, attn_sent), halve(lines_keep, lines_sent), ctx_place),
    )
    branch_zero, projected_zero = backward_attn(middle_zero, kept_attn_zero, weights_zero, tables)
    mlp_zero = sum_rows(pieces[:4])
    attn_one = collect(pieces[4:], "ctx").astype(low_type)
    attn_zero, bias_zero = attn_weight_grads(branch_zero, projected_zero, kept_attn_zero)
    projected_zero, mlp_zero, attn_one, attn_keep, attn_sent = after(
        projected_zero,
        mlp_zero,
        attn_one,
        *split_columns(attn_zero.reshape(attn_shape), section_place),
    )
    grads_zero, attn_gain_zero = backward_in(
        projected_zero, middle_zero, kept_attn_zero, weights_zero
    )
    lines_zero = pack_lines((attn_gain_zero, gain_zero, bias_zero))
    lines_zero = halve(*split_columns(lines_zero, section_place))
    pieces = ctx_blocks(halve(attn_keep, attn_sent), lines_zero, ctx_place)
    mlp_zero = sum_columns(mlp_zero)
    attn_zero = collect(pieces, "ctx").astype(low_type)
    attn_zero, mlp_zero, mlp_one = after(attn_zero, mlp_zero, mlp_one)
    mlp = own_layer(mlp_zero, mlp_one, section_place, column_place)
    pieces = row_blocks(jnp.stack([attn_zero, attn_one]), row_place, 1)
    mlp, *pieces = after(mlp, *pieces)
    attn_both = sum_columns(sum_rows(pieces))
    attn = own_layer(attn_both[0], attn_both[1], section_place, column_place)
    mlp = spread_in_order(mlp, ctx_place).reshape(4, 112, 3, UNITS)
    attn = spread_in_order(attn, ctx_place)

    first = section_place == 0

    def by_layer(values):
        own = jnp.where(first, values[0], values[1])
        other = turn(jnp.where(first, values[1], values[0]), "section", 1)
        return jnp.where(first, jnp.stack([own, other]), jnp.stack([other, own]))[None]

    hidden_states = by_layer(outputs)
    input_grads = by_layer([grads_zero, grads_one])
    attn = attn.transpose(1, 0, 2).reshape(128, 1024).astype(wide)
    gate_up = mlp[:, :, :2].transpose(1, 2, 0, 3).reshape(112, 2, 4 * UNITS)[:, :, :units_all]
    down = mlp[:, :, 2].transpose(0, 2, 1).reshape(4 * UNITS, 112)[:units_all]
    lines = attn[112:113]
    return (
        hidden_states,
        input_grads,
        lines[:, :112],
        attn[None, :112, None, :576],
        lines[None, :, 256:320],
        lines[None, :, 384:392],
        attn[:112, 576:].T[None],
        lines[:, 128:240],
        gate_up.astype(wide)[None],
        down.astype(wide)[None],
    )


def solution(mesh):
    return jax.shard_map(
        per_device,
        mesh=mesh,
        in_specs=(
            P(None, ("fsdp", "ctx"), None),
            P(None, ("fsdp", "ctx"), None),
            P(None, "fsdp", None),
            P("section", "fsdp"),
            P("section", "fsdp", "tp", None),
            P("section", "tp", "fsdp"),
            P("section", "tp", "fsdp"),
            P("section", "fsdp"),
            P("section", "fsdp", None, "tp"),
            P("section", "tp", "fsdp"),
        ),
        out_specs=(
            P("section", None, ("fsdp", "ctx"), None),
            P("section", None, ("fsdp", "ctx"), None),
            P("section", "fsdp"),
            P("section", "fsdp", "tp", None),
            P("section", "tp", "fsdp"),
            P("section", "tp", "fsdp"),
            P("section", "tp", "fsdp"),
            P("section", "fsdp"),
            P("section", "fsdp", None, "tp"),
            P("section", "tp", "fsdp"),
        ),
        check_vma=False,
    )
```

```python
import jax
import jax.numpy as jnp
from jax import lax
from jax.sharding import PartitionSpec as P

HD = 64
UNITS = 640

epsilon = 1e-06
rope_base = 1000000.0
masked_score = -1000000000.0
low_type = jnp.bfloat16
wide = jnp.float32


def contract(left, right, left_dim, right_dim):
    return lax.dot_general(
        left, right, (((left_dim,), (right_dim,)), ((), ())), preferred_element_type=wide
    )


def turn(value, axis, steps):
    count = lax.axis_size(axis)
    return lax.ppermute(value, axis, [(place, (place + steps) % count) for place in range(count)])


def turn_y(value, steps):
    count = lax.axis_size("fsdp")
    return lax.ppermute(
        value, "fsdp", [(place, (place + 2 * steps) % count) for place in range(count)]
    )


def flip_x(value):
    count = lax.axis_size("fsdp")
    return lax.ppermute(value, "fsdp", [(place, place ^ 1) for place in range(count)])


def exchange(blocks):
    return lax.all_to_all(blocks, "ctx", 0, 0, tiled=True)


def spread(block):
    count = lax.axis_size("ctx")
    return exchange(jnp.broadcast_to(block[None], (count,) + block.shape))


def collect(blocks):
    return jnp.sum(exchange(blocks).astype(wide), axis=0)


def pick(array, place, axis):
    return lax.dynamic_index_in_dim(array, place, axis, keepdims=False)


def in_order(pieces, ctx_place):
    own, former, latter, opposite = pieces
    pieces = jnp.stack([own, former, opposite, latter])
    return jnp.stack([pick(pieces, (ctx_place - place) % 4, 0) for place in range(4)])


def turn_ctx(block):
    return [turn(block, "ctx", steps) for steps in (1, 3, 2)]


def tensor_sum(partial_value):
    own = lax.optimization_barrier(partial_value.astype(low_type))
    return own.astype(wide) + turn(own, "tp", 1).astype(wide)


def after(value, *others):
    tied = lax.optimization_barrier((value,) + others)
    return tied[0] if not others else tied


def with_rows(pair, moved):
    former, latter, opposite = moved
    return jnp.concatenate([pair, former, opposite, latter], axis=0)


def with_column(half, received):
    return jnp.stack([half, received])


def turn_rows(pair):
    return [turn_y(pair, steps) for steps in (1, 3, 2)]


def with_halves(part, other, section_place):
    first = section_place == 0
    return jnp.concatenate([jnp.where(first, part, other), jnp.where(first, other, part)], axis=2)


def split_attn(attn, block_order):
    width = 8 * 112
    lines = attn[:, 112]
    bias = jnp.dot(block_order.T, lines[:, 256:328], preferred_element_type=wide)
    lines = lines.astype(wide)
    return (
        lines[:, :112].reshape(width),
        lines[:, 128:240].reshape(width),
        jnp.pad(bias.reshape(576), (0, 64)),
        attn[:, :112].reshape(width, 1024),
    )


def halves_by_layer(block, section_place):
    columns = block.shape[1] // 2
    kept = lax.dynamic_slice_in_dim(block, section_place * columns, columns, 1)
    sent = lax.dynamic_slice_in_dim(block, (1 - section_place) * columns, columns, 1)
    received = turn(sent, "section", 1)
    first = section_place == 0
    return jnp.where(first, kept, received), jnp.where(first, received, kept)


def rotary_tables(position):
    inverse = rope_base ** (-jnp.arange(0, HD, 2, dtype=wide) / HD)
    angles = position.astype(wide)[..., None] * inverse
    angles = jnp.concatenate([angles, angles], axis=-1)
    return (jnp.cos(angles), jnp.sin(angles))


def rotate(values, cosine, sine):
    half_width = values.shape[-1] // 2
    turned = jnp.concatenate([-values[..., half_width:], values[..., :half_width]], axis=-1)
    return values * cosine + turned * sine


def rotate_back(grads, cosine, sine):
    half_width = grads.shape[-1] // 2
    scaled = grads * sine
    turned = jnp.concatenate([scaled[..., half_width:], -scaled[..., :half_width]], axis=-1)
    return grads * cosine + turned


def norm_backward(grad_normed, resid, scale, gain):
    grad_gain = jnp.sum(grad_normed * resid * scale, axis=0)
    inner = grad_normed * gain
    grad_resid = scale * inner - resid * (scale * scale * scale) * jnp.mean(
        inner * resid, axis=-1, keepdims=True
    )
    return (grad_gain, grad_resid)


def mask_tables(lengths, ctx_place, row_count, ctx_count):
    doc_ends = jnp.cumsum(lengths, axis=-1)
    places = jnp.arange(row_count * ctx_count, dtype=jnp.int32)
    passed = places[:, None] >= doc_ends[None, :]
    segment = jnp.sum(passed.astype(jnp.int32), axis=-1)
    doc_start = jnp.sum(jnp.where(passed, lengths[None, :], 0), axis=-1)
    cosine, sine = rotary_tables(places - doc_start)
    offset = ctx_place * row_count
    own = lambda values: lax.dynamic_slice_in_dim(values, offset, row_count, 0)
    allowed = (own(segment)[:, None] == segment[None, :]) & (own(places)[:, None] >= places[None, :])
    return (allowed, own(cosine), own(sine), cosine, sine)


def normed(resid, gain):
    scale = lax.rsqrt(jnp.mean(resid * resid, axis=-1, keepdims=True) + epsilon)
    return scale, (resid * scale * gain).astype(low_type)


def forward_attn(layer_in, rows_all, weights, tables):
    attn_gain, mlp_gain, bias, w_attn = weights
    allowed, cosine, sine, cosine_all, sine_all = tables
    row_count, width = layer_in.shape
    resid = layer_in.astype(wide)
    scale_one, normed_in = normed(resid, attn_gain)
    projected = jnp.dot(normed_in, w_attn[:, :640], preferred_element_type=wide) + bias
    queries = rotate(
        projected[:, :448].reshape(row_count, 7, HD), cosine[:, None, :], sine[:, None, :]
    ).astype(low_type)
    if rows_all is None:
        key_own = rotate(projected[:, 448:512], cosine, sine)
        key_value = jnp.concatenate([key_own, projected[:, 512:576]], axis=1).astype(low_type)
        key_value = spread(key_value).reshape(-1, 2 * HD)
    else:
        normed_all = normed(rows_all.astype(wide), attn_gain)[1]
        projected = jnp.dot(normed_all, w_attn[:, 384:640], preferred_element_type=wide)
        projected = projected + bias[384:640]
        key_value = jnp.concatenate(
            [rotate(projected[:, 64:128], cosine_all, sine_all), projected[:, 128:192]], axis=1
        ).astype(low_type)
    key_all, value_all = key_value[:, :HD], key_value[:, HD:]
    scores = jnp.einsum("qgd,td->gqt", queries, key_all, preferred_element_type=wide) * 0.125
    scores = jnp.where(allowed[None], scores, masked_score)
    largest = jnp.max(scores, axis=-1, keepdims=True)
    raised = jnp.exp(scores - largest)
    totals = jnp.sum(raised, axis=-1, keepdims=True)
    log_total = largest + jnp.log(totals)
    probs = (raised / totals).astype(low_type)
    mixed = jnp.einsum("gqt,td->qgd", probs, value_all, preferred_element_type=wide)
    mixed = jnp.pad(mixed.reshape(row_count, 448).astype(low_type), ((0, 0), (64, 0)))
    kept = (resid, scale_one, normed_in, queries, key_all, value_all, log_total, mixed)
    return contract(mixed, w_attn[:, 512:], 1, 1), kept


def forward_mid(branch, resid, mlp_gain):
    middle = resid + tensor_sum(branch)
    return middle, *normed(middle, mlp_gain)


def forward_mlp(normed_mid, w_mlp):
    gate_up = jnp.dot(normed_mid, w_mlp[:, : 2 * UNITS], preferred_element_type=wide)
    hidden = (jax.nn.silu(gate_up[:, :UNITS]) * gate_up[:, UNITS:]).astype(low_type)
    return gate_up, hidden


def forward_down(hidden, w_mlp, row_count):
    branch = contract(hidden, w_mlp[:, 2 * UNITS : 3 * UNITS], 1, 1).astype(low_type)
    return branch.reshape(-1, row_count, branch.shape[1])


def backward_mlp(grad_all, kept, w_mlp):
    middle, scale_two, normed_mid, gate_up, hidden = kept
    row_count, width = middle.shape
    grad_hidden = jnp.dot(grad_all, w_mlp[:, 2 * UNITS : 3 * UNITS], preferred_element_type=wide)
    gate = gate_up[:, :UNITS]
    upward = gate_up[:, UNITS:]
    sigmoid = jax.nn.sigmoid(gate)
    grad_gate = grad_hidden * upward * sigmoid * (1.0 + gate * (1.0 - sigmoid))
    grad_upward = grad_hidden * gate * sigmoid
    grad_gate_up = jnp.concatenate([grad_gate, grad_upward], axis=1).astype(low_type)
    branch = contract(grad_gate_up, w_mlp[:, : 2 * UNITS], 1, 1).astype(low_type)
    branch = branch.reshape(-1, row_count, width)
    grad_mlp = jnp.concatenate(
        [
            contract(normed_mid, grad_gate_up, 0, 0).astype(low_type),
            contract(grad_all, hidden, 0, 0).astype(low_type),
        ],
        axis=1,
    )
    return branch, grad_mlp


def backward_mid(branch, grad_out, kept, mlp_gain):
    middle, scale_two = kept[:2]
    grad_normed_mid = tensor_sum(branch)
    grad_mlp_gain, grad_middle = norm_backward(grad_normed_mid, middle, scale_two, mlp_gain)
    return grad_middle + grad_out.astype(wide), grad_mlp_gain


def backward_attn(grad_middle, kept, weights, tables):
    attn_gain, mlp_gain, bias, w_attn = weights
    allowed, cosine, sine = tables[:3]
    resid, scale_one, normed_in, queries, key_all, value_all, log_total, mixed = kept
    row_count, width = resid.shape
    grad_branch = grad_middle.astype(low_type)
    grad_mixed = jnp.dot(grad_branch, w_attn[:, 512:], preferred_element_type=wide)
    grad_mixed = grad_mixed[:, 64:].astype(low_type).reshape(queries.shape)
    scores = jnp.einsum("qgd,td->gqt", queries, key_all, preferred_element_type=wide) * 0.125
    probs = jnp.where(allowed[None], jnp.exp(scores - log_total), 0.0)
    grad_probs = jnp.einsum("qgd,td->gqt", grad_mixed, value_all, preferred_element_type=wide)
    grad_value_all = jnp.einsum(
        "gqt,qgd->td", probs.astype(low_type), grad_mixed, preferred_element_type=wide
    )
    row_delta = jnp.sum(grad_probs * probs, axis=-1, keepdims=True)
    grad_scores = (probs * (grad_probs - row_delta)).astype(low_type)
    grad_queries = (
        jnp.einsum("gqt,td->qgd", grad_scores, key_all, preferred_element_type=wide) * 0.125
    )
    grad_key_all = (
        jnp.einsum("gqt,qgd->td", grad_scores, queries, preferred_element_type=wide) * 0.125
    )
    grad_key_value = jnp.concatenate([grad_key_all, grad_value_all], axis=1).astype(low_type)
    grad_key_value = collect(grad_key_value.reshape(-1, row_count, 2 * HD))
    grad_projected = jnp.concatenate(
        [
            rotate_back(grad_queries, cosine[:, None, :], sine[:, None, :]).reshape(row_count, 448),
            rotate_back(grad_key_value[:, :HD], cosine, sine),
            grad_key_value[:, HD:],
            jnp.zeros((row_count, HD), wide),
        ],
        axis=1,
    ).astype(low_type)
    return grad_branch, grad_projected


def backward_in(grad_projected, grad_middle, kept, weights):
    attn_gain, mlp_gain, bias, w_attn = weights
    resid, scale_one = kept[:2]
    grad_normed_in = tensor_sum(contract(grad_projected, w_attn[:, :640], 1, 1))
    grad_attn_gain, grad_resid = norm_backward(grad_normed_in, resid, scale_one, attn_gain)
    return (grad_resid + grad_middle).astype(low_type), grad_attn_gain


def attn_weight_grads(grad_branch, grad_projected, kept):
    normed_in, mixed = kept[2], kept[7]
    grad_bias = jnp.sum(grad_projected.astype(wide), axis=0)
    projection = contract(normed_in, grad_projected, 0, 0)
    output = contract(grad_branch, mixed, 0, 0)
    latter = jnp.pad(projection[:, 512:], ((0, 0), (0, 384))) + output
    return jnp.concatenate([projection[:, :512], latter], axis=1).astype(low_type), grad_bias


def row_blocks(blocks):
    return [blocks[steps] for steps in (0, 1, 3, 2)]


def send_rows(pieces):
    return [turn_y(piece, -steps) for steps, piece in zip((1, 3, 2), pieces)]


def add_all(pieces):
    return sum(piece.astype(wide) for piece in pieces).astype(low_type)


def split_columns(blocks, section_place):
    return pick(blocks, section_place, 1), pick(blocks, 1 - section_place, 1)


def halve(kept, sent):
    return (kept.astype(wide) + turn(sent, "section", 1).astype(wide)).astype(low_type)


def to_column(block):
    return lax.ppermute(
        block, ("section", "fsdp"), [(8 + place, place ^ 1) for place in range(8)]
    )


def to_owner(block):
    return lax.ppermute(block, "section", [(0, 1)])


def pack_lines(small, block_order):
    grad_attn_gain, grad_mlp_gain, grad_bias = small
    queries_keys = jnp.pad(grad_bias[:512].reshape(8, 64), ((0, 0), (0, 64)))
    values = jnp.pad(grad_bias[512:576].reshape(8, 8), ((0, 0), (0, 632)))
    grad_bias = jnp.concatenate([queries_keys, values], axis=1).astype(low_type)
    grad_bias = jnp.dot(block_order, grad_bias, preferred_element_type=wide)
    lines = jnp.concatenate(
        [
            jnp.pad(grad_attn_gain.reshape(8, 112), ((0, 0), (0, 16))),
            jnp.pad(grad_mlp_gain.reshape(8, 112), ((0, 0), (0, 16))),
            grad_bias,
        ],
        axis=1,
    ).astype(low_type)
    return jnp.pad(lines[:, None], ((0, 0), (0, 15), (0, 0))).reshape(4, 2, 16, 1024)


def ctx_blocks(blocks, lines, ctx_place):
    quarters = []
    for steps in (0, 1, 3, 2):
        start = (ctx_place - steps) % 4 * 256
        quarters.append(
            jnp.concatenate(
                [
                    lax.dynamic_slice_in_dim(blocks, start, 256, 2),
                    lax.dynamic_slice_in_dim(lines, start, 256, 2),
                ],
                axis=1,
            )
        )
    return quarters


def send_ctx(pieces):
    return [turn(piece, "ctx", -steps) for steps, piece in zip((1, 3, 2), pieces)]


def per_device(
    layer_input, cotangent, doc_lengths, attn_gain, w_qkv, b_qkv, w_out, mlp_gain, w_gate_up, w_down
):
    section_place = lax.axis_index("section")
    fsdp_place = lax.axis_index("fsdp")
    row_place, column_place = fsdp_place // 2, fsdp_place % 2
    ctx_place = lax.axis_index("ctx")
    places = (section_place, row_place, column_place, ctx_place)
    row_count, width = layer_input.shape[1:]
    units_all = w_down.shape[1]

    line = jnp.concatenate(
        [
            jnp.pad(attn_gain, ((0, 0), (0, 16))),
            jnp.pad(mlp_gain, ((0, 0), (0, 16))),
            jnp.pad(b_qkv[0], ((0, 0), (0, 696))),
        ],
        axis=1,
    )
    attn_block = jnp.concatenate(
        [
            jnp.concatenate([w_qkv[0, :, 0], w_out[0].T], axis=1),
            jnp.pad(line, ((0, 15), (0, 0))),
        ],
        axis=0,
    )
    past = 4 * UNITS - units_all
    mlp_block = jnp.concatenate(
        [
            jnp.pad(w_gate_up[0], ((0, 0), (0, 0), (0, past))),
            jnp.pad(w_down[0].T, ((0, 0), (0, past)))[:, None],
        ],
        axis=1,
    )
    mlp_block = lax.dynamic_slice_in_dim(mlp_block, ctx_place * UNITS, UNITS, 2)
    mlp_block = jnp.pad(mlp_block.reshape(112, 3 * UNITS), ((0, 0), (0, 128)))

    rank = jnp.arange(8, dtype=jnp.int32)
    owner = (row_place - rank // 2) % 4 * 2 + (column_place + rank) % 2
    block_order = (owner[:, None] == rank[None, :]).astype(low_type)
    columns = jnp.arange(width, dtype=jnp.int32)
    source = jnp.repeat(owner, 112) * 112 + columns % 112
    order = (columns[:, None] == source[None, :]).astype(low_type)

    def reorder(rows):
        return jnp.dot(rows, order, preferred_element_type=wide).astype(low_type)

    def restore(rows):
        return contract(rows, order, 1, 1).astype(low_type)

    first = section_place == 0
    layer_in = reorder(pick(layer_input, section_place, 0))
    grads_last = reorder(pick(cotangent, section_place, 0))
    tables = mask_tables(pick(doc_lengths, section_place, 0)[0], ctx_place, row_count, 4)

    half_attn, late_attn = halves_by_layer(attn_block, section_place)
    half_mlp, late_mlp = halves_by_layer(mlp_block, section_place)
    pair_attn = with_column(half_attn, flip_x(half_attn))
    pair_attn, half_mlp, layer_in = after(pair_attn, half_mlp, layer_in)
    rows_attn = turn_rows(pair_attn)
    pair_mlp = with_column(half_mlp, flip_x(half_mlp))
    rows_all = turn_ctx(layer_in)
    pair_attn, pair_mlp, layer_in, *others = after(
        pair_attn, pair_mlp, layer_in, *rows_attn, *rows_all
    )
    rows_attn, rows_all = others[:3], others[3:]
    rows_mlp = turn_rows(pair_mlp)
    part = with_rows(pair_attn, rows_attn)
    weights_zero = split_attn(
        with_halves(part, turn(part, "section", 1), section_place), block_order
    )
    rows_all = in_order([layer_in] + rows_all, ctx_place).reshape(-1, width)

    branch, kept_attn_zero = forward_attn(layer_in, rows_all, weights_zero, tables)
    branch, pair_mlp, late_attn, late_mlp, grads_last, *rows_mlp = after(
        branch, pair_mlp, late_attn, late_mlp, grads_last, *rows_mlp
    )
    part = with_rows(pair_mlp, rows_mlp)
    mlp_other = turn(part, "section", 1)
    pair_attn = with_column(late_attn, flip_x(late_attn))
    pair_mlp = with_column(late_mlp, flip_x(late_mlp))
    grads_all = turn_ctx(grads_last)
    middle, scale_two, normed_mid = forward_mid(branch, kept_attn_zero[0], weights_zero[1])
    normed_mid, part, mlp_other, pair_attn, pair_mlp, *grads_all = after(
        normed_mid, part, mlp_other, pair_attn, pair_mlp, *grads_all
    )
    rows_attn = [turn_y(pair_attn, 1), turn_y(pair_attn, 3)]
    w_mlp_zero = with_halves(part, mlp_other, section_place).reshape(width, 2048)
    normed_mid = spread(normed_mid).reshape(-1, width)
    normed_mid, pair_attn, *rows_attn = after(normed_mid, pair_attn, *rows_attn)
    rows_attn.append(turn_y(pair_attn, 2))
    gate_up, hidden = forward_mlp(normed_mid, w_mlp_zero)
    kept_mlp_zero = (middle, scale_two, normed_mid, gate_up, hidden)
    branch = collect(forward_down(hidden, w_mlp_zero, row_count))
    branch, pair_attn, pair_mlp, *rows_attn = after(branch, pair_attn, pair_mlp, *rows_attn)
    part = with_rows(pair_attn, rows_attn)
    attn_other = turn(part, "section", 1)
    rows_mlp = [turn_y(pair_mlp, 1), turn_y(pair_mlp, 3)]
    out_zero = (middle + tensor_sum(branch)).astype(low_type)
    out_zero, part, attn_other, pair_mlp, *rows_mlp = after(
        out_zero, part, attn_other, pair_mlp, *rows_mlp
    )
    rows_mlp.append(turn_y(pair_mlp, 2))
    weights_one = split_attn(with_halves(part, attn_other, section_place), block_order)

    branch, kept_attn_one = forward_attn(out_zero, None, weights_one, tables)
    branch, pair_mlp, *rows_mlp = after(branch, pair_mlp, *rows_mlp)
    part = with_rows(pair_mlp, rows_mlp)
    mlp_other = turn(part, "section", 1)
    middle, scale_two, normed_mid = forward_mid(branch, kept_attn_one[0], weights_one[1])
    w_mlp_one = with_halves(part, mlp_other, section_place).reshape(width, 2048)
    normed_mid = spread(normed_mid).reshape(-1, width)
    grads_all = in_order([grads_last] + grads_all, ctx_place).reshape(-1, width)
    normed_mid, w_mlp_one, grads_all = after(normed_mid, w_mlp_one, grads_all)
    gate_up, hidden = forward_mlp(normed_mid, w_mlp_one)
    kept_mlp_one = (middle, scale_two, normed_mid, gate_up, hidden)

    mlp_shape = (4, 2, 112, 3 * UNITS)
    attn_shape = (4, 2, 112, 1024)
    branch, mlp_one = backward_mlp(grads_all, kept_mlp_one, w_mlp_one)
    branch = collect(branch)
    down = forward_down(hidden, w_mlp_one, row_count)
    down = [pick(down, (ctx_place - steps) % 4, 0) for steps in (0, 1, 3, 2)]
    branch, mlp_keep, mlp_sent, *down = after(
        branch, *split_columns(mlp_one.reshape(mlp_shape), section_place), *down
    )
    down_moved = send_ctx(down[1:])
    mlp_pieces = row_blocks(halve(mlp_keep, mlp_sent))
    middle_one, gain_one = backward_mid(branch, grads_last, kept_mlp_one, weights_one[1])
    middle_one, *pieces = after(middle_one, down[0], *down_moved, *mlp_pieces)
    down, mlp_pieces = sum(piece.astype(wide) for piece in pieces[:4]), pieces[4:]
    mlp_moved = send_rows(mlp_pieces[1:3])
    out_one = (kept_mlp_one[0] + tensor_sum(down)).astype(low_type)
    branch_one, projected_one = backward_attn(middle_one, kept_attn_one, weights_one, tables)
    projected_one, out_one, *pieces = after(
        projected_one, out_one, mlp_pieces[0], mlp_pieces[3], *mlp_moved
    )
    mlp_pieces = [pieces[0], pieces[2], pieces[3], turn_y(pieces[1], -2)]
    grads_one, attn_gain_one = backward_in(projected_one, middle_one, kept_attn_one, weights_one)
    attn_one, bias_one = attn_weight_grads(branch_one, projected_one, kept_attn_one)
    lines_one = pack_lines((attn_gain_one, gain_one, bias_one), block_order)
    grads_one, *mlp_pieces = after(grads_one, *mlp_pieces)

    mlp_one = add_all(mlp_pieces)
    mlp_one_moved = to_column(mlp_one)
    attn_sums = halve(*split_columns(attn_one.reshape(attn_shape), section_place))
    line_sums = halve(*split_columns(lines_one, section_place))
    grads_all = spread(grads_one).reshape(-1, width)
    grads_all, mlp_one, mlp_one_moved, attn_sums, line_sums = after(
        grads_all, mlp_one, mlp_one_moved, attn_sums, line_sums
    )
    mlp_one = add_all([mlp_one, mlp_one_moved])
    branch, mlp_zero = backward_mlp(grads_all, kept_mlp_zero, w_mlp_zero)
    branch = collect(branch)
    branch, mlp_keep, mlp_sent, mlp_one, *attn_pieces = after(
        branch,
        *split_columns(mlp_zero.reshape(mlp_shape), section_place),
        mlp_one,
        *ctx_blocks(attn_sums, line_sums, ctx_place),
    )
    mlp_pieces = row_blocks(halve(mlp_keep, mlp_sent))
    attn_moved = send_ctx(attn_pieces[1:])
    mlp_one = to_owner(mlp_one)
    middle_zero, gain_zero = backward_mid(branch, grads_one, kept_mlp_zero, weights_zero[1])
    middle_zero, mlp_one, *pieces = after(
        middle_zero, mlp_one, attn_pieces[0], *attn_moved, *mlp_pieces
    )
    attn_one, mlp_pieces = add_all(pieces[:4]), pieces[4:]
    mlp_moved = send_rows(mlp_pieces[1:3])
    branch_zero, projected_zero = backward_attn(middle_zero, kept_attn_zero, weights_zero, tables)
    projected_zero, *pieces = after(projected_zero, mlp_pieces[0], mlp_pieces[3], *mlp_moved)
    mlp_pieces = [pieces[0], pieces[2], pieces[3], turn_y(pieces[1], -2)]
    attn_zero, bias_zero = attn_weight_grads(branch_zero, projected_zero, kept_attn_zero)
    attn_sums = halve(*split_columns(attn_zero.reshape(attn_shape), section_place))
    grads_zero, attn_gain_zero = backward_in(
        projected_zero, middle_zero, kept_attn_zero, weights_zero
    )
    lines_zero = pack_lines((attn_gain_zero, gain_zero, bias_zero), block_order)
    line_sums = halve(*split_columns(lines_zero, section_place))
    attn_pieces = ctx_blocks(attn_sums, line_sums, ctx_place)
    attn_pieces[0], *rest = after(attn_pieces[0], *attn_pieces[1:], *mlp_pieces)

    attn_moved = send_ctx(rest[:3])
    mlp_zero = add_all(rest[3:])
    mlp_moved = to_column(mlp_zero)
    attn_zero = add_all([attn_pieces[0]] + attn_moved)
    attn_zero, attn_one, mlp_zero, mlp_moved = after(attn_zero, attn_one, mlp_zero, mlp_moved)
    mlp = jnp.where(first, add_all([mlp_zero, mlp_moved]), mlp_one)
    attn_pieces = row_blocks(jnp.stack([attn_zero, attn_one], axis=1))
    attn_moved = send_rows(attn_pieces[1:])
    mlp_all = turn_ctx(mlp)[:2]
    attn_both = add_all(attn_pieces[:1] + attn_moved)
    attn_both, mlp = after(attn_both, mlp)
    mlp_all.append(turn(mlp, "ctx", 2))
    attn_both = add_all([attn_both, to_column(attn_both)])
    attn = jnp.where(first, attn_both[0], to_owner(attn_both[1]))
    attn, mlp, *mlp_all = after(attn, mlp, *mlp_all)
    attn_all = turn_ctx(attn)
    mlp = in_order([mlp] + mlp_all, ctx_place).reshape(4, 112, 3, UNITS)
    attn = in_order([attn] + attn_all, ctx_place)
    outputs = [restore(out_zero), restore(out_one)]

    def by_layer(values):
        own = jnp.where(first, values[0], values[1])
        other = turn(jnp.where(first, values[1], values[0]), "section", 1)
        return jnp.where(first, jnp.stack([own, other]), jnp.stack([other, own]))[None]

    hidden_states = by_layer(outputs)
    input_grads = by_layer([restore(grads_zero), restore(grads_one)])
    attn = attn.transpose(1, 0, 2).reshape(128, 1024).astype(wide)
    gate_up = mlp[:, :, :2].transpose(1, 2, 0, 3).reshape(112, 2, 4 * UNITS)[:, :, :units_all]
    down = mlp[:, :, 2].transpose(0, 2, 1).reshape(4 * UNITS, 112)[:units_all]
    lines = attn[112:113]
    return (
        hidden_states,
        input_grads,
        lines[:, :112],
        attn[None, :112, None, :576],
        lines[None, :, 256:320],
        lines[None, :, 384:392],
        attn[:112, 576:].T[None],
        lines[:, 128:240],
        gate_up.astype(wide)[None],
        down.astype(wide)[None],
    )


def solution(mesh):
    return jax.shard_map(
        per_device,
        mesh=mesh,
        in_specs=(
            P(None, ("fsdp", "ctx"), None),
            P(None, ("fsdp", "ctx"), None),
            P(None, "fsdp", None),
            P("section", "fsdp"),
            P("section", "fsdp", "tp", None),
            P("section", "tp", "fsdp"),
            P("section", "tp", "fsdp"),
            P("section", "fsdp"),
            P("section", "fsdp", None, "tp"),
            P("section", "tp", "fsdp"),
        ),
        out_specs=(
            P("section", None, ("fsdp", "ctx"), None),
            P("section", None, ("fsdp", "ctx"), None),
            P("section", "fsdp"),
            P("section", "fsdp", "tp", None),
            P("section", "tp", "fsdp"),
            P("section", "tp", "fsdp"),
            P("section", "tp", "fsdp"),
            P("section", "fsdp"),
            P("section", "fsdp", None, "tp"),
            P("section", "tp", "fsdp"),
        ),
        check_vma=False,
    )
```

```python
import jax
import jax.numpy as jnp
from jax import lax
from jax.experimental import pallas as pl
from jax.experimental.pallas import tpu as pltpu
from jax.sharding import PartitionSpec as P

HD = 64
UNITS = 640

epsilon = 1e-06
rope_base = 1000000.0
masked_score = -1000000000.0
low_type = jnp.bfloat16
wide = jnp.float32


def contract(left, right, left_dim, right_dim):
    return lax.dot_general(
        left, right, (((left_dim,), (right_dim,)), ((), ())), preferred_element_type=wide
    )


def turn(value, axis, steps):
    count = lax.axis_size(axis)
    return lax.ppermute(value, axis, [(place, (place + steps) % count) for place in range(count)])


def turn_y(value, steps):
    count = lax.axis_size("fsdp")
    return lax.ppermute(
        value, "fsdp", [(place, (place + 2 * steps) % count) for place in range(count)]
    )


def flip_x(value):
    count = lax.axis_size("fsdp")
    return lax.ppermute(value, "fsdp", [(place, place ^ 1) for place in range(count)])


def collect(blocks, axis):
    count = lax.axis_size(axis)
    order = [1, count - 1] + list(range(2, count - 1))
    total = blocks[0].astype(wide)
    for steps in order:
        total = total + turn(blocks[steps], axis, -steps).astype(wide)
    return total


def pick(array, place, axis):
    return lax.dynamic_index_in_dim(array, place, axis, keepdims=False)


def turn_ctx(block):
    return [turn(block, "ctx", steps) for steps in (1, 3, 2)]


def stack_rows(own, moved):
    former, latter, opposite = moved
    return jnp.concatenate([own, former, opposite, latter], axis=0)


def tensor_sum(partial_value):
    own = lax.optimization_barrier(partial_value.astype(low_type))
    return own.astype(wide) + turn(own, "tp", 1).astype(wide)


def after(value, *others):
    tied = lax.optimization_barrier((value,) + others)
    return tied[0] if not others else tied


def with_column(half, received, column_place):
    pair = jnp.zeros((2,) + half.shape, half.dtype)
    pair = lax.dynamic_update_slice(pair, half[None], (column_place, 0, 0))
    return lax.dynamic_update_slice(pair, received[None], (1 - column_place, 0, 0))


def turn_rows(pair):
    return [turn_y(pair, steps) for steps in (1, 3, 2)]


def swap_all(pieces):
    return [turn(piece, "section", 1) for piece in pieces]


def place_copies(lines, row_count, places, *refs):
    pieces, outs, sems = refs[:8], refs[8:-1], refs[-1]
    columns = pieces[0].shape[2]
    copies = []
    for index, piece in enumerate(pieces):
        row = lax.rem(places[0] + 4 - (0, 1, 3, 2)[index % 4], 4)
        half = places[1] if index < 4 else 1 - places[1]
        where = (pl.ds(row * 2, 2), slice(None), pl.ds(pl.multiple_of(half * columns, 128), columns))
        source = piece.at[:, pl.ds(0, row_count), :]
        copies.append(pltpu.make_async_copy(source, outs[0].at[where], sems.at[index]))
        if lines:
            source = piece.at[:, pl.ds(row_count, lines), :]
            copies.append(pltpu.make_async_copy(source, outs[1].at[where], sems.at[8 + index]))
    for copy in copies:
        copy.start()
    for copy in copies:
        copy.wait()


def put_together(pieces, others, places, lines):
    rows, columns = pieces[0].shape[1:]
    shapes = [jax.ShapeDtypeStruct((8, rows - lines, 2 * columns), low_type)]
    if lines:
        shapes.append(jax.ShapeDtypeStruct((8, lines, 2 * columns), low_type))
    place = jnp.stack([places[1], places[0]]).astype(jnp.int32)
    size = 8 * rows * 2 * columns * 2
    return pl.pallas_call(
        lambda *refs: place_copies(lines, rows - lines, *refs),
        out_shape=shapes,
        in_specs=[pl.BlockSpec(memory_space=pltpu.SMEM)] + [pl.BlockSpec(memory_space=pl.ANY)] * 8,
        out_specs=[pl.BlockSpec(memory_space=pl.ANY)] * len(shapes),
        scratch_shapes=[pltpu.SemaphoreType.DMA((16,))],
        cost_estimate=pl.CostEstimate(flops=0, bytes_accessed=2 * size, transcendentals=0),
    )(place, *pieces, *others)


def attn_weights(pieces, others, places):
    width = 8 * 112
    w_attn, lines = put_together(pieces, others, places, 16)
    lines = lines[:, 0].astype(wide)
    return (
        lines[:, :112].reshape(width),
        lines[:, 128:240].reshape(width),
        jnp.pad(lines[:, 256:328].reshape(576), (0, 64)),
        w_attn.reshape(width, 1024),
    )


def mlp_weights(pieces, others, places):
    return put_together(pieces, others, places, 0)[0].reshape(8 * 112, 2048)


def halves_by_layer(block, section_place):
    columns = block.shape[1] // 2
    kept = lax.dynamic_slice_in_dim(block, section_place * columns, columns, 1)
    sent = lax.dynamic_slice_in_dim(block, (1 - section_place) * columns, columns, 1)
    received = turn(sent, "section", 1)
    first = section_place == 0
    return jnp.where(first, kept, received), jnp.where(first, received, kept)


def rotary_tables(position):
    inverse = rope_base ** (-jnp.arange(0, HD, 2, dtype=wide) / HD)
    angles = position.astype(wide)[..., None] * inverse
    angles = jnp.concatenate([angles, angles], axis=-1)
    return (jnp.cos(angles), jnp.sin(angles))


def rotate(values, cosine, sine):
    half_width = values.shape[-1] // 2
    turned = jnp.concatenate([-values[..., half_width:], values[..., :half_width]], axis=-1)
    return values * cosine + turned * sine


def rotate_back(grads, cosine, sine):
    half_width = grads.shape[-1] // 2
    scaled = grads * sine
    turned = jnp.concatenate([scaled[..., half_width:], -scaled[..., :half_width]], axis=-1)
    return grads * cosine + turned


def norm_backward(grad_normed, resid, scale, gain):
    grad_gain = jnp.sum(grad_normed * resid * scale, axis=0)
    inner = grad_normed * gain
    grad_resid = scale * inner - resid * (scale * scale * scale) * jnp.mean(
        inner * resid, axis=-1, keepdims=True
    )
    return (grad_gain, grad_resid)


def mask_tables(lengths, ctx_place, row_count, ctx_count):
    doc_ends = jnp.cumsum(lengths, axis=-1)
    blocks = (ctx_place - jnp.arange(ctx_count, dtype=jnp.int32)) % ctx_count
    places = (blocks[:, None] * row_count + jnp.arange(row_count, dtype=jnp.int32)).reshape(-1)
    passed = places[:, None] >= doc_ends[None, :]
    segment = jnp.sum(passed.astype(jnp.int32), axis=-1)
    doc_start = jnp.sum(jnp.where(passed, lengths[None, :], 0), axis=-1)
    position = places - doc_start
    cosine, sine = rotary_tables(position)
    allowed = (segment[:row_count, None] == segment[None, :]) & (
        places[:row_count, None] >= places[None, :]
    )
    return (allowed, cosine[:row_count], sine[:row_count], cosine, sine)


def normed(resid, gain):
    scale = lax.rsqrt(jnp.mean(resid * resid, axis=-1, keepdims=True) + epsilon)
    return scale, (resid * scale * gain).astype(low_type)


def forward_attn(layer_in, rows_all, weights, tables):
    attn_gain, mlp_gain, bias, w_attn = weights
    allowed, cosine, sine, cosine_all, sine_all = tables
    row_count, width = layer_in.shape
    resid = layer_in.astype(wide)
    scale_one, normed_in = normed(resid, attn_gain)
    projected = jnp.dot(normed_in, w_attn[:, :640], preferred_element_type=wide) + bias
    queries = rotate(
        projected[:, :448].reshape(row_count, 7, HD), cosine[:, None, :], sine[:, None, :]
    ).astype(low_type)
    if rows_all is None:
        key_own = rotate(projected[:, 448:512], cosine, sine)
        key_value = jnp.concatenate([key_own, projected[:, 512:576]], axis=1).astype(low_type)
        key_value = stack_rows(key_value, turn_ctx(key_value))
    else:
        normed_all = normed(rows_all.astype(wide), attn_gain)[1]
        projected = jnp.dot(normed_all, w_attn[:, 384:640], preferred_element_type=wide)
        projected = projected + bias[384:640]
        key_value = jnp.concatenate(
            [rotate(projected[:, 64:128], cosine_all, sine_all), projected[:, 128:192]], axis=1
        ).astype(low_type)
    key_all, value_all = key_value[:, :HD], key_value[:, HD:]
    scores = jnp.einsum("qgd,td->gqt", queries, key_all, preferred_element_type=wide) * 0.125
    scores = jnp.where(allowed[None], scores, masked_score)
    largest = jnp.max(scores, axis=-1, keepdims=True)
    raised = jnp.exp(scores - largest)
    totals = jnp.sum(raised, axis=-1, keepdims=True)
    log_total = largest + jnp.log(totals)
    probs = (raised / totals).astype(low_type)
    mixed = jnp.einsum("gqt,td->qgd", probs, value_all, preferred_element_type=wide)
    mixed = jnp.pad(mixed.reshape(row_count, 448).astype(low_type), ((0, 0), (64, 0)))
    kept = (resid, scale_one, normed_in, queries, key_all, value_all, log_total, mixed)
    return contract(mixed, w_attn[:, 512:], 1, 1), kept


def forward_mid(branch, resid, mlp_gain):
    middle = resid + tensor_sum(branch)
    return middle, *normed(middle, mlp_gain)


def forward_mlp(normed_mid, w_mlp):
    gate_up = jnp.dot(normed_mid, w_mlp[:, : 2 * UNITS], preferred_element_type=wide)
    hidden = (jax.nn.silu(gate_up[:, :UNITS]) * gate_up[:, UNITS:]).astype(low_type)
    return gate_up, hidden


def forward_down(hidden, w_mlp, row_count):
    branch = contract(hidden, w_mlp[:, 2 * UNITS : 3 * UNITS], 1, 1).astype(low_type)
    return list(branch.reshape(-1, row_count, branch.shape[1]))


def backward_mlp(grad_all, kept, w_mlp):
    middle, scale_two, normed_mid, gate_up, hidden = kept
    row_count, width = middle.shape
    grad_hidden = jnp.dot(grad_all, w_mlp[:, 2 * UNITS : 3 * UNITS], preferred_element_type=wide)
    gate = gate_up[:, :UNITS]
    upward = gate_up[:, UNITS:]
    sigmoid = jax.nn.sigmoid(gate)
    grad_gate = grad_hidden * upward * sigmoid * (1.0 + gate * (1.0 - sigmoid))
    grad_upward = grad_hidden * gate * sigmoid
    grad_gate_up = jnp.concatenate([grad_gate, grad_upward], axis=1).astype(low_type)
    branch = contract(grad_gate_up, w_mlp[:, : 2 * UNITS], 1, 1).astype(low_type)
    branch = branch.reshape(-1, row_count, width)
    grad_mlp = jnp.concatenate(
        [
            contract(normed_mid, grad_gate_up, 0, 0).astype(low_type),
            contract(grad_all, hidden, 0, 0).astype(low_type),
        ],
        axis=1,
    )
    return branch, grad_mlp


def backward_mid(branch, grad_out, kept, mlp_gain):
    middle, scale_two = kept[:2]
    grad_normed_mid = tensor_sum(branch)
    grad_mlp_gain, grad_middle = norm_backward(grad_normed_mid, middle, scale_two, mlp_gain)
    return grad_middle + grad_out.astype(wide), grad_mlp_gain


def backward_attn(grad_middle, kept, weights, tables):
    attn_gain, mlp_gain, bias, w_attn = weights
    allowed, cosine, sine = tables[:3]
    resid, scale_one, normed_in, queries, key_all, value_all, log_total, mixed = kept
    row_count, width = resid.shape
    grad_branch = grad_middle.astype(low_type)
    grad_mixed = jnp.dot(grad_branch, w_attn[:, 512:], preferred_element_type=wide)
    grad_mixed = grad_mixed[:, 64:].astype(low_type).reshape(queries.shape)
    scores = jnp.einsum("qgd,td->gqt", queries, key_all, preferred_element_type=wide) * 0.125
    probs = jnp.where(allowed[None], jnp.exp(scores - log_total), 0.0)
    grad_probs = jnp.einsum("qgd,td->gqt", grad_mixed, value_all, preferred_element_type=wide)
    grad_value_all = jnp.einsum(
        "gqt,qgd->td", probs.astype(low_type), grad_mixed, preferred_element_type=wide
    )
    row_delta = jnp.sum(grad_probs * probs, axis=-1, keepdims=True)
    grad_scores = (probs * (grad_probs - row_delta)).astype(low_type)
    grad_queries = (
        jnp.einsum("gqt,td->qgd", grad_scores, key_all, preferred_element_type=wide) * 0.125
    )
    grad_key_all = (
        jnp.einsum("gqt,qgd->td", grad_scores, queries, preferred_element_type=wide) * 0.125
    )
    grad_key_value = jnp.concatenate([grad_key_all, grad_value_all], axis=1).astype(low_type)
    grad_key_value = collect(list(grad_key_value.reshape(-1, row_count, 2 * HD)), "ctx")
    grad_projected = jnp.concatenate(
        [
            rotate_back(grad_queries, cosine[:, None, :], sine[:, None, :]).reshape(row_count, 448),
            rotate_back(grad_key_value[:, :HD], cosine, sine),
            grad_key_value[:, HD:],
            jnp.zeros((row_count, HD), wide),
        ],
        axis=1,
    ).astype(low_type)
    return grad_branch, grad_projected


def backward_in(grad_projected, grad_middle, kept, weights):
    attn_gain, mlp_gain, bias, w_attn = weights
    resid, scale_one = kept[:2]
    grad_normed_in = tensor_sum(contract(grad_projected, w_attn[:, :640], 1, 1))
    grad_attn_gain, grad_resid = norm_backward(grad_normed_in, resid, scale_one, attn_gain)
    return (grad_resid + grad_middle).astype(low_type), grad_attn_gain


def attn_weight_grads(grad_branch, grad_projected, kept):
    normed_in, mixed = kept[2], kept[7]
    grad_bias = jnp.sum(grad_projected.astype(wide), axis=0)
    projection = contract(normed_in, grad_projected, 0, 0)
    output = contract(grad_branch, mixed, 0, 0)
    latter = jnp.pad(projection[:, 512:], ((0, 0), (0, 384))) + output
    return jnp.concatenate([projection[:, :512], latter], axis=1).astype(low_type), grad_bias


def row_blocks(blocks, row_place, axis):
    return [pick(blocks, (row_place + steps) % 4, axis) for steps in (0, 1, 3, 2)]


def send_rows(pieces):
    return [turn_y(piece, steps) for steps, piece in zip((1, 3, 2), pieces)]


def add_all(pieces):
    return sum(piece.astype(wide) for piece in pieces).astype(low_type)


def split_columns(blocks, section_place):
    return pick(blocks, section_place, 1), pick(blocks, 1 - section_place, 1)


def halve(kept, sent):
    return (kept.astype(wide) + turn(sent, "section", 1).astype(wide)).astype(low_type)


def to_column(block):
    hops = []
    for row in range(4):
        hops.append((8 + 2 * row, 8 + 2 * row + 1))
        hops.append((2 * row + 1, 2 * row))
    return lax.ppermute(block, ("section", "fsdp"), hops)


def own_layer(block_zero, block_one, section_place, column_place):
    first = section_place == 0
    hops = []
    for row in range(4):
        hops.append((2 * row, 8 + 2 * row))
        hops.append((8 + 2 * row + 1, 2 * row + 1))
    own = jnp.where(first, block_zero, block_one)
    sent = jnp.where(first, block_one, block_zero)
    received = lax.ppermute(sent, ("section", "fsdp"), hops)
    return jnp.where(section_place == column_place, own, received)


def in_order(pieces, ctx_place):
    own, former, latter, opposite = pieces
    pieces = jnp.stack([own, former, opposite, latter])
    return jnp.stack([pick(pieces, (ctx_place - place) % 4, 0) for place in range(4)])


def pack_lines(small):
    grad_attn_gain, grad_mlp_gain, grad_bias = small
    lines = jnp.concatenate(
        [
            jnp.pad(grad_attn_gain.reshape(8, 112), ((0, 0), (0, 16))),
            jnp.pad(grad_mlp_gain.reshape(8, 112), ((0, 0), (0, 16))),
            jnp.pad(grad_bias[:512].reshape(8, 64), ((0, 0), (0, 64))),
            jnp.pad(grad_bias[512:576].reshape(8, 8), ((0, 0), (0, 632))),
        ],
        axis=1,
    ).astype(low_type)
    return jnp.pad(lines[:, None], ((0, 0), (0, 15), (0, 0))).reshape(4, 2, 16, 1024)


def ctx_blocks(blocks, lines, ctx_place):
    quarters = []
    for steps in (0, 1, 3, 2):
        start = (ctx_place - steps) % 4 * 256
        quarters.append(
            jnp.concatenate(
                [
                    lax.dynamic_slice_in_dim(blocks, start, 256, 2),
                    lax.dynamic_slice_in_dim(lines, start, 256, 2),
                ],
                axis=1,
            )
        )
    return quarters


def send_ctx(pieces):
    return [turn(piece, "ctx", -steps) for steps, piece in zip((1, 3, 2), pieces)]


def per_device(
    layer_input, cotangent, doc_lengths, attn_gain, w_qkv, b_qkv, w_out, mlp_gain, w_gate_up, w_down
):
    section_place = lax.axis_index("section")
    fsdp_place = lax.axis_index("fsdp")
    row_place, column_place = fsdp_place // 2, fsdp_place % 2
    ctx_place = lax.axis_index("ctx")
    places = (section_place, row_place, column_place, ctx_place)
    row_count, width = layer_input.shape[1:]
    units_all = w_down.shape[1]

    line = jnp.concatenate(
        [
            jnp.pad(attn_gain, ((0, 0), (0, 16))),
            jnp.pad(mlp_gain, ((0, 0), (0, 16))),
            jnp.pad(b_qkv[0], ((0, 0), (0, 696))),
        ],
        axis=1,
    )
    attn_block = jnp.concatenate(
        [
            jnp.concatenate([w_qkv[0, :, 0], w_out[0].T], axis=1),
            jnp.pad(line, ((0, 15), (0, 0))),
        ],
        axis=0,
    )
    past = 4 * UNITS - units_all
    mlp_block = jnp.concatenate(
        [
            jnp.pad(w_gate_up[0], ((0, 0), (0, 0), (0, past))),
            jnp.pad(w_down[0].T, ((0, 0), (0, past)))[:, None],
        ],
        axis=1,
    )
    mlp_block = lax.dynamic_slice_in_dim(mlp_block, ctx_place * UNITS, UNITS, 2)
    mlp_block = jnp.pad(mlp_block.reshape(112, 3 * UNITS), ((0, 0), (0, 128)))

    first = section_place == 0
    layer_in = pick(layer_input, section_place, 0)
    grads_last = pick(cotangent, section_place, 0)
    tables = mask_tables(pick(doc_lengths, section_place, 0)[0], ctx_place, row_count, 4)

    rows_all = turn_ctx(layer_in)
    half_attn, late_attn = halves_by_layer(attn_block, section_place)
    half_mlp, late_mlp = halves_by_layer(mlp_block, section_place)
    pair_attn = with_column(half_attn, flip_x(half_attn), column_place)
    pair_attn, half_mlp, layer_in, *rows_all = after(pair_attn, half_mlp, layer_in, *rows_all)
    rows_attn = turn_rows(pair_attn)
    pair_mlp = with_column(half_mlp, flip_x(half_mlp), column_place)
    pair_attn, pair_mlp, grads_last, *rows_attn = after(
        pair_attn, pair_mlp, grads_last, *rows_attn
    )
    rows_mlp = turn_rows(pair_mlp)
    pieces = [pair_attn] + rows_attn
    weights_zero = attn_weights(pieces, swap_all(pieces), places)
    rows_all = stack_rows(layer_in, rows_all)
    grads_all = turn_ctx(grads_last)

    branch, kept_attn_zero = forward_attn(layer_in, rows_all, weights_zero, tables)
    branch, late_attn, late_mlp, *pieces = after(
        branch, late_attn, late_mlp, pair_mlp, *rows_mlp, *grads_all
    )
    pieces, grads_all = pieces[:4], pieces[4:]
    others = swap_all(pieces)
    pair_attn = with_column(late_attn, flip_x(late_attn), column_place)
    pair_mlp = with_column(late_mlp, flip_x(late_mlp), column_place)
    middle, scale_two, normed_mid = forward_mid(branch, kept_attn_zero[0], weights_zero[1])
    normed_mid, pair_attn, pair_mlp, *pieces = after(
        normed_mid, pair_attn, pair_mlp, *pieces, *others
    )
    rows_attn = [turn_y(pair_attn, 1), turn_y(pair_attn, 3)]
    w_mlp_zero = mlp_weights(pieces[:4], pieces[4:], places)
    normed_mid = stack_rows(normed_mid, turn_ctx(normed_mid))
    normed_mid, pair_attn, *rows_attn = after(normed_mid, pair_attn, *rows_attn)
    rows_attn.append(turn_y(pair_attn, 2))
    gate_up, hidden = forward_mlp(normed_mid, w_mlp_zero)
    kept_mlp_zero = (middle, scale_two, normed_mid, gate_up, hidden)
    branch = collect(forward_down(hidden, w_mlp_zero, row_count), "ctx")
    branch, pair_mlp, *pieces = after(branch, pair_mlp, pair_attn, *rows_attn)
    others = swap_all(pieces)
    rows_mlp = [turn_y(pair_mlp, 1), turn_y(pair_mlp, 3)]
    out_zero = (middle + tensor_sum(branch)).astype(low_type)
    out_zero, pair_mlp, *rest = after(out_zero, pair_mlp, *rows_mlp, *pieces, *others)
    rows_mlp = rest[:2] + [turn_y(pair_mlp, 2)]
    weights_one = attn_weights(rest[2:6], rest[6:], places)

    branch, kept_attn_one = forward_attn(out_zero, None, weights_one, tables)
    branch, *pieces = after(branch, pair_mlp, *rows_mlp)
    others = swap_all(pieces)
    middle, scale_two, normed_mid = forward_mid(branch, kept_attn_one[0], weights_one[1])
    normed_mid, *pieces = after(normed_mid, *pieces, *others)
    w_mlp_one = mlp_weights(pieces[:4], pieces[4:], places)
    grads_all = stack_rows(grads_last, grads_all)
    normed_mid = stack_rows(normed_mid, turn_ctx(normed_mid))
    gate_up, hidden = forward_mlp(normed_mid, w_mlp_one)
    kept_mlp_one = (middle, scale_two, normed_mid, gate_up, hidden)

    mlp_shape = (4, 2, 112, 3 * UNITS)
    attn_shape = (4, 2, 112, 1024)
    branch, mlp_one = backward_mlp(grads_all, kept_mlp_one, w_mlp_one)
    branch = collect(list(branch), "ctx")
    down = forward_down(hidden, w_mlp_one, row_count)
    down = [down[steps] for steps in (0, 1, 3, 2)]
    branch, mlp_keep, mlp_sent, *down = after(
        branch, *split_columns(mlp_one.reshape(mlp_shape), section_place), *down
    )
    down_moved = send_ctx(down[1:])
    mlp_pieces = row_blocks(halve(mlp_keep, mlp_sent), row_place, 0)
    middle_one, gain_one = backward_mid(branch, grads_last, kept_mlp_one, weights_one[1])
    middle_one, *pieces = after(middle_one, down[0], *down_moved, *mlp_pieces)
    down, mlp_pieces = sum(piece.astype(wide) for piece in pieces[:4]), pieces[4:]
    mlp_moved = send_rows(mlp_pieces[1:3])
    out_one = (kept_mlp_one[0] + tensor_sum(down)).astype(low_type)
    branch_one, projected_one = backward_attn(middle_one, kept_attn_one, weights_one, tables)
    projected_one, out_one, *pieces = after(
        projected_one, out_one, mlp_pieces[0], mlp_pieces[3], *mlp_moved
    )
    mlp_pieces = [pieces[0], pieces[2], pieces[3], turn_y(pieces[1], 2)]
    grads_one, attn_gain_one = backward_in(projected_one, middle_one, kept_attn_one, weights_one)
    attn_one, bias_one = attn_weight_grads(branch_one, projected_one, kept_attn_one)
    lines_one = pack_lines((attn_gain_one, gain_one, bias_one))
    grads_one, *mlp_pieces = after(grads_one, *mlp_pieces)

    mlp_one = add_all(mlp_pieces)
    mlp_one_moved = to_column(mlp_one)
    attn_sums = halve(*split_columns(attn_one.reshape(attn_shape), section_place))
    line_sums = halve(*split_columns(lines_one, section_place))
    grads_all = stack_rows(grads_one, turn_ctx(grads_one))
    grads_all, mlp_one, mlp_one_moved, attn_sums, line_sums = after(
        grads_all, mlp_one, mlp_one_moved, attn_sums, line_sums
    )
    mlp_one = add_all([mlp_one, mlp_one_moved])
    branch, mlp_zero = backward_mlp(grads_all, kept_mlp_zero, w_mlp_zero)
    branch = collect(list(branch), "ctx")
    branch, mlp_keep, mlp_sent, mlp_one, *attn_pieces = after(
        branch,
        *split_columns(mlp_zero.reshape(mlp_shape), section_place),
        mlp_one,
        *ctx_blocks(attn_sums, line_sums, ctx_place),
    )
    mlp_pieces = row_blocks(halve(mlp_keep, mlp_sent), row_place, 0)
    attn_moved = send_ctx(attn_pieces[1:])
    middle_zero, gain_zero = backward_mid(branch, grads_one, kept_mlp_zero, weights_zero[1])
    middle_zero, *pieces = after(middle_zero, attn_pieces[0], *attn_moved, *mlp_pieces)
    attn_one, mlp_pieces = add_all(pieces[:4]), pieces[4:]
    mlp_moved = send_rows(mlp_pieces[1:3])
    branch_zero, projected_zero = backward_attn(middle_zero, kept_attn_zero, weights_zero, tables)
    projected_zero, *pieces = after(projected_zero, mlp_pieces[0], mlp_pieces[3], *mlp_moved)
    mlp_pieces = [pieces[0], pieces[2], pieces[3], turn_y(pieces[1], 2)]
    attn_zero, bias_zero = attn_weight_grads(branch_zero, projected_zero, kept_attn_zero)
    attn_sums = halve(*split_columns(attn_zero.reshape(attn_shape), section_place))
    grads_zero, attn_gain_zero = backward_in(
        projected_zero, middle_zero, kept_attn_zero, weights_zero
    )
    lines_zero = pack_lines((attn_gain_zero, gain_zero, bias_zero))
    line_sums = halve(*split_columns(lines_zero, section_place))

    attn_pieces = ctx_blocks(attn_sums, line_sums, ctx_place)
    attn_moved = send_ctx(attn_pieces[1:])
    mlp_zero = add_all(mlp_pieces)
    mlp_moved = to_column(mlp_zero)
    attn_zero = add_all([attn_pieces[0]] + attn_moved)
    attn_zero, mlp_zero, mlp_moved = after(attn_zero, mlp_zero, mlp_moved)
    mlp_zero = add_all([mlp_zero, mlp_moved])
    mlp = own_layer(mlp_zero, mlp_one, section_place, column_place)
    attn_pieces = row_blocks(jnp.stack([attn_zero, attn_one]), row_place, 1)
    mlp, *attn_pieces = after(mlp, *attn_pieces)
    mlp_all = [turn(mlp, "ctx", 1), turn(mlp, "ctx", 3)]
    attn_both = add_all(attn_pieces[:1] + send_rows(attn_pieces[1:]))
    attn_both, mlp, *mlp_all = after(attn_both, mlp, *mlp_all)
    mlp_all.append(turn(mlp, "ctx", 2))
    attn_both = add_all([attn_both, to_column(attn_both)])
    attn = own_layer(attn_both[0], attn_both[1], section_place, column_place)
    attn_all = turn_ctx(attn)
    mlp = in_order([mlp] + mlp_all, ctx_place).reshape(4, 112, 3, UNITS)
    attn = in_order([attn] + attn_all, ctx_place)
    outputs = [out_zero, out_one]

    def by_layer(values):
        own = jnp.where(first, values[0], values[1])
        other = turn(jnp.where(first, values[1], values[0]), "section", 1)
        return jnp.where(first, jnp.stack([own, other]), jnp.stack([other, own]))[None]

    hidden_states = by_layer(outputs)
    input_grads = by_layer([grads_zero, grads_one])
    attn = attn.transpose(1, 0, 2).reshape(128, 1024).astype(wide)
    gate_up = mlp[:, :, :2].transpose(1, 2, 0, 3).reshape(112, 2, 4 * UNITS)[:, :, :units_all]
    down = mlp[:, :, 2].transpose(0, 2, 1).reshape(4 * UNITS, 112)[:units_all]
    lines = attn[112:113]
    return (
        hidden_states,
        input_grads,
        lines[:, :112],
        attn[None, :112, None, :576],
        lines[None, :, 256:320],
        lines[None, :, 384:392],
        attn[:112, 576:].T[None],
        lines[:, 128:240],
        gate_up.astype(wide)[None],
        down.astype(wide)[None],
    )


def solution(mesh):
    return jax.shard_map(
        per_device,
        mesh=mesh,
        in_specs=(
            P(None, ("fsdp", "ctx"), None),
            P(None, ("fsdp", "ctx"), None),
            P(None, "fsdp", None),
            P("section", "fsdp"),
            P("section", "fsdp", "tp", None),
            P("section", "tp", "fsdp"),
            P("section", "tp", "fsdp"),
            P("section", "fsdp"),
            P("section", "fsdp", None, "tp"),
            P("section", "tp", "fsdp"),
        ),
        out_specs=(
            P("section", None, ("fsdp", "ctx"), None),
            P("section", None, ("fsdp", "ctx"), None),
            P("section", "fsdp"),
            P("section", "fsdp", "tp", None),
            P("section", "tp", "fsdp"),
            P("section", "tp", "fsdp"),
            P("section", "tp", "fsdp"),
            P("section", "fsdp"),
            P("section", "fsdp", None, "tp"),
            P("section", "tp", "fsdp"),
        ),
        check_vma=False,
    )
```

```python
import jax
import jax.numpy as jnp
from jax import lax
from jax.experimental import pallas as pl
from jax.experimental.pallas import tpu as pltpu
from jax.sharding import PartitionSpec as P

HD = 64
UNITS = 640

epsilon = 1e-06
rope_base = 1000000.0
masked_score = -1000000000.0
low_type = jnp.bfloat16
wide = jnp.float32


def contract(left, right, left_dim, right_dim):
    return lax.dot_general(
        left, right, (((left_dim,), (right_dim,)), ((), ())), preferred_element_type=wide
    )


def turn(value, axis, steps):
    count = lax.axis_size(axis)
    return lax.ppermute(value, axis, [(place, (place + steps) % count) for place in range(count)])


def turn_y(value, steps):
    count = lax.axis_size("fsdp")
    return lax.ppermute(
        value, "fsdp", [(place, (place + 2 * steps) % count) for place in range(count)]
    )


def flip_x(value):
    count = lax.axis_size("fsdp")
    return lax.ppermute(value, "fsdp", [(place, place ^ 1) for place in range(count)])


def collect(blocks, axis):
    count = lax.axis_size(axis)
    order = [1, count - 1] + list(range(2, count - 1))
    total = blocks[0].astype(wide)
    for steps in order:
        total = total + turn(blocks[steps], axis, -steps).astype(wide)
    return total


def pick(array, place, axis):
    return lax.dynamic_index_in_dim(array, place, axis, keepdims=False)


def turn_ctx(block):
    return [turn(block, "ctx", steps) for steps in (1, 3, 2)]


def stack_rows(own, moved):
    former, latter, opposite = moved
    return jnp.concatenate([own, former, opposite, latter], axis=0)


def tensor_sum(partial_value):
    own = lax.optimization_barrier(partial_value.astype(low_type))
    return own.astype(wide) + turn(own, "tp", 1).astype(wide)


def after(value, *others):
    tied = lax.optimization_barrier((value,) + others)
    return tied[0] if not others else tied


def with_column(half, received, column_place):
    pair = jnp.zeros((2,) + half.shape, half.dtype)
    pair = lax.dynamic_update_slice(pair, half[None], (column_place, 0, 0))
    return lax.dynamic_update_slice(pair, received[None], (1 - column_place, 0, 0))


def turn_rows(pair):
    return [turn_y(pair, steps) for steps in (1, 3, 2)]


def swap_all(pieces):
    return [turn(piece, "section", 1) for piece in pieces]


def place_pieces(lines, row_count, places, *refs):
    pieces, outs = refs[:8], refs[8:]
    columns = pieces[0].shape[2]
    for index, piece in enumerate(pieces):
        row = lax.rem(places[0] + 4 - (0, 1, 3, 2)[index % 4], 4)
        half = places[1] if index < 4 else 1 - places[1]
        start = pl.multiple_of(half * columns, 128)
        for column in range(2):
            where = (row * 2 + column, slice(None), pl.ds(start, columns))
            outs[0][where] = piece[column, pl.ds(0, row_count), :]
            if lines:
                outs[1][where] = piece[column, pl.ds(row_count, lines), :]


def put_together(pieces, others, places, lines):
    rows, columns = pieces[0].shape[1:]
    shapes = [jax.ShapeDtypeStruct((8, rows - lines, 2 * columns), low_type)]
    if lines:
        shapes.append(jax.ShapeDtypeStruct((8, lines, 2 * columns), low_type))
    place = jnp.stack([places[1], places[0]]).astype(jnp.int32)
    size = 8 * rows * 2 * columns * 2
    return pl.pallas_call(
        lambda *refs: place_pieces(lines, rows - lines, *refs),
        out_shape=shapes,
        in_specs=[pl.BlockSpec(memory_space=pltpu.SMEM)] + [pl.BlockSpec(memory_space=pltpu.VMEM)] * 8,
        out_specs=[pl.BlockSpec(memory_space=pltpu.VMEM)] * len(shapes),
        compiler_params=pltpu.CompilerParams(vmem_limit_bytes=20 << 20),
        cost_estimate=pl.CostEstimate(flops=0, bytes_accessed=2 * size, transcendentals=0),
    )(place, *pieces, *others)


def attn_weights(pieces, others, places):
    width = 8 * 112
    w_attn, lines = put_together(pieces, others, places, 16)
    lines = lines[:, 0].astype(wide)
    return (
        lines[:, :112].reshape(width),
        lines[:, 128:240].reshape(width),
        jnp.pad(lines[:, 256:328].reshape(576), (0, 64)),
        w_attn.reshape(width, 1024),
    )


def mlp_weights(pieces, others, places):
    return put_together(pieces, others, places, 0)[0].reshape(8 * 112, 2048)


def halves_by_layer(block, section_place):
    columns = block.shape[1] // 2
    kept = lax.dynamic_slice_in_dim(block, section_place * columns, columns, 1)
    sent = lax.dynamic_slice_in_dim(block, (1 - section_place) * columns, columns, 1)
    received = turn(sent, "section", 1)
    first = section_place == 0
    return jnp.where(first, kept, received), jnp.where(first, received, kept)


def rotary_tables(position):
    inverse = rope_base ** (-jnp.arange(0, HD, 2, dtype=wide) / HD)
    angles = position.astype(wide)[..., None] * inverse
    angles = jnp.concatenate([angles, angles], axis=-1)
    return (jnp.cos(angles), jnp.sin(angles))


def rotate(values, cosine, sine):
    half_width = values.shape[-1] // 2
    turned = jnp.concatenate([-values[..., half_width:], values[..., :half_width]], axis=-1)
    return values * cosine + turned * sine


def rotate_back(grads, cosine, sine):
    half_width = grads.shape[-1] // 2
    scaled = grads * sine
    turned = jnp.concatenate([scaled[..., half_width:], -scaled[..., :half_width]], axis=-1)
    return grads * cosine + turned


def norm_backward(grad_normed, resid, scale, gain):
    grad_gain = jnp.sum(grad_normed * resid * scale, axis=0)
    inner = grad_normed * gain
    grad_resid = scale * inner - resid * (scale * scale * scale) * jnp.mean(
        inner * resid, axis=-1, keepdims=True
    )
    return (grad_gain, grad_resid)


def mask_tables(lengths, ctx_place, row_count, ctx_count):
    doc_ends = jnp.cumsum(lengths, axis=-1)
    blocks = (ctx_place - jnp.arange(ctx_count, dtype=jnp.int32)) % ctx_count
    places = (blocks[:, None] * row_count + jnp.arange(row_count, dtype=jnp.int32)).reshape(-1)
    passed = places[:, None] >= doc_ends[None, :]
    segment = jnp.sum(passed.astype(jnp.int32), axis=-1)
    doc_start = jnp.sum(jnp.where(passed, lengths[None, :], 0), axis=-1)
    position = places - doc_start
    cosine, sine = rotary_tables(position)
    allowed = (segment[:row_count, None] == segment[None, :]) & (
        places[:row_count, None] >= places[None, :]
    )
    return (allowed, cosine[:row_count], sine[:row_count], cosine, sine)


def normed(resid, gain):
    scale = lax.rsqrt(jnp.mean(resid * resid, axis=-1, keepdims=True) + epsilon)
    return scale, (resid * scale * gain).astype(low_type)


def forward_attn(layer_in, rows_all, weights, tables):
    attn_gain, mlp_gain, bias, w_attn = weights
    allowed, cosine, sine, cosine_all, sine_all = tables
    row_count, width = layer_in.shape
    resid = layer_in.astype(wide)
    scale_one, normed_in = normed(resid, attn_gain)
    projected = jnp.dot(normed_in, w_attn[:, :640], preferred_element_type=wide) + bias
    queries = rotate(
        projected[:, :448].reshape(row_count, 7, HD), cosine[:, None, :], sine[:, None, :]
    ).astype(low_type)
    if rows_all is None:
        key_own = rotate(projected[:, 448:512], cosine, sine)
        key_value = jnp.concatenate([key_own, projected[:, 512:576]], axis=1).astype(low_type)
        key_value = stack_rows(key_value, turn_ctx(key_value))
    else:
        normed_all = normed(rows_all.astype(wide), attn_gain)[1]
        projected = jnp.dot(normed_all, w_attn[:, 384:640], preferred_element_type=wide)
        projected = projected + bias[384:640]
        key_value = jnp.concatenate(
            [rotate(projected[:, 64:128], cosine_all, sine_all), projected[:, 128:192]], axis=1
        ).astype(low_type)
    key_all, value_all = key_value[:, :HD], key_value[:, HD:]
    scores = jnp.einsum("qgd,td->gqt", queries, key_all, preferred_element_type=wide) * 0.125
    scores = jnp.where(allowed[None], scores, masked_score)
    largest = jnp.max(scores, axis=-1, keepdims=True)
    raised = jnp.exp(scores - largest)
    totals = jnp.sum(raised, axis=-1, keepdims=True)
    log_total = largest + jnp.log(totals)
    probs = (raised / totals).astype(low_type)
    mixed = jnp.einsum("gqt,td->qgd", probs, value_all, preferred_element_type=wide)
    mixed = jnp.pad(mixed.reshape(row_count, 448).astype(low_type), ((0, 0), (64, 0)))
    kept = (resid, scale_one, normed_in, queries, key_all, value_all, log_total, mixed)
    return contract(mixed, w_attn[:, 512:], 1, 1), kept


def forward_mid(branch, resid, mlp_gain):
    middle = resid + tensor_sum(branch)
    return middle, *normed(middle, mlp_gain)


def forward_mlp(normed_mid, w_mlp):
    gate_up = jnp.dot(normed_mid, w_mlp[:, : 2 * UNITS], preferred_element_type=wide)
    hidden = (jax.nn.silu(gate_up[:, :UNITS]) * gate_up[:, UNITS:]).astype(low_type)
    return gate_up, hidden


def forward_down(hidden, w_mlp, row_count):
    branch = contract(hidden, w_mlp[:, 2 * UNITS : 3 * UNITS], 1, 1).astype(low_type)
    return list(branch.reshape(-1, row_count, branch.shape[1]))


def backward_mlp(grad_all, kept, w_mlp):
    middle, scale_two, normed_mid, gate_up, hidden = kept
    row_count, width = middle.shape
    grad_hidden = jnp.dot(grad_all, w_mlp[:, 2 * UNITS : 3 * UNITS], preferred_element_type=wide)
    gate = gate_up[:, :UNITS]
    upward = gate_up[:, UNITS:]
    sigmoid = jax.nn.sigmoid(gate)
    grad_gate = grad_hidden * upward * sigmoid * (1.0 + gate * (1.0 - sigmoid))
    grad_upward = grad_hidden * gate * sigmoid
    grad_gate_up = jnp.concatenate([grad_gate, grad_upward], axis=1).astype(low_type)
    branch = contract(grad_gate_up, w_mlp[:, : 2 * UNITS], 1, 1).astype(low_type)
    branch = branch.reshape(-1, row_count, width)
    grad_mlp = jnp.concatenate(
        [
            contract(normed_mid, grad_gate_up, 0, 0).astype(low_type),
            contract(grad_all, hidden, 0, 0).astype(low_type),
        ],
        axis=1,
    )
    return branch, grad_mlp


def backward_mid(branch, grad_out, kept, mlp_gain):
    middle, scale_two = kept[:2]
    grad_normed_mid = tensor_sum(branch)
    grad_mlp_gain, grad_middle = norm_backward(grad_normed_mid, middle, scale_two, mlp_gain)
    return grad_middle + grad_out.astype(wide), grad_mlp_gain


def backward_attn(grad_middle, kept, weights, tables):
    attn_gain, mlp_gain, bias, w_attn = weights
    allowed, cosine, sine = tables[:3]
    resid, scale_one, normed_in, queries, key_all, value_all, log_total, mixed = kept
    row_count, width = resid.shape
    grad_branch = grad_middle.astype(low_type)
    grad_mixed = jnp.dot(grad_branch, w_attn[:, 512:], preferred_element_type=wide)
    grad_mixed = grad_mixed[:, 64:].astype(low_type).reshape(queries.shape)
    scores = jnp.einsum("qgd,td->gqt", queries, key_all, preferred_element_type=wide) * 0.125
    probs = jnp.where(allowed[None], jnp.exp(scores - log_total), 0.0)
    grad_probs = jnp.einsum("qgd,td->gqt", grad_mixed, value_all, preferred_element_type=wide)
    grad_value_all = jnp.einsum(
        "gqt,qgd->td", probs.astype(low_type), grad_mixed, preferred_element_type=wide
    )
    row_delta = jnp.sum(grad_probs * probs, axis=-1, keepdims=True)
    grad_scores = (probs * (grad_probs - row_delta)).astype(low_type)
    grad_queries = (
        jnp.einsum("gqt,td->qgd", grad_scores, key_all, preferred_element_type=wide) * 0.125
    )
    grad_key_all = (
        jnp.einsum("gqt,qgd->td", grad_scores, queries, preferred_element_type=wide) * 0.125
    )
    grad_key_value = jnp.concatenate([grad_key_all, grad_value_all], axis=1).astype(low_type)
    grad_key_value = collect(list(grad_key_value.reshape(-1, row_count, 2 * HD)), "ctx")
    grad_projected = jnp.concatenate(
        [
            rotate_back(grad_queries, cosine[:, None, :], sine[:, None, :]).reshape(row_count, 448),
            rotate_back(grad_key_value[:, :HD], cosine, sine),
            grad_key_value[:, HD:],
            jnp.zeros((row_count, HD), wide),
        ],
        axis=1,
    ).astype(low_type)
    return grad_branch, grad_projected


def backward_in(grad_projected, grad_middle, kept, weights):
    attn_gain, mlp_gain, bias, w_attn = weights
    resid, scale_one = kept[:2]
    grad_normed_in = tensor_sum(contract(grad_projected, w_attn[:, :640], 1, 1))
    grad_attn_gain, grad_resid = norm_backward(grad_normed_in, resid, scale_one, attn_gain)
    return (grad_resid + grad_middle).astype(low_type), grad_attn_gain


def attn_weight_grads(grad_branch, grad_projected, kept):
    normed_in, mixed = kept[2], kept[7]
    grad_bias = jnp.sum(grad_projected.astype(wide), axis=0)
    projection = contract(normed_in, grad_projected, 0, 0)
    output = contract(grad_branch, mixed, 0, 0)
    latter = jnp.pad(projection[:, 512:], ((0, 0), (0, 384))) + output
    return jnp.concatenate([projection[:, :512], latter], axis=1).astype(low_type), grad_bias


def row_blocks(blocks, row_place, axis):
    return [pick(blocks, (row_place + steps) % 4, axis) for steps in (0, 1, 3, 2)]


def send_rows(pieces):
    return [turn_y(piece, steps) for steps, piece in zip((1, 3, 2), pieces)]


def add_all(pieces):
    return sum(piece.astype(wide) for piece in pieces).astype(low_type)


def split_columns(blocks, section_place):
    return pick(blocks, section_place, 1), pick(blocks, 1 - section_place, 1)


def halve(kept, sent):
    return (kept.astype(wide) + turn(sent, "section", 1).astype(wide)).astype(low_type)


def to_column(block):
    hops = []
    for row in range(4):
        hops.append((8 + 2 * row, 8 + 2 * row + 1))
        hops.append((2 * row + 1, 2 * row))
    return lax.ppermute(block, ("section", "fsdp"), hops)


def own_layer(block_zero, block_one, section_place, column_place):
    first = section_place == 0
    hops = []
    for row in range(4):
        hops.append((2 * row, 8 + 2 * row))
        hops.append((8 + 2 * row + 1, 2 * row + 1))
    own = jnp.where(first, block_zero, block_one)
    sent = jnp.where(first, block_one, block_zero)
    received = lax.ppermute(sent, ("section", "fsdp"), hops)
    return jnp.where(section_place == column_place, own, received)


def in_order(pieces, ctx_place):
    own, former, latter, opposite = pieces
    pieces = jnp.stack([own, former, opposite, latter])
    return jnp.stack([pick(pieces, (ctx_place - place) % 4, 0) for place in range(4)])


def pack_lines(small):
    grad_attn_gain, grad_mlp_gain, grad_bias = small
    lines = jnp.concatenate(
        [
            jnp.pad(grad_attn_gain.reshape(8, 112), ((0, 0), (0, 16))),
            jnp.pad(grad_mlp_gain.reshape(8, 112), ((0, 0), (0, 16))),
            jnp.pad(grad_bias[:512].reshape(8, 64), ((0, 0), (0, 64))),
            jnp.pad(grad_bias[512:576].reshape(8, 8), ((0, 0), (0, 632))),
        ],
        axis=1,
    ).astype(low_type)
    return jnp.pad(lines[:, None], ((0, 0), (0, 15), (0, 0))).reshape(4, 2, 16, 1024)


def ctx_blocks(blocks, lines, ctx_place):
    quarters = []
    for steps in (0, 1, 3, 2):
        start = (ctx_place - steps) % 4 * 256
        quarters.append(
            jnp.concatenate(
                [
                    lax.dynamic_slice_in_dim(blocks, start, 256, 2),
                    lax.dynamic_slice_in_dim(lines, start, 256, 2),
                ],
                axis=1,
            )
        )
    return quarters


def send_ctx(pieces):
    return [turn(piece, "ctx", -steps) for steps, piece in zip((1, 3, 2), pieces)]


def per_device(
    layer_input, cotangent, doc_lengths, attn_gain, w_qkv, b_qkv, w_out, mlp_gain, w_gate_up, w_down
):
    section_place = lax.axis_index("section")
    fsdp_place = lax.axis_index("fsdp")
    row_place, column_place = fsdp_place // 2, fsdp_place % 2
    ctx_place = lax.axis_index("ctx")
    places = (section_place, row_place, column_place, ctx_place)
    row_count, width = layer_input.shape[1:]
    units_all = w_down.shape[1]

    line = jnp.concatenate(
        [
            jnp.pad(attn_gain, ((0, 0), (0, 16))),
            jnp.pad(mlp_gain, ((0, 0), (0, 16))),
            jnp.pad(b_qkv[0], ((0, 0), (0, 696))),
        ],
        axis=1,
    )
    attn_block = jnp.concatenate(
        [
            jnp.concatenate([w_qkv[0, :, 0], w_out[0].T], axis=1),
            jnp.pad(line, ((0, 15), (0, 0))),
        ],
        axis=0,
    )
    past = 4 * UNITS - units_all
    mlp_block = jnp.concatenate(
        [
            jnp.pad(w_gate_up[0], ((0, 0), (0, 0), (0, past))),
            jnp.pad(w_down[0].T, ((0, 0), (0, past)))[:, None],
        ],
        axis=1,
    )
    mlp_block = lax.dynamic_slice_in_dim(mlp_block, ctx_place * UNITS, UNITS, 2)
    mlp_block = jnp.pad(mlp_block.reshape(112, 3 * UNITS), ((0, 0), (0, 128)))

    first = section_place == 0
    layer_in = pick(layer_input, section_place, 0)
    grads_last = pick(cotangent, section_place, 0)
    tables = mask_tables(pick(doc_lengths, section_place, 0)[0], ctx_place, row_count, 4)

    rows_all = turn_ctx(layer_in)
    half_attn, late_attn = halves_by_layer(attn_block, section_place)
    half_mlp, late_mlp = halves_by_layer(mlp_block, section_place)
    pair_attn = with_column(half_attn, flip_x(half_attn), column_place)
    pair_attn, half_mlp, layer_in, *rows_all = after(pair_attn, half_mlp, layer_in, *rows_all)
    rows_attn = turn_rows(pair_attn)
    pair_mlp = with_column(half_mlp, flip_x(half_mlp), column_place)
    pair_attn, pair_mlp, grads_last, *rows_attn = after(
        pair_attn, pair_mlp, grads_last, *rows_attn
    )
    rows_mlp = turn_rows(pair_mlp)
    pieces = [pair_attn] + rows_attn
    weights_zero = attn_weights(pieces, swap_all(pieces), places)
    rows_all = stack_rows(layer_in, rows_all)
    grads_all = turn_ctx(grads_last)

    branch, kept_attn_zero = forward_attn(layer_in, rows_all, weights_zero, tables)
    branch, late_attn, late_mlp, *pieces = after(
        branch, late_attn, late_mlp, pair_mlp, *rows_mlp, *grads_all
    )
    pieces, grads_all = pieces[:4], pieces[4:]
    others = swap_all(pieces)
    pair_attn = with_column(late_attn, flip_x(late_attn), column_place)
    pair_mlp = with_column(late_mlp, flip_x(late_mlp), column_place)
    middle, scale_two, normed_mid = forward_mid(branch, kept_attn_zero[0], weights_zero[1])
    normed_mid, pair_attn, pair_mlp, *pieces = after(
        normed_mid, pair_attn, pair_mlp, *pieces, *others
    )
    rows_attn = [turn_y(pair_attn, 1), turn_y(pair_attn, 3)]
    w_mlp_zero = mlp_weights(pieces[:4], pieces[4:], places)
    normed_mid = stack_rows(normed_mid, turn_ctx(normed_mid))
    normed_mid, pair_attn, *rows_attn = after(normed_mid, pair_attn, *rows_attn)
    rows_attn.append(turn_y(pair_attn, 2))
    gate_up, hidden = forward_mlp(normed_mid, w_mlp_zero)
    kept_mlp_zero = (middle, scale_two, normed_mid, gate_up, hidden)
    branch = collect(forward_down(hidden, w_mlp_zero, row_count), "ctx")
    branch, pair_mlp, *pieces = after(branch, pair_mlp, pair_attn, *rows_attn)
    others = swap_all(pieces)
    rows_mlp = [turn_y(pair_mlp, 1), turn_y(pair_mlp, 3)]
    out_zero = (middle + tensor_sum(branch)).astype(low_type)
    out_zero, pair_mlp, *rest = after(out_zero, pair_mlp, *rows_mlp, *pieces, *others)
    rows_mlp = rest[:2] + [turn_y(pair_mlp, 2)]
    weights_one = attn_weights(rest[2:6], rest[6:], places)

    branch, kept_attn_one = forward_attn(out_zero, None, weights_one, tables)
    branch, *pieces = after(branch, pair_mlp, *rows_mlp)
    others = swap_all(pieces)
    middle, scale_two, normed_mid = forward_mid(branch, kept_attn_one[0], weights_one[1])
    normed_mid, *pieces = after(normed_mid, *pieces, *others)
    w_mlp_one = mlp_weights(pieces[:4], pieces[4:], places)
    grads_all = stack_rows(grads_last, grads_all)
    normed_mid = stack_rows(normed_mid, turn_ctx(normed_mid))
    gate_up, hidden = forward_mlp(normed_mid, w_mlp_one)
    kept_mlp_one = (middle, scale_two, normed_mid, gate_up, hidden)

    mlp_shape = (4, 2, 112, 3 * UNITS)
    attn_shape = (4, 2, 112, 1024)
    branch, mlp_one = backward_mlp(grads_all, kept_mlp_one, w_mlp_one)
    branch = collect(list(branch), "ctx")
    down = forward_down(hidden, w_mlp_one, row_count)
    down = [down[steps] for steps in (0, 1, 3, 2)]
    branch, mlp_keep, mlp_sent, *down = after(
        branch, *split_columns(mlp_one.reshape(mlp_shape), section_place), *down
    )
    down_moved = send_ctx(down[1:])
    mlp_pieces = row_blocks(halve(mlp_keep, mlp_sent), row_place, 0)
    middle_one, gain_one = backward_mid(branch, grads_last, kept_mlp_one, weights_one[1])
    middle_one, *pieces = after(middle_one, down[0], *down_moved, *mlp_pieces)
    down, mlp_pieces = sum(piece.astype(wide) for piece in pieces[:4]), pieces[4:]
    mlp_moved = send_rows(mlp_pieces[1:3])
    out_one = (kept_mlp_one[0] + tensor_sum(down)).astype(low_type)
    branch_one, projected_one = backward_attn(middle_one, kept_attn_one, weights_one, tables)
    projected_one, out_one, *pieces = after(
        projected_one, out_one, mlp_pieces[0], mlp_pieces[3], *mlp_moved
    )
    mlp_pieces = [pieces[0], pieces[2], pieces[3], turn_y(pieces[1], 2)]
    grads_one, attn_gain_one = backward_in(projected_one, middle_one, kept_attn_one, weights_one)
    attn_one, bias_one = attn_weight_grads(branch_one, projected_one, kept_attn_one)
    lines_one = pack_lines((attn_gain_one, gain_one, bias_one))
    grads_one, *mlp_pieces = after(grads_one, *mlp_pieces)

    mlp_one = add_all(mlp_pieces)
    mlp_one_moved = to_column(mlp_one)
    attn_sums = halve(*split_columns(attn_one.reshape(attn_shape), section_place))
    line_sums = halve(*split_columns(lines_one, section_place))
    grads_all = stack_rows(grads_one, turn_ctx(grads_one))
    grads_all, mlp_one, mlp_one_moved, attn_sums, line_sums = after(
        grads_all, mlp_one, mlp_one_moved, attn_sums, line_sums
    )
    mlp_one = add_all([mlp_one, mlp_one_moved])
    branch, mlp_zero = backward_mlp(grads_all, kept_mlp_zero, w_mlp_zero)
    branch = collect(list(branch), "ctx")
    branch, mlp_keep, mlp_sent, mlp_one, *attn_pieces = after(
        branch,
        *split_columns(mlp_zero.reshape(mlp_shape), section_place),
        mlp_one,
        *ctx_blocks(attn_sums, line_sums, ctx_place),
    )
    mlp_pieces = row_blocks(halve(mlp_keep, mlp_sent), row_place, 0)
    attn_moved = send_ctx(attn_pieces[1:])
    middle_zero, gain_zero = backward_mid(branch, grads_one, kept_mlp_zero, weights_zero[1])
    middle_zero, *pieces = after(middle_zero, attn_pieces[0], *attn_moved, *mlp_pieces)
    attn_one, mlp_pieces = add_all(pieces[:4]), pieces[4:]
    mlp_moved = send_rows(mlp_pieces[1:3])
    branch_zero, projected_zero = backward_attn(middle_zero, kept_attn_zero, weights_zero, tables)
    projected_zero, *pieces = after(projected_zero, mlp_pieces[0], mlp_pieces[3], *mlp_moved)
    mlp_pieces = [pieces[0], pieces[2], pieces[3], turn_y(pieces[1], 2)]
    attn_zero, bias_zero = attn_weight_grads(branch_zero, projected_zero, kept_attn_zero)
    attn_sums = halve(*split_columns(attn_zero.reshape(attn_shape), section_place))
    grads_zero, attn_gain_zero = backward_in(
        projected_zero, middle_zero, kept_attn_zero, weights_zero
    )
    lines_zero = pack_lines((attn_gain_zero, gain_zero, bias_zero))
    line_sums = halve(*split_columns(lines_zero, section_place))

    attn_pieces = ctx_blocks(attn_sums, line_sums, ctx_place)
    attn_moved = send_ctx(attn_pieces[1:])
    mlp_zero = add_all(mlp_pieces)
    mlp_moved = to_column(mlp_zero)
    attn_zero = add_all([attn_pieces[0]] + attn_moved)
    attn_zero, mlp_zero, mlp_moved = after(attn_zero, mlp_zero, mlp_moved)
    mlp_zero = add_all([mlp_zero, mlp_moved])
    mlp = own_layer(mlp_zero, mlp_one, section_place, column_place)
    attn_pieces = row_blocks(jnp.stack([attn_zero, attn_one]), row_place, 1)
    mlp, *attn_pieces = after(mlp, *attn_pieces)
    mlp_all = [turn(mlp, "ctx", 1), turn(mlp, "ctx", 3)]
    attn_both = add_all(attn_pieces[:1] + send_rows(attn_pieces[1:]))
    attn_both, mlp, *mlp_all = after(attn_both, mlp, *mlp_all)
    mlp_all.append(turn(mlp, "ctx", 2))
    attn_both = add_all([attn_both, to_column(attn_both)])
    attn = own_layer(attn_both[0], attn_both[1], section_place, column_place)
    attn_all = turn_ctx(attn)
    mlp = in_order([mlp] + mlp_all, ctx_place).reshape(4, 112, 3, UNITS)
    attn = in_order([attn] + attn_all, ctx_place)
    outputs = [out_zero, out_one]

    def by_layer(values):
        own = jnp.where(first, values[0], values[1])
        other = turn(jnp.where(first, values[1], values[0]), "section", 1)
        return jnp.where(first, jnp.stack([own, other]), jnp.stack([other, own]))[None]

    hidden_states = by_layer(outputs)
    input_grads = by_layer([grads_zero, grads_one])
    attn = attn.transpose(1, 0, 2).reshape(128, 1024).astype(wide)
    gate_up = mlp[:, :, :2].transpose(1, 2, 0, 3).reshape(112, 2, 4 * UNITS)[:, :, :units_all]
    down = mlp[:, :, 2].transpose(0, 2, 1).reshape(4 * UNITS, 112)[:units_all]
    lines = attn[112:113]
    return (
        hidden_states,
        input_grads,
        lines[:, :112],
        attn[None, :112, None, :576],
        lines[None, :, 256:320],
        lines[None, :, 384:392],
        attn[:112, 576:].T[None],
        lines[:, 128:240],
        gate_up.astype(wide)[None],
        down.astype(wide)[None],
    )


def solution(mesh):
    return jax.shard_map(
        per_device,
        mesh=mesh,
        in_specs=(
            P(None, ("fsdp", "ctx"), None),
            P(None, ("fsdp", "ctx"), None),
            P(None, "fsdp", None),
            P("section", "fsdp"),
            P("section", "fsdp", "tp", None),
            P("section", "tp", "fsdp"),
            P("section", "tp", "fsdp"),
            P("section", "fsdp"),
            P("section", "fsdp", None, "tp"),
            P("section", "tp", "fsdp"),
        ),
        out_specs=(
            P("section", None, ("fsdp", "ctx"), None),
            P("section", None, ("fsdp", "ctx"), None),
            P("section", "fsdp"),
            P("section", "fsdp", "tp", None),
            P("section", "tp", "fsdp"),
            P("section", "tp", "fsdp"),
            P("section", "tp", "fsdp"),
            P("section", "fsdp"),
            P("section", "fsdp", None, "tp"),
            P("section", "tp", "fsdp"),
        ),
        check_vma=False,
    )
```

```python
import jax
import jax.numpy as jnp
from jax import lax
from jax.experimental import pallas as pl
from jax.experimental.pallas import tpu as pltpu
from jax.sharding import PartitionSpec as P

HD = 64
UNITS = 640

epsilon = 1e-06
rope_base = 1000000.0
masked_score = -1000000000.0
low_type = jnp.bfloat16
wide = jnp.float32


def contract(left, right, left_dim, right_dim):
    return lax.dot_general(
        left, right, (((left_dim,), (right_dim,)), ((), ())), preferred_element_type=wide
    )


def turn(value, axis, steps):
    count = lax.axis_size(axis)
    return lax.ppermute(value, axis, [(place, (place + steps) % count) for place in range(count)])


def turn_y(value, steps):
    count = lax.axis_size("fsdp")
    return lax.ppermute(
        value, "fsdp", [(place, (place + 2 * steps) % count) for place in range(count)]
    )


def flip_x(value):
    count = lax.axis_size("fsdp")
    return lax.ppermute(value, "fsdp", [(place, place ^ 1) for place in range(count)])


def collect(blocks, axis):
    count = lax.axis_size(axis)
    order = [1, count - 1] + list(range(2, count - 1))
    total = blocks[0].astype(wide)
    for steps in order:
        total = total + turn(blocks[steps], axis, -steps).astype(wide)
    return total


def pick(array, place, axis):
    return lax.dynamic_index_in_dim(array, place, axis, keepdims=False)


def turn_ctx(block):
    return [turn(block, "ctx", steps) for steps in (1, 3, 2)]


def stack_rows(own, moved):
    former, latter, opposite = moved
    return jnp.concatenate([own, former, opposite, latter], axis=0)


def tensor_sum(partial_value):
    own = lax.optimization_barrier(partial_value.astype(low_type))
    return own.astype(wide) + turn(own, "tp", 1).astype(wide)


def after(value, *others):
    tied = lax.optimization_barrier((value,) + others)
    return tied[0] if not others else tied


def with_column(half, received, column_place):
    pair = jnp.zeros((2,) + half.shape, half.dtype)
    pair = lax.dynamic_update_slice(pair, half[None], (column_place, 0, 0))
    return lax.dynamic_update_slice(pair, received[None], (1 - column_place, 0, 0))


def turn_rows(pair):
    return [turn_y(pair, steps) for steps in (1, 3, 2)]


def swap_all(pieces):
    return [turn(piece, "section", 1) for piece in pieces]


def place_pieces(lines, row_count, places, *refs):
    pieces, outs = refs[:8], refs[8:]
    columns = pieces[0].shape[2]
    for index, piece in enumerate(pieces):
        row = lax.rem(places[0] + 4 - (0, 1, 3, 2)[index % 4], 4)
        half = places[1] if index < 4 else 1 - places[1]
        start = pl.multiple_of(half * columns, 128)
        for column in range(2):
            where = (row * 2 + column, slice(None), pl.ds(start, columns))
            outs[0][where] = piece[column, pl.ds(0, row_count), :]
            if lines:
                outs[1][where] = piece[column, pl.ds(row_count, lines), :]


def put_together(pieces, others, places, lines):
    rows, columns = pieces[0].shape[1:]
    shapes = [jax.ShapeDtypeStruct((8, rows - lines, 2 * columns), low_type)]
    if lines:
        shapes.append(jax.ShapeDtypeStruct((8, lines, 2 * columns), low_type))
    place = jnp.stack([places[1], places[0]]).astype(jnp.int32)
    size = 8 * rows * 2 * columns * 2
    return pl.pallas_call(
        lambda *refs: place_pieces(lines, rows - lines, *refs),
        out_shape=shapes,
        in_specs=[pl.BlockSpec(memory_space=pltpu.SMEM)] + [pl.BlockSpec(memory_space=pltpu.VMEM)] * 8,
        out_specs=[pl.BlockSpec(memory_space=pltpu.VMEM)] * len(shapes),
        compiler_params=pltpu.CompilerParams(vmem_limit_bytes=20 << 20),
        cost_estimate=pl.CostEstimate(flops=0, bytes_accessed=2 * size, transcendentals=0),
    )(place, *pieces, *others)


def attn_weights(pieces, others, places):
    width = 8 * 112
    w_attn, lines = put_together(pieces, others, places, 16)
    lines = lines[:, 0].astype(wide)
    return (
        lines[:, :112].reshape(width),
        lines[:, 128:240].reshape(width),
        jnp.pad(lines[:, 256:328].reshape(576), (0, 64)),
        w_attn.reshape(width, 1024),
    )


def mlp_weights(pieces, others, places):
    return put_together(pieces, others, places, 0)[0].reshape(8 * 112, 2048)


def halves_by_layer(block, section_place):
    columns = block.shape[1] // 2
    kept = lax.dynamic_slice_in_dim(block, section_place * columns, columns, 1)
    sent = lax.dynamic_slice_in_dim(block, (1 - section_place) * columns, columns, 1)
    received = turn(sent, "section", 1)
    first = section_place == 0
    return jnp.where(first, kept, received), jnp.where(first, received, kept)


def rotary_tables(position):
    inverse = rope_base ** (-jnp.arange(0, HD, 2, dtype=wide) / HD)
    angles = position.astype(wide)[..., None] * inverse
    angles = jnp.concatenate([angles, angles], axis=-1)
    return (jnp.cos(angles), jnp.sin(angles))


def rotate(values, cosine, sine):
    half_width = values.shape[-1] // 2
    turned = jnp.concatenate([-values[..., half_width:], values[..., :half_width]], axis=-1)
    return values * cosine + turned * sine


def rotate_back(grads, cosine, sine):
    half_width = grads.shape[-1] // 2
    scaled = grads * sine
    turned = jnp.concatenate([scaled[..., half_width:], -scaled[..., :half_width]], axis=-1)
    return grads * cosine + turned


def norm_backward(grad_normed, resid, scale, gain):
    grad_gain = jnp.sum(grad_normed * resid * scale, axis=0)
    inner = grad_normed * gain
    grad_resid = scale * inner - resid * (scale * scale * scale) * jnp.mean(
        inner * resid, axis=-1, keepdims=True
    )
    return (grad_gain, grad_resid)


def mask_tables(lengths, ctx_place, row_count, ctx_count):
    doc_ends = jnp.cumsum(lengths, axis=-1)
    blocks = (ctx_place - jnp.arange(ctx_count, dtype=jnp.int32)) % ctx_count
    places = (blocks[:, None] * row_count + jnp.arange(row_count, dtype=jnp.int32)).reshape(-1)
    passed = places[:, None] >= doc_ends[None, :]
    segment = jnp.sum(passed.astype(jnp.int32), axis=-1)
    doc_start = jnp.sum(jnp.where(passed, lengths[None, :], 0), axis=-1)
    position = places - doc_start
    cosine, sine = rotary_tables(position[:row_count])
    allowed = (segment[:row_count, None] == segment[None, :]) & (
        places[:row_count, None] >= places[None, :]
    )
    return (allowed, cosine, sine)


def normed(resid, gain):
    scale = lax.rsqrt(jnp.mean(resid * resid, axis=-1, keepdims=True) + epsilon)
    return scale, (resid * scale * gain).astype(low_type)


def forward_attn(layer_in, weights, tables, tie):
    attn_gain, mlp_gain, bias, w_attn = weights
    allowed, cosine, sine = tables
    row_count, width = layer_in.shape
    resid = layer_in.astype(wide)
    scale_one, normed_in = normed(resid, attn_gain)
    projected = jnp.dot(normed_in, w_attn[:, :640], preferred_element_type=wide) + bias
    queries = rotate(
        projected[:, :448].reshape(row_count, 7, HD), cosine[:, None, :], sine[:, None, :]
    ).astype(low_type)
    key_own = rotate(projected[:, 448:512], cosine, sine)
    key_value = jnp.concatenate([key_own, projected[:, 512:576]], axis=1).astype(low_type)
    key_value = tie(stack_rows(key_value, turn_ctx(key_value)))
    key_all, value_all = key_value[:, :HD], key_value[:, HD:]
    scores = jnp.einsum("qgd,td->gqt", queries, key_all, preferred_element_type=wide) * 0.125
    scores = jnp.where(allowed[None], scores, masked_score)
    largest = jnp.max(scores, axis=-1, keepdims=True)
    raised = jnp.exp(scores - largest)
    totals = jnp.sum(raised, axis=-1, keepdims=True)
    log_total = largest + jnp.log(totals)
    probs = (raised / totals).astype(low_type)
    mixed = jnp.einsum("gqt,td->qgd", probs, value_all, preferred_element_type=wide)
    mixed = jnp.pad(mixed.reshape(row_count, 448).astype(low_type), ((0, 0), (64, 0)))
    kept = (resid, scale_one, normed_in, queries, key_all, value_all, log_total, mixed)
    return contract(mixed, w_attn[:, 512:], 1, 1), kept


def forward_mid(branch, resid, mlp_gain):
    middle = resid + tensor_sum(branch)
    return middle, *normed(middle, mlp_gain)


def forward_mlp(normed_mid, w_mlp):
    gate_up = jnp.dot(normed_mid, w_mlp[:, : 2 * UNITS], preferred_element_type=wide)
    hidden = (jax.nn.silu(gate_up[:, :UNITS]) * gate_up[:, UNITS:]).astype(low_type)
    return gate_up, hidden


def forward_down(hidden, w_mlp, row_count):
    branch = contract(hidden, w_mlp[:, 2 * UNITS : 3 * UNITS], 1, 1).astype(low_type)
    return list(branch.reshape(-1, row_count, branch.shape[1]))


def backward_mlp(grad_all, kept, w_mlp):
    middle, scale_two, normed_mid, gate_up, hidden = kept
    row_count, width = middle.shape
    grad_hidden = jnp.dot(grad_all, w_mlp[:, 2 * UNITS : 3 * UNITS], preferred_element_type=wide)
    gate = gate_up[:, :UNITS]
    upward = gate_up[:, UNITS:]
    sigmoid = jax.nn.sigmoid(gate)
    grad_gate = grad_hidden * upward * sigmoid * (1.0 + gate * (1.0 - sigmoid))
    grad_upward = grad_hidden * gate * sigmoid
    grad_gate_up = jnp.concatenate([grad_gate, grad_upward], axis=1).astype(low_type)
    branch = contract(grad_gate_up, w_mlp[:, : 2 * UNITS], 1, 1).astype(low_type)
    branch = branch.reshape(-1, row_count, width)
    grad_mlp = jnp.concatenate(
        [
            contract(normed_mid, grad_gate_up, 0, 0).astype(low_type),
            contract(grad_all, hidden, 0, 0).astype(low_type),
        ],
        axis=1,
    )
    return branch, grad_mlp


def backward_mid(branch, grad_out, kept, mlp_gain):
    middle, scale_two = kept[:2]
    grad_normed_mid = tensor_sum(branch)
    grad_mlp_gain, grad_middle = norm_backward(grad_normed_mid, middle, scale_two, mlp_gain)
    return grad_middle + grad_out.astype(wide), grad_mlp_gain


def backward_attn(grad_middle, kept, weights, tables):
    attn_gain, mlp_gain, bias, w_attn = weights
    allowed, cosine, sine = tables
    resid, scale_one, normed_in, queries, key_all, value_all, log_total, mixed = kept
    row_count, width = resid.shape
    grad_branch = grad_middle.astype(low_type)
    grad_mixed = jnp.dot(grad_branch, w_attn[:, 512:], preferred_element_type=wide)
    grad_mixed = grad_mixed[:, 64:].astype(low_type).reshape(queries.shape)
    scores = jnp.einsum("qgd,td->gqt", queries, key_all, preferred_element_type=wide) * 0.125
    probs = jnp.where(allowed[None], jnp.exp(scores - log_total), 0.0)
    grad_probs = jnp.einsum("qgd,td->gqt", grad_mixed, value_all, preferred_element_type=wide)
    grad_value_all = jnp.einsum(
        "gqt,qgd->td", probs.astype(low_type), grad_mixed, preferred_element_type=wide
    )
    row_delta = jnp.sum(grad_probs * probs, axis=-1, keepdims=True)
    grad_scores = (probs * (grad_probs - row_delta)).astype(low_type)
    grad_queries = (
        jnp.einsum("gqt,td->qgd", grad_scores, key_all, preferred_element_type=wide) * 0.125
    )
    grad_key_all = (
        jnp.einsum("gqt,qgd->td", grad_scores, queries, preferred_element_type=wide) * 0.125
    )
    grad_key_value = jnp.concatenate([grad_key_all, grad_value_all], axis=1).astype(low_type)
    grad_key_value = collect(list(grad_key_value.reshape(-1, row_count, 2 * HD)), "ctx")
    grad_projected = jnp.concatenate(
        [
            rotate_back(grad_queries, cosine[:, None, :], sine[:, None, :]).reshape(row_count, 448),
            rotate_back(grad_key_value[:, :HD], cosine, sine),
            grad_key_value[:, HD:],
            jnp.zeros((row_count, HD), wide),
        ],
        axis=1,
    ).astype(low_type)
    return grad_branch, grad_projected


def backward_in(grad_projected, grad_middle, kept, weights):
    attn_gain, mlp_gain, bias, w_attn = weights
    resid, scale_one = kept[:2]
    grad_normed_in = tensor_sum(contract(grad_projected, w_attn[:, :640], 1, 1))
    grad_attn_gain, grad_resid = norm_backward(grad_normed_in, resid, scale_one, attn_gain)
    return (grad_resid + grad_middle).astype(low_type), grad_attn_gain


def attn_weight_grads(grad_branch, grad_projected, kept):
    normed_in, mixed = kept[2], kept[7]
    grad_bias = jnp.sum(grad_projected.astype(wide), axis=0)
    projection = contract(normed_in, grad_projected, 0, 0)
    output = contract(grad_branch, mixed, 0, 0)
    latter = jnp.pad(projection[:, 512:], ((0, 0), (0, 384))) + output
    return jnp.concatenate([projection[:, :512], latter], axis=1).astype(low_type), grad_bias


def row_blocks(blocks, row_place, axis):
    return [pick(blocks, (row_place + steps) % 4, axis) for steps in (0, 1, 3, 2)]


def send_rows(pieces):
    return [turn_y(piece, steps) for steps, piece in zip((1, 3, 2), pieces)]


def add_all(pieces):
    return sum(piece.astype(wide) for piece in pieces).astype(low_type)


def split_columns(blocks, section_place):
    return pick(blocks, section_place, 1), pick(blocks, 1 - section_place, 1)


def halve(kept, sent):
    return (kept.astype(wide) + turn(sent, "section", 1).astype(wide)).astype(low_type)


def to_column(block):
    hops = []
    for row in range(4):
        hops.append((8 + 2 * row, 8 + 2 * row + 1))
        hops.append((2 * row + 1, 2 * row))
    return lax.ppermute(block, ("section", "fsdp"), hops)


def own_layer(block_zero, block_one, section_place, column_place):
    first = section_place == 0
    hops = []
    for row in range(4):
        hops.append((2 * row, 8 + 2 * row))
        hops.append((8 + 2 * row + 1, 2 * row + 1))
    own = jnp.where(first, block_zero, block_one)
    sent = jnp.where(first, block_one, block_zero)
    received = lax.ppermute(sent, ("section", "fsdp"), hops)
    return jnp.where(section_place == column_place, own, received)


def in_order(pieces, ctx_place):
    own, former, latter, opposite = pieces
    pieces = jnp.stack([own, former, opposite, latter])
    return jnp.stack([pick(pieces, (ctx_place - place) % 4, 0) for place in range(4)])


def pack_lines(small):
    grad_attn_gain, grad_mlp_gain, grad_bias = small
    lines = jnp.concatenate(
        [
            jnp.pad(grad_attn_gain.reshape(8, 112), ((0, 0), (0, 16))),
            jnp.pad(grad_mlp_gain.reshape(8, 112), ((0, 0), (0, 16))),
            jnp.pad(grad_bias[:512].reshape(8, 64), ((0, 0), (0, 64))),
            jnp.pad(grad_bias[512:576].reshape(8, 8), ((0, 0), (0, 632))),
        ],
        axis=1,
    ).astype(low_type)
    return jnp.pad(lines[:, None], ((0, 0), (0, 15), (0, 0))).reshape(4, 2, 16, 1024)


def ctx_blocks(blocks, lines, ctx_place):
    quarters = []
    for steps in (0, 1, 3, 2):
        start = (ctx_place - steps) % 4 * 256
        quarters.append(
            jnp.concatenate(
                [
                    lax.dynamic_slice_in_dim(blocks, start, 256, 2),
                    lax.dynamic_slice_in_dim(lines, start, 256, 2),
                ],
                axis=1,
            )
        )
    return quarters


def send_ctx(pieces):
    return [turn(piece, "ctx", -steps) for steps, piece in zip((1, 3, 2), pieces)]


def per_device(
    layer_input, cotangent, doc_lengths, attn_gain, w_qkv, b_qkv, w_out, mlp_gain, w_gate_up, w_down
):
    section_place = lax.axis_index("section")
    fsdp_place = lax.axis_index("fsdp")
    row_place, column_place = fsdp_place // 2, fsdp_place % 2
    ctx_place = lax.axis_index("ctx")
    places = (section_place, row_place, column_place, ctx_place)
    row_count, width = layer_input.shape[1:]
    units_all = w_down.shape[1]

    line = jnp.concatenate(
        [
            jnp.pad(attn_gain, ((0, 0), (0, 16))),
            jnp.pad(mlp_gain, ((0, 0), (0, 16))),
            jnp.pad(b_qkv[0], ((0, 0), (0, 696))),
        ],
        axis=1,
    )
    attn_block = jnp.concatenate(
        [
            jnp.concatenate([w_qkv[0, :, 0], w_out[0].T], axis=1),
            jnp.pad(line, ((0, 15), (0, 0))),
        ],
        axis=0,
    )
    past = 4 * UNITS - units_all
    mlp_block = jnp.concatenate(
        [
            jnp.pad(w_gate_up[0], ((0, 0), (0, 0), (0, past))),
            jnp.pad(w_down[0].T, ((0, 0), (0, past)))[:, None],
        ],
        axis=1,
    )
    mlp_block = lax.dynamic_slice_in_dim(mlp_block, ctx_place * UNITS, UNITS, 2)
    mlp_block = jnp.pad(mlp_block.reshape(112, 3 * UNITS), ((0, 0), (0, 128)))

    first = section_place == 0
    layer_in = pick(layer_input, section_place, 0)
    grads_last = pick(cotangent, section_place, 0)
    tables = mask_tables(pick(doc_lengths, section_place, 0)[0], ctx_place, row_count, 4)

    half_attn, late_attn = halves_by_layer(attn_block, section_place)
    half_mlp, late_mlp = halves_by_layer(mlp_block, section_place)
    pair_attn = with_column(half_attn, flip_x(half_attn), column_place)
    pair_attn, half_mlp = after(pair_attn, half_mlp)
    rows_attn = turn_rows(pair_attn)
    pair_mlp = with_column(half_mlp, flip_x(half_mlp), column_place)
    pair_attn, pair_mlp, *rows_attn = after(pair_attn, pair_mlp, *rows_attn)
    moved = [pair_mlp, turn_y(pair_mlp, 1), turn_y(pair_mlp, 3)]
    pieces = [pair_attn] + rows_attn
    weights_zero = attn_weights(pieces, swap_all(pieces), places)

    def tie_last_row(key_value):
        key_value, *moved[:] = after(key_value, *moved)
        moved.append(turn_y(moved[0], 2))
        return key_value

    branch, kept_attn_zero = forward_attn(layer_in, weights_zero, tables, tie_last_row)
    branch, late_attn, late_mlp, grads_last, *pieces = after(
        branch, late_attn, late_mlp, grads_last, *moved
    )
    others = swap_all(pieces)
    grads_all = turn_ctx(grads_last)
    middle, scale_two, normed_mid = forward_mid(branch, kept_attn_zero[0], weights_zero[1])
    normed_mid, late_attn, late_mlp, *pieces = after(
        normed_mid, late_attn, late_mlp, *pieces, *others, *grads_all
    )
    pieces, grads_all = pieces[:8], pieces[8:]
    pair_attn = with_column(late_attn, flip_x(late_attn), column_place)
    pair_mlp = with_column(late_mlp, flip_x(late_mlp), column_place)
    w_mlp_zero = mlp_weights(pieces[:4], pieces[4:], places)
    normed_mid = stack_rows(normed_mid, turn_ctx(normed_mid))
    normed_mid, pair_attn, pair_mlp = after(normed_mid, pair_attn, pair_mlp)
    rows_attn = [turn_y(pair_attn, 1), turn_y(pair_attn, 3)]
    gate_up, hidden = forward_mlp(normed_mid, w_mlp_zero)
    kept_mlp_zero = (middle, scale_two, normed_mid, gate_up, hidden)
    branch = collect(forward_down(hidden, w_mlp_zero, row_count), "ctx")
    branch, pair_mlp, *pieces = after(branch, pair_mlp, pair_attn, *rows_attn)
    others = swap_all(pieces)
    last_row = turn_y(pieces[0], 2)
    out_zero = (middle + tensor_sum(branch)).astype(low_type)
    out_zero, pair_mlp, last_row, *rest = after(out_zero, pair_mlp, last_row, *pieces, *others)
    moved[:] = [pair_mlp, turn_y(pair_mlp, 1), turn_y(pair_mlp, 3)]
    last_other = turn(last_row, "section", 1)
    weights_one = attn_weights(rest[:3] + [last_row], rest[3:] + [last_other], places)

    branch, kept_attn_one = forward_attn(out_zero, weights_one, tables, tie_last_row)
    last_row = moved.pop()
    branch, *pieces = after(branch, *moved)
    others = swap_all(pieces)
    middle, scale_two, normed_mid = forward_mid(branch, kept_attn_one[0], weights_one[1])
    normed_mid, last_row, *pieces = after(normed_mid, last_row, *pieces, *others)
    last_other = turn(last_row, "section", 1)
    w_mlp_one = mlp_weights(pieces[:3] + [last_row], pieces[3:] + [last_other], places)
    grads_all = stack_rows(grads_last, grads_all)
    normed_mid = stack_rows(normed_mid, turn_ctx(normed_mid))
    gate_up, hidden = forward_mlp(normed_mid, w_mlp_one)
    kept_mlp_one = (middle, scale_two, normed_mid, gate_up, hidden)

    mlp_shape = (4, 2, 112, 3 * UNITS)
    attn_shape = (4, 2, 112, 1024)
    branch, mlp_one = backward_mlp(grads_all, kept_mlp_one, w_mlp_one)
    branch = collect(list(branch), "ctx")
    down = forward_down(hidden, w_mlp_one, row_count)
    down = [down[steps] for steps in (0, 1, 3, 2)]
    branch, mlp_keep, mlp_sent, *down = after(
        branch, *split_columns(mlp_one.reshape(mlp_shape), section_place), *down
    )
    down_moved = send_ctx(down[1:])
    mlp_pieces = row_blocks(halve(mlp_keep, mlp_sent), row_place, 0)
    middle_one, gain_one = backward_mid(branch, grads_last, kept_mlp_one, weights_one[1])
    middle_one, *pieces = after(middle_one, down[0], *down_moved, *mlp_pieces)
    down, mlp_pieces = sum(piece.astype(wide) for piece in pieces[:4]), pieces[4:]
    mlp_moved = send_rows(mlp_pieces[1:3])
    branch_one, projected_one = backward_attn(middle_one, kept_attn_one, weights_one, tables)
    grads_one, attn_gain_one = backward_in(projected_one, middle_one, kept_attn_one, weights_one)
    attn_one, bias_one = attn_weight_grads(branch_one, projected_one, kept_attn_one)
    lines_one = pack_lines((attn_gain_one, gain_one, bias_one))
    grads_one, *mlp_pieces = after(grads_one, mlp_pieces[0], mlp_pieces[3], *mlp_moved)

    mlp_pieces[1] = turn_y(mlp_pieces[1], 2)
    attn_sums = halve(*split_columns(attn_one.reshape(attn_shape), section_place))
    line_sums = halve(*split_columns(lines_one, section_place))
    grads_all = stack_rows(grads_one, turn_ctx(grads_one))
    grads_all, attn_sums, line_sums, down, *mlp_pieces = after(
        grads_all, attn_sums, line_sums, down, *mlp_pieces
    )
    mlp_one = add_all(mlp_pieces)
    mlp_one = add_all([mlp_one, to_column(mlp_one)])
    out_one = (kept_mlp_one[0] + tensor_sum(down)).astype(low_type)
    branch, mlp_zero = backward_mlp(grads_all, kept_mlp_zero, w_mlp_zero)
    branch = collect(list(branch), "ctx")
    branch, mlp_keep, mlp_sent, mlp_one, out_one, *attn_pieces = after(
        branch,
        *split_columns(mlp_zero.reshape(mlp_shape), section_place),
        mlp_one,
        out_one,
        *ctx_blocks(attn_sums, line_sums, ctx_place),
    )
    mlp_pieces = row_blocks(halve(mlp_keep, mlp_sent), row_place, 0)
    attn_moved = send_ctx(attn_pieces[1:])
    middle_zero, gain_zero = backward_mid(branch, grads_one, kept_mlp_zero, weights_zero[1])
    middle_zero, *pieces = after(middle_zero, attn_pieces[0], *attn_moved, *mlp_pieces)
    attn_one, mlp_pieces = add_all(pieces[:4]), pieces[4:]
    mlp_moved = send_rows(mlp_pieces[1:3])
    branch_zero, projected_zero = backward_attn(middle_zero, kept_attn_zero, weights_zero, tables)
    projected_zero, *pieces = after(projected_zero, mlp_pieces[0], mlp_pieces[3], *mlp_moved)
    mlp_pieces = [pieces[0], pieces[2], pieces[3], turn_y(pieces[1], 2)]
    attn_zero, bias_zero = attn_weight_grads(branch_zero, projected_zero, kept_attn_zero)
    attn_sums = halve(*split_columns(attn_zero.reshape(attn_shape), section_place))
    grads_zero, attn_gain_zero = backward_in(
        projected_zero, middle_zero, kept_attn_zero, weights_zero
    )
    lines_zero = pack_lines((attn_gain_zero, gain_zero, bias_zero))
    line_sums = halve(*split_columns(lines_zero, section_place))

    attn_pieces = ctx_blocks(attn_sums, line_sums, ctx_place)
    attn_moved = send_ctx(attn_pieces[1:])
    mlp_zero = add_all(mlp_pieces)
    mlp_moved = to_column(mlp_zero)
    attn_zero = add_all([attn_pieces[0]] + attn_moved)
    attn_zero, mlp_zero, mlp_moved = after(attn_zero, mlp_zero, mlp_moved)
    mlp_zero = add_all([mlp_zero, mlp_moved])
    mlp = own_layer(mlp_zero, mlp_one, section_place, column_place)
    attn_pieces = row_blocks(jnp.stack([attn_zero, attn_one]), row_place, 1)
    mlp, *attn_pieces = after(mlp, *attn_pieces)
    mlp_all = [turn(mlp, "ctx", 1), turn(mlp, "ctx", 3)]
    attn_both = add_all(attn_pieces[:1] + send_rows(attn_pieces[1:]))
    attn_both, mlp, *mlp_all = after(attn_both, mlp, *mlp_all)
    mlp_all.append(turn(mlp, "ctx", 2))
    attn_both = add_all([attn_both, to_column(attn_both)])
    attn = own_layer(attn_both[0], attn_both[1], section_place, column_place)
    attn, mlp, *mlp_all = after(attn, mlp, *mlp_all)
    attn_all = turn_ctx(attn)
    mlp = in_order([mlp] + mlp_all, ctx_place).reshape(4, 112, 3, UNITS)
    gate_up = mlp[:, :, :2].transpose(1, 2, 0, 3).reshape(112, 2, 4 * UNITS)[:, :, :units_all]
    down = mlp[:, :, 2].transpose(0, 2, 1).reshape(4 * UNITS, 112)[:units_all]
    gate_up, down, *attn_all = after(gate_up.astype(wide), down.astype(wide), *attn_all)
    attn = in_order([attn] + attn_all, ctx_place)
    outputs = [out_zero, out_one]

    def by_layer(values):
        own = jnp.where(first, values[0], values[1])
        other = turn(jnp.where(first, values[1], values[0]), "section", 1)
        return jnp.where(first, jnp.stack([own, other]), jnp.stack([other, own]))[None]

    hidden_states = by_layer(outputs)
    input_grads = by_layer([grads_zero, grads_one])
    attn = attn.transpose(1, 0, 2).reshape(128, 1024).astype(wide)
    lines = attn[112:113]
    return (
        hidden_states,
        input_grads,
        lines[:, :112],
        attn[None, :112, None, :576],
        lines[None, :, 256:320],
        lines[None, :, 384:392],
        attn[:112, 576:].T[None],
        lines[:, 128:240],
        gate_up[None],
        down[None],
    )


def solution(mesh):
    return jax.shard_map(
        per_device,
        mesh=mesh,
        in_specs=(
            P(None, ("fsdp", "ctx"), None),
            P(None, ("fsdp", "ctx"), None),
            P(None, "fsdp", None),
            P("section", "fsdp"),
            P("section", "fsdp", "tp", None),
            P("section", "tp", "fsdp"),
            P("section", "tp", "fsdp"),
            P("section", "fsdp"),
            P("section", "fsdp", None, "tp"),
            P("section", "tp", "fsdp"),
        ),
        out_specs=(
            P("section", None, ("fsdp", "ctx"), None),
            P("section", None, ("fsdp", "ctx"), None),
            P("section", "fsdp"),
            P("section", "fsdp", "tp", None),
            P("section", "tp", "fsdp"),
            P("section", "tp", "fsdp"),
            P("section", "tp", "fsdp"),
            P("section", "fsdp"),
            P("section", "fsdp", None, "tp"),
            P("section", "tp", "fsdp"),
        ),
        check_vma=False,
    )
```

```python
import jax
import jax.numpy as jnp
from jax import lax
from jax.experimental import pallas as pl
from jax.experimental.pallas import tpu as pltpu
from jax.sharding import PartitionSpec as P

HD = 64
UNITS = 640

epsilon = 1e-06
rope_base = 1000000.0
masked_score = -1000000000.0
low_type = jnp.bfloat16
wide = jnp.float32


def contract(left, right, left_dim, right_dim):
    return lax.dot_general(
        left, right, (((left_dim,), (right_dim,)), ((), ())), preferred_element_type=wide
    )


def turn(value, axis, steps):
    count = lax.axis_size(axis)
    return lax.ppermute(value, axis, [(place, (place + steps) % count) for place in range(count)])


def turn_y(value, steps):
    count = lax.axis_size("fsdp")
    return lax.ppermute(
        value, "fsdp", [(place, (place + 2 * steps) % count) for place in range(count)]
    )


def flip_x(value):
    count = lax.axis_size("fsdp")
    return lax.ppermute(value, "fsdp", [(place, place ^ 1) for place in range(count)])


def collect(blocks, axis):
    count = lax.axis_size(axis)
    order = [1, count - 1] + list(range(2, count - 1))
    total = blocks[0].astype(wide)
    for steps in order:
        total = total + turn(blocks[steps], axis, -steps).astype(wide)
    return total


def pick(array, place, axis):
    return lax.dynamic_index_in_dim(array, place, axis, keepdims=False)


def turn_ctx(block):
    return [turn(block, "ctx", steps) for steps in (1, 3, 2)]


def stack_rows(own, moved):
    former, latter, opposite = moved
    return jnp.concatenate([own, former, opposite, latter], axis=0)


def tensor_sum(partial_value):
    own = lax.optimization_barrier(partial_value.astype(low_type))
    return own.astype(wide) + turn(own, "tp", 1).astype(wide)


def after(value, *others):
    tied = lax.optimization_barrier((value,) + others)
    return tied[0] if not others else tied


def with_column(half, received, column_place):
    pair = jnp.zeros((2,) + half.shape, half.dtype)
    pair = lax.dynamic_update_slice(pair, half[None], (column_place, 0, 0))
    return lax.dynamic_update_slice(pair, received[None], (1 - column_place, 0, 0))


def turn_rows(pair):
    return [turn_y(pair, steps) for steps in (1, 3, 2)]


def swap_all(pieces):
    return [turn(piece, "section", 1) for piece in pieces]


def place_pieces(lines, row_count, places, *refs):
    pieces, outs = refs[:8], refs[8:]
    columns = pieces[0].shape[2]
    for index, piece in enumerate(pieces):
        row = lax.rem(places[0] + 4 - (0, 1, 3, 2)[index % 4], 4)
        half = places[1] if index < 4 else 1 - places[1]
        start = pl.multiple_of(half * columns, 128)
        for column in range(2):
            where = (row * 2 + column, slice(None), pl.ds(start, columns))
            outs[0][where] = piece[column, pl.ds(0, row_count), :]
            if lines:
                outs[1][where] = piece[column, pl.ds(row_count, lines), :]


def put_together(pieces, others, places, lines):
    rows, columns = pieces[0].shape[1:]
    shapes = [jax.ShapeDtypeStruct((8, rows - lines, 2 * columns), low_type)]
    if lines:
        shapes.append(jax.ShapeDtypeStruct((8, lines, 2 * columns), low_type))
    place = jnp.stack([places[1], places[0]]).astype(jnp.int32)
    size = 8 * rows * 2 * columns * 2
    return pl.pallas_call(
        lambda *refs: place_pieces(lines, rows - lines, *refs),
        out_shape=shapes,
        in_specs=[pl.BlockSpec(memory_space=pltpu.SMEM)] + [pl.BlockSpec(memory_space=pltpu.VMEM)] * 8,
        out_specs=[pl.BlockSpec(memory_space=pltpu.VMEM)] * len(shapes),
        compiler_params=pltpu.CompilerParams(vmem_limit_bytes=20 << 20),
        cost_estimate=pl.CostEstimate(flops=0, bytes_accessed=2 * size, transcendentals=0),
    )(place, *pieces, *others)


def attn_weights(pieces, others, places):
    width = 8 * 112
    w_attn, lines = put_together(pieces, others, places, 16)
    lines = lines[:, 0].astype(wide)
    return (
        lines[:, :112].reshape(width),
        lines[:, 128:240].reshape(width),
        jnp.pad(lines[:, 256:328].reshape(576), (0, 64)),
        w_attn.reshape(width, 1024),
    )


def mlp_weights(pieces, others, places):
    return put_together(pieces, others, places, 0)[0].reshape(8 * 112, 2048)


def halves_by_layer(block, section_place):
    columns = block.shape[1] // 2
    kept = lax.dynamic_slice_in_dim(block, section_place * columns, columns, 1)
    sent = lax.dynamic_slice_in_dim(block, (1 - section_place) * columns, columns, 1)
    received = turn(sent, "section", 1)
    first = section_place == 0
    return jnp.where(first, kept, received), jnp.where(first, received, kept)


def rotary_tables(position):
    inverse = rope_base ** (-jnp.arange(0, HD, 2, dtype=wide) / HD)
    angles = position.astype(wide)[..., None] * inverse
    angles = jnp.concatenate([angles, angles], axis=-1)
    return (jnp.cos(angles), jnp.sin(angles))


def rotate(values, cosine, sine):
    half_width = values.shape[-1] // 2
    turned = jnp.concatenate([-values[..., half_width:], values[..., :half_width]], axis=-1)
    return values * cosine + turned * sine


def rotate_back(grads, cosine, sine):
    half_width = grads.shape[-1] // 2
    scaled = grads * sine
    turned = jnp.concatenate([scaled[..., half_width:], -scaled[..., :half_width]], axis=-1)
    return grads * cosine + turned


def norm_backward(grad_normed, resid, scale, gain):
    grad_gain = jnp.sum(grad_normed * resid * scale, axis=0)
    inner = grad_normed * gain
    grad_resid = scale * inner - resid * (scale * scale * scale) * jnp.mean(
        inner * resid, axis=-1, keepdims=True
    )
    return (grad_gain, grad_resid)


def mask_tables(lengths, ctx_place, row_count, ctx_count):
    doc_ends = jnp.cumsum(lengths, axis=-1)
    blocks = (ctx_place - jnp.arange(ctx_count, dtype=jnp.int32)) % ctx_count
    places = (blocks[:, None] * row_count + jnp.arange(row_count, dtype=jnp.int32)).reshape(-1)
    passed = places[:, None] >= doc_ends[None, :]
    segment = jnp.sum(passed.astype(jnp.int32), axis=-1)
    doc_start = jnp.sum(jnp.where(passed, lengths[None, :], 0), axis=-1)
    position = places - doc_start
    cosine, sine = rotary_tables(position[:row_count])
    allowed = (segment[:row_count, None] == segment[None, :]) & (
        places[:row_count, None] >= places[None, :]
    )
    return (allowed, cosine, sine)


def normed(resid, gain):
    scale = lax.rsqrt(jnp.mean(resid * resid, axis=-1, keepdims=True) + epsilon)
    return scale, (resid * scale * gain).astype(low_type)


def forward_attn(layer_in, weights, tables, tie):
    attn_gain, mlp_gain, bias, w_attn = weights
    allowed, cosine, sine = tables
    row_count, width = layer_in.shape
    resid = layer_in.astype(wide)
    scale_one, normed_in = normed(resid, attn_gain)
    projected = jnp.dot(normed_in, w_attn[:, :640], preferred_element_type=wide) + bias
    queries = rotate(
        projected[:, :448].reshape(row_count, 7, HD), cosine[:, None, :], sine[:, None, :]
    ).astype(low_type)
    key_own = rotate(projected[:, 448:512], cosine, sine)
    key_value = jnp.concatenate([key_own, projected[:, 512:576]], axis=1).astype(low_type)
    key_value = tie(stack_rows(key_value, turn_ctx(key_value)))
    key_all, value_all = key_value[:, :HD], key_value[:, HD:]
    scores = jnp.einsum("qgd,td->gqt", queries, key_all, preferred_element_type=wide) * 0.125
    scores = jnp.where(allowed[None], scores, masked_score)
    largest = jnp.max(scores, axis=-1, keepdims=True)
    raised = jnp.exp(scores - largest)
    totals = jnp.sum(raised, axis=-1, keepdims=True)
    log_total = largest + jnp.log(totals)
    probs = (raised / totals).astype(low_type)
    mixed = jnp.einsum("gqt,td->qgd", probs, value_all, preferred_element_type=wide)
    mixed = jnp.pad(mixed.reshape(row_count, 448).astype(low_type), ((0, 0), (64, 0)))
    kept = (resid, scale_one, normed_in, queries, key_all, value_all, log_total, mixed)
    return contract(mixed, w_attn[:, 512:], 1, 1), kept


def forward_mid(branch, resid, mlp_gain):
    middle = resid + tensor_sum(branch)
    return middle, *normed(middle, mlp_gain)


def forward_mlp(normed_mid, w_mlp):
    gate_up = jnp.dot(normed_mid, w_mlp[:, : 2 * UNITS], preferred_element_type=wide)
    hidden = (jax.nn.silu(gate_up[:, :UNITS]) * gate_up[:, UNITS:]).astype(low_type)
    return gate_up, hidden


def forward_down(hidden, w_mlp, row_count):
    branch = contract(hidden, w_mlp[:, 2 * UNITS : 3 * UNITS], 1, 1).astype(low_type)
    return list(branch.reshape(-1, row_count, branch.shape[1]))


def backward_mlp(grad_all, kept, w_mlp):
    middle, scale_two, normed_mid, gate_up, hidden = kept
    row_count, width = middle.shape
    grad_hidden = jnp.dot(grad_all, w_mlp[:, 2 * UNITS : 3 * UNITS], preferred_element_type=wide)
    gate = gate_up[:, :UNITS]
    upward = gate_up[:, UNITS:]
    sigmoid = jax.nn.sigmoid(gate)
    grad_gate = grad_hidden * upward * sigmoid * (1.0 + gate * (1.0 - sigmoid))
    grad_upward = grad_hidden * gate * sigmoid
    grad_gate_up = jnp.concatenate([grad_gate, grad_upward], axis=1).astype(low_type)
    branch = contract(grad_gate_up, w_mlp[:, : 2 * UNITS], 1, 1).astype(low_type)
    branch = branch.reshape(-1, row_count, width)
    grad_mlp = jnp.concatenate(
        [
            contract(normed_mid, grad_gate_up, 0, 0).astype(low_type),
            contract(grad_all, hidden, 0, 0).astype(low_type),
        ],
        axis=1,
    )
    return branch, grad_mlp


def backward_mid(branch, grad_out, kept, mlp_gain):
    middle, scale_two = kept[:2]
    grad_normed_mid = tensor_sum(branch)
    grad_mlp_gain, grad_middle = norm_backward(grad_normed_mid, middle, scale_two, mlp_gain)
    return grad_middle + grad_out.astype(wide), grad_mlp_gain


def backward_attn(grad_middle, kept, weights, tables):
    attn_gain, mlp_gain, bias, w_attn = weights
    allowed, cosine, sine = tables
    resid, scale_one, normed_in, queries, key_all, value_all, log_total, mixed = kept
    row_count, width = resid.shape
    grad_branch = grad_middle.astype(low_type)
    grad_mixed = jnp.dot(grad_branch, w_attn[:, 512:], preferred_element_type=wide)
    grad_mixed = grad_mixed[:, 64:].astype(low_type).reshape(queries.shape)
    scores = jnp.einsum("qgd,td->gqt", queries, key_all, preferred_element_type=wide) * 0.125
    probs = jnp.where(allowed[None], jnp.exp(scores - log_total), 0.0)
    grad_probs = jnp.einsum("qgd,td->gqt", grad_mixed, value_all, preferred_element_type=wide)
    grad_value_all = jnp.einsum(
        "gqt,qgd->td", probs.astype(low_type), grad_mixed, preferred_element_type=wide
    )
    row_delta = jnp.sum(grad_probs * probs, axis=-1, keepdims=True)
    grad_scores = (probs * (grad_probs - row_delta)).astype(low_type)
    grad_queries = (
        jnp.einsum("gqt,td->qgd", grad_scores, key_all, preferred_element_type=wide) * 0.125
    )
    grad_key_all = (
        jnp.einsum("gqt,qgd->td", grad_scores, queries, preferred_element_type=wide) * 0.125
    )
    grad_key_value = jnp.concatenate([grad_key_all, grad_value_all], axis=1).astype(low_type)
    grad_key_value = collect(list(grad_key_value.reshape(-1, row_count, 2 * HD)), "ctx")
    grad_projected = jnp.concatenate(
        [
            rotate_back(grad_queries, cosine[:, None, :], sine[:, None, :]).reshape(row_count, 448),
            rotate_back(grad_key_value[:, :HD], cosine, sine),
            grad_key_value[:, HD:],
            jnp.zeros((row_count, HD), wide),
        ],
        axis=1,
    ).astype(low_type)
    return grad_branch, grad_projected


def backward_in(grad_projected, grad_middle, kept, weights):
    attn_gain, mlp_gain, bias, w_attn = weights
    resid, scale_one = kept[:2]
    grad_normed_in = tensor_sum(contract(grad_projected, w_attn[:, :640], 1, 1))
    grad_attn_gain, grad_resid = norm_backward(grad_normed_in, resid, scale_one, attn_gain)
    return (grad_resid + grad_middle).astype(low_type), grad_attn_gain


def attn_weight_grads(grad_branch, grad_projected, kept):
    normed_in, mixed = kept[2], kept[7]
    grad_bias = jnp.sum(grad_projected.astype(wide), axis=0)
    projection = contract(normed_in, grad_projected, 0, 0)
    output = contract(grad_branch, mixed, 0, 0)
    latter = jnp.pad(projection[:, 512:], ((0, 0), (0, 384))) + output
    return jnp.concatenate([projection[:, :512], latter], axis=1).astype(low_type), grad_bias


def row_blocks(blocks, row_place, axis):
    return [pick(blocks, (row_place + steps) % 4, axis) for steps in (0, 1, 3, 2)]


def send_rows(pieces):
    return [turn_y(piece, steps) for steps, piece in zip((1, 3, 2), pieces)]


def add_all(pieces):
    return sum(piece.astype(wide) for piece in pieces).astype(low_type)


def split_columns(blocks, section_place):
    return pick(blocks, section_place, 1), pick(blocks, 1 - section_place, 1)


def halve(kept, sent):
    return (kept.astype(wide) + turn(sent, "section", 1).astype(wide)).astype(low_type)


def to_column(block):
    hops = []
    for row in range(4):
        hops.append((8 + 2 * row, 8 + 2 * row + 1))
        hops.append((2 * row + 1, 2 * row))
    return lax.ppermute(block, ("section", "fsdp"), hops)


def own_layer(block_zero, block_one, section_place, column_place):
    first = section_place == 0
    hops = []
    for row in range(4):
        hops.append((2 * row, 8 + 2 * row))
        hops.append((8 + 2 * row + 1, 2 * row + 1))
    own = jnp.where(first, block_zero, block_one)
    sent = jnp.where(first, block_one, block_zero)
    received = lax.ppermute(sent, ("section", "fsdp"), hops)
    return jnp.where(section_place == column_place, own, received)


def in_order(pieces, ctx_place):
    own, former, latter, opposite = pieces
    pieces = jnp.stack([own, former, opposite, latter])
    return jnp.stack([pick(pieces, (ctx_place - place) % 4, 0) for place in range(4)])


def pack_lines(small):
    grad_attn_gain, grad_mlp_gain, grad_bias = small
    lines = jnp.concatenate(
        [
            jnp.pad(grad_attn_gain.reshape(8, 112), ((0, 0), (0, 16))),
            jnp.pad(grad_mlp_gain.reshape(8, 112), ((0, 0), (0, 16))),
            jnp.pad(grad_bias[:512].reshape(8, 64), ((0, 0), (0, 64))),
            jnp.pad(grad_bias[512:576].reshape(8, 8), ((0, 0), (0, 632))),
        ],
        axis=1,
    ).astype(low_type)
    return jnp.pad(lines[:, None], ((0, 0), (0, 15), (0, 0))).reshape(4, 2, 16, 1024)


def ctx_blocks(blocks, ctx_place):
    return [
        lax.dynamic_slice_in_dim(blocks, (ctx_place - steps) % 4 * 256, 256, 2)
        for steps in (0, 1, 3, 2)
    ]


def send_ctx(pieces):
    return [turn(piece, "ctx", -steps) for steps, piece in zip((1, 3, 2), pieces)]


def per_device(
    layer_input, cotangent, doc_lengths, attn_gain, w_qkv, b_qkv, w_out, mlp_gain, w_gate_up, w_down
):
    section_place = lax.axis_index("section")
    fsdp_place = lax.axis_index("fsdp")
    row_place, column_place = fsdp_place // 2, fsdp_place % 2
    ctx_place = lax.axis_index("ctx")
    places = (section_place, row_place, column_place, ctx_place)
    row_count, width = layer_input.shape[1:]
    units_all = w_down.shape[1]

    line = jnp.concatenate(
        [
            jnp.pad(attn_gain, ((0, 0), (0, 16))),
            jnp.pad(mlp_gain, ((0, 0), (0, 16))),
            jnp.pad(b_qkv[0], ((0, 0), (0, 696))),
        ],
        axis=1,
    )
    attn_block = jnp.concatenate(
        [
            jnp.concatenate([w_qkv[0, :, 0], w_out[0].T], axis=1),
            jnp.pad(line, ((0, 15), (0, 0))),
        ],
        axis=0,
    )
    past = 4 * UNITS - units_all
    mlp_block = jnp.concatenate(
        [
            jnp.pad(w_gate_up[0], ((0, 0), (0, 0), (0, past))),
            jnp.pad(w_down[0].T, ((0, 0), (0, past)))[:, None],
        ],
        axis=1,
    )
    mlp_block = lax.dynamic_slice_in_dim(mlp_block, ctx_place * UNITS, UNITS, 2)
    mlp_block = jnp.pad(mlp_block.reshape(112, 3 * UNITS), ((0, 0), (0, 128)))

    first = section_place == 0
    layer_in = pick(layer_input, section_place, 0)
    grads_last = pick(cotangent, section_place, 0)
    tables = mask_tables(pick(doc_lengths, section_place, 0)[0], ctx_place, row_count, 4)

    half_attn, late_attn = halves_by_layer(attn_block, section_place)
    half_mlp, late_mlp = halves_by_layer(mlp_block, section_place)
    pair_attn = with_column(half_attn, flip_x(half_attn), column_place)
    pair_attn, half_mlp = after(pair_attn, half_mlp)
    rows_attn = turn_rows(pair_attn)
    pair_mlp = with_column(half_mlp, flip_x(half_mlp), column_place)
    pair_attn, pair_mlp, *rows_attn = after(pair_attn, pair_mlp, *rows_attn)
    moved = [pair_mlp, turn_y(pair_mlp, 1), turn_y(pair_mlp, 3)]
    pieces = [pair_attn] + rows_attn
    weights_zero = attn_weights(pieces, swap_all(pieces), places)

    late = [late_attn, late_mlp]

    def tie_zero(key_value):
        key_value, late[0], late[1], *moved[:] = after(key_value, *late, *moved)
        moved.append(turn_y(moved[0], 2))
        late[:] = [with_column(half, flip_x(half), column_place) for half in late]
        return key_value

    branch, kept_attn_zero = forward_attn(layer_in, weights_zero, tables, tie_zero)
    branch, pair_attn, pair_mlp, grads_last, *pieces = after(branch, *late, grads_last, *moved)
    others = swap_all(pieces)
    grads_all = turn_ctx(grads_last)
    middle, scale_two, normed_mid = forward_mid(branch, kept_attn_zero[0], weights_zero[1])
    normed_mid, pair_attn, *pieces = after(normed_mid, pair_attn, *pieces, *others, *grads_all)
    pieces, grads_all = pieces[:8], pieces[8:]
    rows_attn = [turn_y(pair_attn, 1), turn_y(pair_attn, 3)]
    w_mlp_zero = mlp_weights(pieces[:4], pieces[4:], places)
    normed_mid = stack_rows(normed_mid, turn_ctx(normed_mid))
    normed_mid, pair_attn, pair_mlp, *rows_attn = after(normed_mid, pair_attn, pair_mlp, *rows_attn)
    rows_attn.append(turn_y(pair_attn, 2))
    former = turn_y(pair_mlp, 1)
    gate_up, hidden = forward_mlp(normed_mid, w_mlp_zero)
    kept_mlp_zero = (middle, scale_two, normed_mid, gate_up, hidden)
    branch = collect(forward_down(hidden, w_mlp_zero, row_count), "ctx")
    branch, pair_mlp, *pieces = after(branch, pair_mlp, pair_attn, *rows_attn)
    others = swap_all(pieces)
    latter = turn_y(pair_mlp, 3)
    out_zero = (middle + tensor_sum(branch)).astype(low_type)
    out_zero, pair_mlp, former, latter, *rest = after(
        out_zero, pair_mlp, former, latter, *pieces, *others
    )
    moved[:] = [pair_mlp, former, latter, turn_y(pair_mlp, 2)]
    weights_one = attn_weights(rest[:4], rest[4:], places)

    branch, kept_attn_one = forward_attn(out_zero, weights_one, tables, lambda key_value: key_value)
    branch, *pieces = after(branch, *moved)
    others = swap_all(pieces)
    middle, scale_two, normed_mid = forward_mid(branch, kept_attn_one[0], weights_one[1])
    normed_mid, *pieces = after(normed_mid, *pieces, *others)
    w_mlp_one = mlp_weights(pieces[:4], pieces[4:], places)
    grads_all = stack_rows(grads_last, grads_all)
    normed_mid = stack_rows(normed_mid, turn_ctx(normed_mid))
    gate_up, hidden = forward_mlp(normed_mid, w_mlp_one)
    kept_mlp_one = (middle, scale_two, normed_mid, gate_up, hidden)

    mlp_shape = (4, 2, 112, 3 * UNITS)
    attn_shape = (4, 2, 112, 1024)
    branch, mlp_one = backward_mlp(grads_all, kept_mlp_one, w_mlp_one)
    branch = collect(list(branch), "ctx")
    down = forward_down(hidden, w_mlp_one, row_count)
    down = [down[steps] for steps in (0, 1, 3, 2)]
    branch, mlp_keep, mlp_sent, *down = after(
        branch, *split_columns(mlp_one.reshape(mlp_shape), section_place), *down
    )
    down_moved = send_ctx(down[1:])
    mlp_pieces = row_blocks(halve(mlp_keep, mlp_sent), row_place, 0)
    middle_one, gain_one = backward_mid(branch, grads_last, kept_mlp_one, weights_one[1])
    middle_one, *pieces = after(middle_one, down[0], *down_moved, *mlp_pieces)
    down, mlp_pieces = sum(piece.astype(wide) for piece in pieces[:4]), pieces[4:]
    mlp_moved = send_rows(mlp_pieces[1:3])
    branch_one, projected_one = backward_attn(middle_one, kept_attn_one, weights_one, tables)
    grads_one, attn_gain_one = backward_in(projected_one, middle_one, kept_attn_one, weights_one)
    attn_one, bias_one = attn_weight_grads(branch_one, projected_one, kept_attn_one)
    grads_one, *mlp_pieces = after(grads_one, mlp_pieces[0], mlp_pieces[3], *mlp_moved)

    mlp_pieces[1] = turn_y(mlp_pieces[1], 2)
    attn_sums = halve(*split_columns(attn_one.reshape(attn_shape), section_place))
    grads_all = stack_rows(grads_one, turn_ctx(grads_one))
    grads_all, attn_sums, down, attn_gain_one, bias_one, *mlp_pieces = after(
        grads_all, attn_sums, down, attn_gain_one, bias_one, *mlp_pieces
    )
    lines_one = pack_lines((attn_gain_one, gain_one, bias_one))
    line_sums = halve(*split_columns(lines_one, section_place))
    mlp_one = add_all(mlp_pieces)
    mlp_one = add_all([mlp_one, to_column(mlp_one)])
    out_one = (kept_mlp_one[0] + tensor_sum(down)).astype(low_type)
    branch, mlp_zero = backward_mlp(grads_all, kept_mlp_zero, w_mlp_zero)
    branch = collect(list(branch), "ctx")
    branch, mlp_keep, mlp_sent, mlp_one, out_one, *attn_pieces = after(
        branch,
        *split_columns(mlp_zero.reshape(mlp_shape), section_place),
        mlp_one,
        out_one,
        *ctx_blocks(jnp.concatenate([attn_sums, line_sums], axis=1), ctx_place),
    )
    mlp_pieces = row_blocks(halve(mlp_keep, mlp_sent), row_place, 0)
    attn_moved = send_ctx(attn_pieces[1:])
    middle_zero, gain_zero = backward_mid(branch, grads_one, kept_mlp_zero, weights_zero[1])
    middle_zero, *pieces = after(middle_zero, attn_pieces[0], *attn_moved, *mlp_pieces)
    attn_one, mlp_pieces = add_all(pieces[:4]), pieces[4:]
    mlp_moved = send_rows(mlp_pieces[1:3])
    branch_zero, projected_zero = backward_attn(middle_zero, kept_attn_zero, weights_zero, tables)
    projected_zero, *pieces = after(projected_zero, mlp_pieces[0], mlp_pieces[3], *mlp_moved)
    mlp_pieces = [pieces[0], pieces[2], pieces[3], turn_y(pieces[1], 2)]
    attn_zero, bias_zero = attn_weight_grads(branch_zero, projected_zero, kept_attn_zero)
    attn_sums = halve(*split_columns(attn_zero.reshape(attn_shape), section_place))
    attn_pieces = ctx_blocks(attn_sums, ctx_place)
    attn_moved = send_ctx(attn_pieces[1:])
    grads_zero, attn_gain_zero = backward_in(
        projected_zero, middle_zero, kept_attn_zero, weights_zero
    )
    attn_gain_zero, *mlp_pieces = after(attn_gain_zero, *mlp_pieces)

    mlp_zero = add_all(mlp_pieces)
    mlp_moved = to_column(mlp_zero)
    lines_zero = pack_lines((attn_gain_zero, gain_zero, bias_zero))
    line_pieces = ctx_blocks(halve(*split_columns(lines_zero, section_place)), ctx_place)
    line_moved = send_ctx(line_pieces[1:])
    attn_zero = jnp.concatenate(
        [add_all([attn_pieces[0]] + attn_moved), add_all([line_pieces[0]] + line_moved)], axis=1
    )
    attn_zero, mlp_zero, mlp_moved = after(attn_zero, mlp_zero, mlp_moved)
    mlp_zero = add_all([mlp_zero, mlp_moved])
    mlp = own_layer(mlp_zero, mlp_one, section_place, column_place)
    attn_pieces = row_blocks(jnp.stack([attn_zero, attn_one]), row_place, 1)
    mlp, *attn_pieces = after(mlp, *attn_pieces)
    mlp_all = [turn(mlp, "ctx", 1), turn(mlp, "ctx", 3)]
    attn_both = add_all(attn_pieces[:1] + send_rows(attn_pieces[1:]))
    attn_both, mlp, *mlp_all = after(attn_both, mlp, *mlp_all)
    mlp_all.append(turn(mlp, "ctx", 2))
    attn_both = add_all([attn_both, to_column(attn_both)])
    attn = own_layer(attn_both[0], attn_both[1], section_place, column_place)
    attn, mlp, *mlp_all = after(attn, mlp, *mlp_all)
    attn_all = turn_ctx(attn)
    mlp = in_order([mlp] + mlp_all, ctx_place).reshape(4, 112, 3, UNITS)
    gate_up = mlp[:, :, :2].transpose(1, 2, 0, 3).reshape(112, 2, 4 * UNITS)[:, :, :units_all]
    down = mlp[:, :, 2].transpose(0, 2, 1).reshape(4 * UNITS, 112)[:units_all]
    attn = in_order([attn] + attn_all, ctx_place)
    outputs = [out_zero, out_one]

    def by_layer(values):
        own = jnp.where(first, values[0], values[1])
        other = turn(jnp.where(first, values[1], values[0]), "section", 1)
        return jnp.where(first, jnp.stack([own, other]), jnp.stack([other, own]))[None]

    hidden_states = by_layer(outputs)
    input_grads = by_layer([grads_zero, grads_one])
    attn = attn.transpose(1, 0, 2).reshape(128, 1024).astype(wide)
    lines = attn[112:113]
    return (
        hidden_states,
        input_grads,
        lines[:, :112],
        attn[None, :112, None, :576],
        lines[None, :, 256:320],
        lines[None, :, 384:392],
        attn[:112, 576:].T[None],
        lines[:, 128:240],
        gate_up.astype(wide)[None],
        down.astype(wide)[None],
    )


def solution(mesh):
    return jax.shard_map(
        per_device,
        mesh=mesh,
        in_specs=(
            P(None, ("fsdp", "ctx"), None),
            P(None, ("fsdp", "ctx"), None),
            P(None, "fsdp", None),
            P("section", "fsdp"),
            P("section", "fsdp", "tp", None),
            P("section", "tp", "fsdp"),
            P("section", "tp", "fsdp"),
            P("section", "fsdp"),
            P("section", "fsdp", None, "tp"),
            P("section", "tp", "fsdp"),
        ),
        out_specs=(
            P("section", None, ("fsdp", "ctx"), None),
            P("section", None, ("fsdp", "ctx"), None),
            P("section", "fsdp"),
            P("section", "fsdp", "tp", None),
            P("section", "tp", "fsdp"),
            P("section", "tp", "fsdp"),
            P("section", "tp", "fsdp"),
            P("section", "fsdp"),
            P("section", "fsdp", None, "tp"),
            P("section", "tp", "fsdp"),
        ),
        check_vma=False,
    )
```

```python
import jax
import jax.numpy as jnp
from jax import lax
from jax.experimental import pallas as pl
from jax.experimental.pallas import tpu as pltpu
from jax.sharding import PartitionSpec as P

HD = 64
UNITS = 640

epsilon = 1e-06
rope_base = 1000000.0
masked_score = -1000000000.0
low_type = jnp.bfloat16
wide = jnp.float32


def contract(left, right, left_dim, right_dim):
    return lax.dot_general(
        left, right, (((left_dim,), (right_dim,)), ((), ())), preferred_element_type=wide
    )


def turn(value, axis, steps):
    count = lax.axis_size(axis)
    return lax.ppermute(value, axis, [(place, (place + steps) % count) for place in range(count)])


def turn_y(value, steps):
    count = lax.axis_size("fsdp")
    return lax.ppermute(
        value, "fsdp", [(place, (place + 2 * steps) % count) for place in range(count)]
    )


def flip_x(value):
    count = lax.axis_size("fsdp")
    return lax.ppermute(value, "fsdp", [(place, place ^ 1) for place in range(count)])


def collect(blocks, axis):
    count = lax.axis_size(axis)
    order = [1, count - 1] + list(range(2, count - 1))
    total = blocks[0].astype(wide)
    for steps in order:
        total = total + turn(blocks[steps], axis, -steps).astype(wide)
    return total


def pick(array, place, axis):
    return lax.dynamic_index_in_dim(array, place, axis, keepdims=False)


def turn_ctx(block):
    return [turn(block, "ctx", steps) for steps in (1, 3, 2)]


def stack_rows(own, moved):
    former, latter, opposite = moved
    return jnp.concatenate([own, former, opposite, latter], axis=0)


def tensor_sum(partial_value):
    own = lax.optimization_barrier(partial_value.astype(low_type))
    return own.astype(wide) + turn(own, "tp", 1).astype(wide)


def after(value, *others):
    tied = lax.optimization_barrier((value,) + others)
    return tied[0] if not others else tied


def with_column(half, received, column_place):
    pair = jnp.zeros((2,) + half.shape, half.dtype)
    pair = lax.dynamic_update_slice(pair, half[None], (column_place, 0, 0))
    return lax.dynamic_update_slice(pair, received[None], (1 - column_place, 0, 0))


def turn_rows(pair):
    return [turn_y(pair, steps) for steps in (1, 3, 2)]


def swap_all(pieces):
    return [turn(piece, "section", 1) for piece in pieces]


def place_pieces(lines, row_count, places, *refs):
    pieces, outs = refs[:8], refs[8:]
    columns = pieces[0].shape[2]
    for index, piece in enumerate(pieces):
        row = lax.rem(places[0] + 4 - (0, 1, 3, 2)[index % 4], 4)
        half = places[1] if index < 4 else 1 - places[1]
        start = pl.multiple_of(half * columns, 128)
        for column in range(2):
            where = (row * 2 + column, slice(None), pl.ds(start, columns))
            outs[0][where] = piece[column, pl.ds(0, row_count), :]
            if lines:
                outs[1][where] = piece[column, pl.ds(row_count, lines), :]


def put_together(pieces, others, places, lines):
    rows, columns = pieces[0].shape[1:]
    shapes = [jax.ShapeDtypeStruct((8, rows - lines, 2 * columns), low_type)]
    if lines:
        shapes.append(jax.ShapeDtypeStruct((8, lines, 2 * columns), low_type))
    place = jnp.stack([places[1], places[0]]).astype(jnp.int32)
    size = 8 * rows * 2 * columns * 2
    return pl.pallas_call(
        lambda *refs: place_pieces(lines, rows - lines, *refs),
        out_shape=shapes,
        in_specs=[pl.BlockSpec(memory_space=pltpu.SMEM)] + [pl.BlockSpec(memory_space=pltpu.VMEM)] * 8,
        out_specs=[pl.BlockSpec(memory_space=pltpu.VMEM)] * len(shapes),
        compiler_params=pltpu.CompilerParams(vmem_limit_bytes=20 << 20),
        cost_estimate=pl.CostEstimate(flops=0, bytes_accessed=2 * size, transcendentals=0),
    )(place, *pieces, *others)


def attn_weights(pieces, others, places):
    width = 8 * 112
    w_attn, lines = put_together(pieces, others, places, 16)
    lines = lines[:, 0].astype(wide)
    return (
        lines[:, :112].reshape(width),
        lines[:, 128:240].reshape(width),
        jnp.pad(lines[:, 256:328].reshape(576), (0, 64)),
        w_attn.reshape(width, 1024),
    )


def mlp_weights(pieces, others, places):
    return put_together(pieces, others, places, 0)[0].reshape(8 * 112, 2048)


def halves_by_layer(block, section_place):
    columns = block.shape[1] // 2
    kept = lax.dynamic_slice_in_dim(block, section_place * columns, columns, 1)
    sent = lax.dynamic_slice_in_dim(block, (1 - section_place) * columns, columns, 1)
    received = turn(sent, "section", 1)
    first = section_place == 0
    return jnp.where(first, kept, received), jnp.where(first, received, kept)


def rotary_tables(position):
    inverse = rope_base ** (-jnp.arange(0, HD, 2, dtype=wide) / HD)
    angles = position.astype(wide)[..., None] * inverse
    angles = jnp.concatenate([angles, angles], axis=-1)
    return (jnp.cos(angles), jnp.sin(angles))


def rotate(values, cosine, sine):
    half_width = values.shape[-1] // 2
    turned = jnp.concatenate([-values[..., half_width:], values[..., :half_width]], axis=-1)
    return values * cosine + turned * sine


def rotate_back(grads, cosine, sine):
    half_width = grads.shape[-1] // 2
    scaled = grads * sine
    turned = jnp.concatenate([scaled[..., half_width:], -scaled[..., :half_width]], axis=-1)
    return grads * cosine + turned


def norm_backward(grad_normed, resid, scale, gain):
    grad_gain = jnp.sum(grad_normed * resid * scale, axis=0)
    inner = grad_normed * gain
    grad_resid = scale * inner - resid * (scale * scale * scale) * jnp.mean(
        inner * resid, axis=-1, keepdims=True
    )
    return (grad_gain, grad_resid)


def mask_tables(lengths, ctx_place, row_count, ctx_count):
    doc_ends = jnp.cumsum(lengths, axis=-1)
    blocks = (ctx_place - jnp.arange(ctx_count, dtype=jnp.int32)) % ctx_count
    places = (blocks[:, None] * row_count + jnp.arange(row_count, dtype=jnp.int32)).reshape(-1)
    passed = places[:, None] >= doc_ends[None, :]
    segment = jnp.sum(passed.astype(jnp.int32), axis=-1)
    doc_start = jnp.sum(jnp.where(passed, lengths[None, :], 0), axis=-1)
    position = places - doc_start
    cosine, sine = rotary_tables(position[:row_count])
    allowed = (segment[:row_count, None] == segment[None, :]) & (
        places[:row_count, None] >= places[None, :]
    )
    return (allowed, cosine, sine)


def normed(resid, gain):
    scale = lax.rsqrt(jnp.mean(resid * resid, axis=-1, keepdims=True) + epsilon)
    return scale, (resid * scale * gain).astype(low_type)


def forward_attn(layer_in, weights, tables, tie):
    attn_gain, mlp_gain, bias, w_attn = weights
    allowed, cosine, sine = tables
    row_count, width = layer_in.shape
    resid = layer_in.astype(wide)
    scale_one, normed_in = normed(resid, attn_gain)
    projected = jnp.dot(normed_in, w_attn[:, :640], preferred_element_type=wide) + bias
    queries = rotate(
        projected[:, :448].reshape(row_count, 7, HD), cosine[:, None, :], sine[:, None, :]
    ).astype(low_type)
    key_own = rotate(projected[:, 448:512], cosine, sine)
    key_value = jnp.concatenate([key_own, projected[:, 512:576]], axis=1).astype(low_type)
    key_value = tie(stack_rows(key_value, turn_ctx(key_value)))
    key_all, value_all = key_value[:, :HD], key_value[:, HD:]
    scores = jnp.einsum("qgd,td->gqt", queries, key_all, preferred_element_type=wide) * 0.125
    scores = jnp.where(allowed[None], scores, masked_score)
    largest = jnp.max(scores, axis=-1, keepdims=True)
    raised = jnp.exp(scores - largest)
    totals = jnp.sum(raised, axis=-1, keepdims=True)
    log_total = largest + jnp.log(totals)
    probs = (raised / totals).astype(low_type)
    mixed = jnp.einsum("gqt,td->qgd", probs, value_all, preferred_element_type=wide)
    mixed = jnp.pad(mixed.reshape(row_count, 448).astype(low_type), ((0, 0), (64, 0)))
    kept = (resid, scale_one, normed_in, queries, key_all, value_all, log_total, mixed)
    return contract(mixed, w_attn[:, 512:], 1, 1), kept


def forward_mid(branch, resid, mlp_gain):
    middle = resid + tensor_sum(branch)
    return middle, *normed(middle, mlp_gain)


def forward_mlp(normed_mid, w_mlp):
    gate_up = jnp.dot(normed_mid, w_mlp[:, : 2 * UNITS], preferred_element_type=wide)
    hidden = (jax.nn.silu(gate_up[:, :UNITS]) * gate_up[:, UNITS:]).astype(low_type)
    return gate_up, hidden


def forward_down(hidden, w_mlp, row_count):
    branch = contract(hidden, w_mlp[:, 2 * UNITS : 3 * UNITS], 1, 1).astype(low_type)
    return list(branch.reshape(-1, row_count, branch.shape[1]))


def backward_mlp(grad_all, kept, w_mlp):
    middle, scale_two, normed_mid, gate_up, hidden = kept
    row_count, width = middle.shape
    grad_hidden = jnp.dot(grad_all, w_mlp[:, 2 * UNITS : 3 * UNITS], preferred_element_type=wide)
    gate = gate_up[:, :UNITS]
    upward = gate_up[:, UNITS:]
    sigmoid = jax.nn.sigmoid(gate)
    grad_gate = grad_hidden * upward * sigmoid * (1.0 + gate * (1.0 - sigmoid))
    grad_upward = grad_hidden * gate * sigmoid
    grad_gate_up = jnp.concatenate([grad_gate, grad_upward], axis=1).astype(low_type)
    branch = contract(grad_gate_up, w_mlp[:, : 2 * UNITS], 1, 1).astype(low_type)
    branch = branch.reshape(-1, row_count, width)
    grad_mlp = jnp.concatenate(
        [
            contract(normed_mid, grad_gate_up, 0, 0).astype(low_type),
            contract(grad_all, hidden, 0, 0).astype(low_type),
        ],
        axis=1,
    )
    return branch, grad_mlp


def backward_mid(branch, grad_out, kept, mlp_gain):
    middle, scale_two = kept[:2]
    grad_normed_mid = tensor_sum(branch)
    grad_mlp_gain, grad_middle = norm_backward(grad_normed_mid, middle, scale_two, mlp_gain)
    return grad_middle + grad_out.astype(wide), grad_mlp_gain


def backward_attn(grad_middle, kept, weights, tables):
    attn_gain, mlp_gain, bias, w_attn = weights
    allowed, cosine, sine = tables
    resid, scale_one, normed_in, queries, key_all, value_all, log_total, mixed = kept
    row_count, width = resid.shape
    grad_branch = grad_middle.astype(low_type)
    grad_mixed = jnp.dot(grad_branch, w_attn[:, 512:], preferred_element_type=wide)
    grad_mixed = grad_mixed[:, 64:].astype(low_type).reshape(queries.shape)
    scores = jnp.einsum("qgd,td->gqt", queries, key_all, preferred_element_type=wide) * 0.125
    probs = jnp.where(allowed[None], jnp.exp(scores - log_total), 0.0)
    grad_probs = jnp.einsum("qgd,td->gqt", grad_mixed, value_all, preferred_element_type=wide)
    grad_value_all = jnp.einsum(
        "gqt,qgd->td", probs.astype(low_type), grad_mixed, preferred_element_type=wide
    )
    row_delta = jnp.sum(grad_probs * probs, axis=-1, keepdims=True)
    grad_scores = (probs * (grad_probs - row_delta)).astype(low_type)
    grad_queries = (
        jnp.einsum("gqt,td->qgd", grad_scores, key_all, preferred_element_type=wide) * 0.125
    )
    grad_key_all = (
        jnp.einsum("gqt,qgd->td", grad_scores, queries, preferred_element_type=wide) * 0.125
    )
    grad_key_value = jnp.concatenate([grad_key_all, grad_value_all], axis=1).astype(low_type)
    grad_key_value = collect(list(grad_key_value.reshape(-1, row_count, 2 * HD)), "ctx")
    grad_projected = jnp.concatenate(
        [
            rotate_back(grad_queries, cosine[:, None, :], sine[:, None, :]).reshape(row_count, 448),
            rotate_back(grad_key_value[:, :HD], cosine, sine),
            grad_key_value[:, HD:],
            jnp.zeros((row_count, HD), wide),
        ],
        axis=1,
    ).astype(low_type)
    return grad_branch, grad_projected


def backward_in(grad_projected, grad_middle, kept, weights):
    attn_gain, mlp_gain, bias, w_attn = weights
    resid, scale_one = kept[:2]
    grad_normed_in = tensor_sum(contract(grad_projected, w_attn[:, :640], 1, 1))
    grad_attn_gain, grad_resid = norm_backward(grad_normed_in, resid, scale_one, attn_gain)
    return (grad_resid + grad_middle).astype(low_type), grad_attn_gain


def attn_weight_grads(grad_branch, grad_projected, kept):
    normed_in, mixed = kept[2], kept[7]
    grad_bias = jnp.sum(grad_projected.astype(wide), axis=0)
    projection = contract(normed_in, grad_projected, 0, 0)
    output = contract(grad_branch, mixed, 0, 0)
    latter = jnp.pad(projection[:, 512:], ((0, 0), (0, 384))) + output
    return jnp.concatenate([projection[:, :512], latter], axis=1).astype(low_type), grad_bias


def row_blocks(blocks, row_place, axis):
    return [pick(blocks, (row_place + steps) % 4, axis) for steps in (0, 1, 3, 2)]


def send_rows(pieces):
    return [turn_y(piece, steps) for steps, piece in zip((1, 3, 2), pieces)]


def add_all(pieces):
    return sum(piece.astype(wide) for piece in pieces).astype(low_type)


def split_columns(blocks, section_place):
    return pick(blocks, section_place, 1), pick(blocks, 1 - section_place, 1)


def halve(kept, sent):
    return (kept.astype(wide) + turn(sent, "section", 1).astype(wide)).astype(low_type)


def to_column(block):
    hops = []
    for row in range(4):
        hops.append((8 + 2 * row, 8 + 2 * row + 1))
        hops.append((2 * row + 1, 2 * row))
    return lax.ppermute(block, ("section", "fsdp"), hops)


def own_layer(block_zero, block_one, section_place, column_place):
    first = section_place == 0
    hops = []
    for row in range(4):
        hops.append((2 * row, 8 + 2 * row))
        hops.append((8 + 2 * row + 1, 2 * row + 1))
    own = jnp.where(first, block_zero, block_one)
    sent = jnp.where(first, block_one, block_zero)
    received = lax.ppermute(sent, ("section", "fsdp"), hops)
    return jnp.where(section_place == column_place, own, received)


def in_order(pieces, ctx_place):
    own, former, latter, opposite = pieces
    pieces = jnp.stack([own, former, opposite, latter])
    return jnp.stack([pick(pieces, (ctx_place - place) % 4, 0) for place in range(4)])


def pack_lines(small):
    grad_attn_gain, grad_mlp_gain, grad_bias = small
    lines = jnp.concatenate(
        [
            jnp.pad(grad_attn_gain.reshape(8, 112), ((0, 0), (0, 16))),
            jnp.pad(grad_mlp_gain.reshape(8, 112), ((0, 0), (0, 16))),
            jnp.pad(grad_bias[:512].reshape(8, 64), ((0, 0), (0, 64))),
            jnp.pad(grad_bias[512:576].reshape(8, 8), ((0, 0), (0, 632))),
        ],
        axis=1,
    ).astype(low_type)
    return jnp.pad(lines[:, None], ((0, 0), (0, 15), (0, 0))).reshape(4, 2, 16, 1024)


def ctx_blocks(blocks, ctx_place):
    return [
        lax.dynamic_slice_in_dim(blocks, (ctx_place - steps) % 4 * 256, 256, 2)
        for steps in (0, 1, 3, 2)
    ]


def send_ctx(pieces):
    return [turn(piece, "ctx", -steps) for steps, piece in zip((1, 3, 2), pieces)]


def per_device(
    layer_input, cotangent, doc_lengths, attn_gain, w_qkv, b_qkv, w_out, mlp_gain, w_gate_up, w_down
):
    section_place = lax.axis_index("section")
    fsdp_place = lax.axis_index("fsdp")
    row_place, column_place = fsdp_place // 2, fsdp_place % 2
    ctx_place = lax.axis_index("ctx")
    places = (section_place, row_place, column_place, ctx_place)
    row_count, width = layer_input.shape[1:]
    units_all = w_down.shape[1]

    line = jnp.concatenate(
        [
            jnp.pad(attn_gain, ((0, 0), (0, 16))),
            jnp.pad(mlp_gain, ((0, 0), (0, 16))),
            jnp.pad(b_qkv[0], ((0, 0), (0, 696))),
        ],
        axis=1,
    )
    attn_block = jnp.concatenate(
        [
            jnp.concatenate([w_qkv[0, :, 0], w_out[0].T], axis=1),
            jnp.pad(line, ((0, 15), (0, 0))),
        ],
        axis=0,
    )
    past = 4 * UNITS - units_all
    mlp_block = jnp.concatenate(
        [
            jnp.pad(w_gate_up[0], ((0, 0), (0, 0), (0, past))),
            jnp.pad(w_down[0].T, ((0, 0), (0, past)))[:, None],
        ],
        axis=1,
    )
    mlp_block = lax.dynamic_slice_in_dim(mlp_block, ctx_place * UNITS, UNITS, 2)
    mlp_block = jnp.pad(mlp_block.reshape(112, 3 * UNITS), ((0, 0), (0, 128)))

    first = section_place == 0
    layer_in = pick(layer_input, section_place, 0)
    grads_last = pick(cotangent, section_place, 0)
    tables = mask_tables(pick(doc_lengths, section_place, 0)[0], ctx_place, row_count, 4)

    half_attn, late_attn = halves_by_layer(attn_block, section_place)
    half_mlp, late_mlp = halves_by_layer(mlp_block, section_place)
    pair_attn = with_column(half_attn, flip_x(half_attn), column_place)
    pair_attn, half_mlp = after(pair_attn, half_mlp)
    rows_attn = turn_rows(pair_attn)
    pair_mlp = with_column(half_mlp, flip_x(half_mlp), column_place)
    pair_attn, pair_mlp, *rows_attn = after(pair_attn, pair_mlp, *rows_attn)
    moved = [pair_mlp, turn_y(pair_mlp, 1), turn_y(pair_mlp, 3)]
    pieces = [pair_attn] + rows_attn
    weights_zero = attn_weights(pieces, swap_all(pieces), places)

    late = [late_attn, late_mlp]

    def tie_zero(key_value):
        key_value, late[0], late[1], *moved[:] = after(key_value, *late, *moved)
        moved.append(turn_y(moved[0], 2))
        late[:] = [with_column(half, flip_x(half), column_place) for half in late]
        return key_value

    branch, kept_attn_zero = forward_attn(layer_in, weights_zero, tables, tie_zero)
    branch, pair_attn, pair_mlp, *pieces = after(branch, *late, *moved)
    others = swap_all(pieces)
    middle, scale_two, normed_mid = forward_mid(branch, kept_attn_zero[0], weights_zero[1])
    normed_mid, pair_attn, *pieces = after(normed_mid, pair_attn, *pieces, *others)
    rows_attn = [turn_y(pair_attn, 1), turn_y(pair_attn, 3)]
    w_mlp_zero = mlp_weights(pieces[:4], pieces[4:], places)
    normed_mid = stack_rows(normed_mid, turn_ctx(normed_mid))
    normed_mid, pair_attn, pair_mlp, *rows_attn = after(normed_mid, pair_attn, pair_mlp, *rows_attn)
    rows_attn.append(turn_y(pair_attn, 2))
    gate_up, hidden = forward_mlp(normed_mid, w_mlp_zero)
    kept_mlp_zero = (middle, scale_two, normed_mid, gate_up, hidden)
    branch = collect(forward_down(hidden, w_mlp_zero, row_count), "ctx")
    branch, pair_mlp, *pieces = after(branch, pair_mlp, pair_attn, *rows_attn)
    others = swap_all(pieces)
    former, latter = turn_y(pair_mlp, 1), turn_y(pair_mlp, 3)
    out_zero = (middle + tensor_sum(branch)).astype(low_type)
    out_zero, pair_mlp, former, latter, *rest = after(
        out_zero, pair_mlp, former, latter, *pieces, *others
    )
    moved[:] = [pair_mlp, former, latter, turn_y(pair_mlp, 2)]
    weights_one = attn_weights(rest[:4], rest[4:], places)

    branch, kept_attn_one = forward_attn(out_zero, weights_one, tables, lambda key_value: key_value)
    branch, grads_last, *pieces = after(branch, grads_last, *moved)
    grads_all = turn_ctx(grads_last)
    others = swap_all(pieces)
    middle, scale_two, normed_mid = forward_mid(branch, kept_attn_one[0], weights_one[1])
    normed_mid, *pieces = after(normed_mid, *pieces, *others, *grads_all)
    pieces, grads_all = pieces[:8], pieces[8:]
    w_mlp_one = mlp_weights(pieces[:4], pieces[4:], places)
    grads_all = stack_rows(grads_last, grads_all)
    normed_mid = stack_rows(normed_mid, turn_ctx(normed_mid))
    gate_up, hidden = forward_mlp(normed_mid, w_mlp_one)
    kept_mlp_one = (middle, scale_two, normed_mid, gate_up, hidden)

    mlp_shape = (4, 2, 112, 3 * UNITS)
    attn_shape = (4, 2, 112, 1024)
    branch, mlp_one = backward_mlp(grads_all, kept_mlp_one, w_mlp_one)
    branch = collect(list(branch), "ctx")
    down = forward_down(hidden, w_mlp_one, row_count)
    down = [down[steps] for steps in (0, 1, 3, 2)]
    branch, mlp_keep, mlp_sent, *down = after(
        branch, *split_columns(mlp_one.reshape(mlp_shape), section_place), *down
    )
    down_moved = send_ctx(down[1:])
    mlp_pieces = row_blocks(halve(mlp_keep, mlp_sent), row_place, 0)
    middle_one, gain_one = backward_mid(branch, grads_last, kept_mlp_one, weights_one[1])
    middle_one, *pieces = after(middle_one, down[0], *down_moved, *mlp_pieces)
    down, mlp_pieces = sum(piece.astype(wide) for piece in pieces[:4]), pieces[4:]
    mlp_moved = send_rows(mlp_pieces[1:3])
    branch_one, projected_one = backward_attn(middle_one, kept_attn_one, weights_one, tables)
    grads_one, attn_gain_one = backward_in(projected_one, middle_one, kept_attn_one, weights_one)
    attn_one, bias_one = attn_weight_grads(branch_one, projected_one, kept_attn_one)
    grads_one, *mlp_pieces = after(grads_one, mlp_pieces[0], mlp_pieces[3], *mlp_moved)

    mlp_pieces[1] = turn_y(mlp_pieces[1], 2)
    attn_sums = halve(*split_columns(attn_one.reshape(attn_shape), section_place))
    grads_all = stack_rows(grads_one, turn_ctx(grads_one))
    grads_all, attn_sums, down, attn_gain_one, bias_one, *mlp_pieces = after(
        grads_all, attn_sums, down, attn_gain_one, bias_one, *mlp_pieces
    )
    lines_one = pack_lines((attn_gain_one, gain_one, bias_one))
    line_sums = halve(*split_columns(lines_one, section_place))
    mlp_one = add_all(mlp_pieces)
    mlp_one = add_all([mlp_one, to_column(mlp_one)])
    out_one = (kept_mlp_one[0] + tensor_sum(down)).astype(low_type)
    branch, mlp_zero = backward_mlp(grads_all, kept_mlp_zero, w_mlp_zero)
    branch = collect(list(branch), "ctx")
    branch, mlp_keep, mlp_sent, mlp_one, out_one, *attn_pieces = after(
        branch,
        *split_columns(mlp_zero.reshape(mlp_shape), section_place),
        mlp_one,
        out_one,
        *ctx_blocks(jnp.concatenate([attn_sums, line_sums], axis=1), ctx_place),
    )
    mlp_pieces = row_blocks(halve(mlp_keep, mlp_sent), row_place, 0)
    attn_moved = send_ctx(attn_pieces[1:])
    middle_zero, gain_zero = backward_mid(branch, grads_one, kept_mlp_zero, weights_zero[1])
    middle_zero, *pieces = after(middle_zero, attn_pieces[0], *attn_moved, *mlp_pieces)
    attn_one, mlp_pieces = add_all(pieces[:4]), pieces[4:]
    mlp_moved = send_rows(mlp_pieces[1:3])
    branch_zero, projected_zero = backward_attn(middle_zero, kept_attn_zero, weights_zero, tables)
    projected_zero, *pieces = after(projected_zero, mlp_pieces[0], mlp_pieces[3], *mlp_moved)
    mlp_pieces = [pieces[0], pieces[2], pieces[3], turn_y(pieces[1], 2)]
    attn_zero, bias_zero = attn_weight_grads(branch_zero, projected_zero, kept_attn_zero)
    attn_sums = halve(*split_columns(attn_zero.reshape(attn_shape), section_place))
    attn_pieces = ctx_blocks(attn_sums, ctx_place)
    attn_moved = send_ctx(attn_pieces[1:])
    grads_zero, attn_gain_zero = backward_in(
        projected_zero, middle_zero, kept_attn_zero, weights_zero
    )
    attn_gain_zero, *pieces = after(
        attn_gain_zero, attn_pieces[0], *attn_moved, *mlp_pieces
    )

    attn_zero, mlp_zero = add_all(pieces[:4]), add_all(pieces[4:])
    mlp_zero = add_all([mlp_zero, to_column(mlp_zero)])
    mlp = own_layer(mlp_zero, mlp_one, section_place, column_place)
    lines_zero = pack_lines((attn_gain_zero, gain_zero, bias_zero))
    line_pieces = ctx_blocks(halve(*split_columns(lines_zero, section_place)), ctx_place)
    lines_zero = add_all(line_pieces[:1] + send_ctx(line_pieces[1:]))
    lines_zero, attn_zero, mlp = after(lines_zero, attn_zero, mlp)
    attn_zero = jnp.concatenate([attn_zero, lines_zero], axis=1)
    attn_pieces = row_blocks(jnp.stack([attn_zero, attn_one]), row_place, 1)
    mlp_all = [turn(mlp, "ctx", 1), turn(mlp, "ctx", 3)]
    attn_both = add_all(attn_pieces[:1] + send_rows(attn_pieces[1:]))
    attn_both, mlp, *mlp_all = after(attn_both, mlp, *mlp_all)
    mlp_all.append(turn(mlp, "ctx", 2))
    attn_both = add_all([attn_both, to_column(attn_both)])
    attn = own_layer(attn_both[0], attn_both[1], section_place, column_place)
    attn, mlp, *mlp_all = after(attn, mlp, *mlp_all)
    attn_all = turn_ctx(attn)
    mlp = in_order([mlp] + mlp_all, ctx_place).reshape(4, 112, 3, UNITS)
    gate_up = mlp[:, :, :2].transpose(1, 2, 0, 3).reshape(112, 2, 4 * UNITS)[:, :, :units_all]
    down = mlp[:, :, 2].transpose(0, 2, 1).reshape(4 * UNITS, 112)[:units_all]
    attn = in_order([attn] + attn_all, ctx_place)
    outputs = [out_zero, out_one]

    def by_layer(values):
        own = jnp.where(first, values[0], values[1])
        other = turn(jnp.where(first, values[1], values[0]), "section", 1)
        return jnp.where(first, jnp.stack([own, other]), jnp.stack([other, own]))[None]

    hidden_states = by_layer(outputs)
    input_grads = by_layer([grads_zero, grads_one])
    attn = attn.transpose(1, 0, 2).reshape(128, 1024).astype(wide)
    lines = attn[112:113]
    return (
        hidden_states,
        input_grads,
        lines[:, :112],
        attn[None, :112, None, :576],
        lines[None, :, 256:320],
        lines[None, :, 384:392],
        attn[:112, 576:].T[None],
        lines[:, 128:240],
        gate_up.astype(wide)[None],
        down.astype(wide)[None],
    )


def solution(mesh):
    return jax.shard_map(
        per_device,
        mesh=mesh,
        in_specs=(
            P(None, ("fsdp", "ctx"), None),
            P(None, ("fsdp", "ctx"), None),
            P(None, "fsdp", None),
            P("section", "fsdp"),
            P("section", "fsdp", "tp", None),
            P("section", "tp", "fsdp"),
            P("section", "tp", "fsdp"),
            P("section", "fsdp"),
            P("section", "fsdp", None, "tp"),
            P("section", "tp", "fsdp"),
        ),
        out_specs=(
            P("section", None, ("fsdp", "ctx"), None),
            P("section", None, ("fsdp", "ctx"), None),
            P("section", "fsdp"),
            P("section", "fsdp", "tp", None),
            P("section", "tp", "fsdp"),
            P("section", "tp", "fsdp"),
            P("section", "tp", "fsdp"),
            P("section", "fsdp"),
            P("section", "fsdp", None, "tp"),
            P("section", "tp", "fsdp"),
        ),
        check_vma=False,
    )
```

```python
import jax
import jax.numpy as jnp
from jax import lax
from jax.experimental import pallas as pl
from jax.experimental.pallas import tpu as pltpu
from jax.sharding import PartitionSpec as P

HD = 64
UNITS = 640

epsilon = 1e-06
rope_base = 1000000.0
masked_score = -1000000000.0
low_type = jnp.bfloat16
wide = jnp.float32


def contract(left, right, left_dim, right_dim):
    return lax.dot_general(
        left, right, (((left_dim,), (right_dim,)), ((), ())), preferred_element_type=wide
    )


def turn(value, axis, steps):
    count = lax.axis_size(axis)
    return lax.ppermute(value, axis, [(place, (place + steps) % count) for place in range(count)])


def turn_y(value, steps):
    count = lax.axis_size("fsdp")
    return lax.ppermute(
        value, "fsdp", [(place, (place + 2 * steps) % count) for place in range(count)]
    )


def flip_x(value):
    count = lax.axis_size("fsdp")
    return lax.ppermute(value, "fsdp", [(place, place ^ 1) for place in range(count)])


def collect(blocks, axis):
    count = lax.axis_size(axis)
    order = [1, count - 1] + list(range(2, count - 1))
    total = blocks[0].astype(wide)
    for steps in order:
        total = total + turn(blocks[steps], axis, -steps).astype(wide)
    return total


def pick(array, place, axis):
    return lax.dynamic_index_in_dim(array, place, axis, keepdims=False)


def turn_ctx(block):
    return [turn(block, "ctx", steps) for steps in (1, 3, 2)]


def stack_rows(own, moved):
    former, latter, opposite = moved
    return jnp.concatenate([own, former, opposite, latter], axis=0)


def tensor_sum(partial_value):
    own = lax.optimization_barrier(partial_value.astype(low_type))
    return own.astype(wide) + turn(own, "tp", 1).astype(wide)


def after(value, *others):
    tied = lax.optimization_barrier((value,) + others)
    return tied[0] if not others else tied


def with_column(half, received, column_place):
    pair = jnp.zeros((2,) + half.shape, half.dtype)
    pair = lax.dynamic_update_slice(pair, half[None], (column_place, 0, 0))
    return lax.dynamic_update_slice(pair, received[None], (1 - column_place, 0, 0))


def turn_rows(pair):
    return [turn_y(pair, steps) for steps in (1, 3, 2)]


def swap_all(pieces):
    return [turn(piece, "section", 1) for piece in pieces]


def place_pieces(lines, row_count, places, *refs):
    pieces, outs = refs[:8], refs[8:]
    columns = pieces[0].shape[2]
    for index, piece in enumerate(pieces):
        row = lax.rem(places[0] + 4 - (0, 1, 3, 2)[index % 4], 4)
        half = places[1] if index < 4 else 1 - places[1]
        start = pl.multiple_of(half * columns, 128)
        for column in range(2):
            where = (row * 2 + column, slice(None), pl.ds(start, columns))
            outs[0][where] = piece[column, pl.ds(0, row_count), :]
            if lines:
                outs[1][where] = piece[column, pl.ds(row_count, lines), :]


def put_together(pieces, others, places, lines):
    rows, columns = pieces[0].shape[1:]
    shapes = [jax.ShapeDtypeStruct((8, rows - lines, 2 * columns), low_type)]
    if lines:
        shapes.append(jax.ShapeDtypeStruct((8, lines, 2 * columns), low_type))
    place = jnp.stack([places[1], places[0]]).astype(jnp.int32)
    size = 8 * rows * 2 * columns * 2
    return pl.pallas_call(
        lambda *refs: place_pieces(lines, rows - lines, *refs),
        out_shape=shapes,
        in_specs=[pl.BlockSpec(memory_space=pltpu.SMEM)] + [pl.BlockSpec(memory_space=pltpu.VMEM)] * 8,
        out_specs=[pl.BlockSpec(memory_space=pltpu.VMEM)] * len(shapes),
        compiler_params=pltpu.CompilerParams(vmem_limit_bytes=20 << 20),
        cost_estimate=pl.CostEstimate(flops=0, bytes_accessed=2 * size, transcendentals=0),
    )(place, *pieces, *others)


def attn_weights(pieces, others, places):
    width = 8 * 112
    w_attn, lines = put_together(pieces, others, places, 16)
    lines = lines[:, 0].astype(wide)
    return (
        lines[:, :112].reshape(width),
        lines[:, 128:240].reshape(width),
        jnp.pad(lines[:, 256:328].reshape(576), (0, 64)),
        w_attn.reshape(width, 1024),
    )


def mlp_weights(pieces, others, places):
    return put_together(pieces, others, places, 0)[0].reshape(8 * 112, 2048)


def halves_by_layer(block, section_place):
    columns = block.shape[1] // 2
    kept = lax.dynamic_slice_in_dim(block, section_place * columns, columns, 1)
    sent = lax.dynamic_slice_in_dim(block, (1 - section_place) * columns, columns, 1)
    received = turn(sent, "section", 1)
    first = section_place == 0
    return jnp.where(first, kept, received), jnp.where(first, received, kept)


def rotary_tables(position):
    inverse = rope_base ** (-jnp.arange(0, HD, 2, dtype=wide) / HD)
    angles = position.astype(wide)[..., None] * inverse
    angles = jnp.concatenate([angles, angles], axis=-1)
    return (jnp.cos(angles), jnp.sin(angles))


def rotate(values, cosine, sine):
    half_width = values.shape[-1] // 2
    turned = jnp.concatenate([-values[..., half_width:], values[..., :half_width]], axis=-1)
    return values * cosine + turned * sine


def rotate_back(grads, cosine, sine):
    half_width = grads.shape[-1] // 2
    scaled = grads * sine
    turned = jnp.concatenate([scaled[..., half_width:], -scaled[..., :half_width]], axis=-1)
    return grads * cosine + turned


def norm_backward(grad_normed, resid, scale, gain):
    grad_gain = jnp.sum(grad_normed * resid * scale, axis=0)
    inner = grad_normed * gain
    grad_resid = scale * inner - resid * (scale * scale * scale) * jnp.mean(
        inner * resid, axis=-1, keepdims=True
    )
    return (grad_gain, grad_resid)


def mask_tables(lengths, ctx_place, row_count, ctx_count):
    doc_ends = jnp.cumsum(lengths, axis=-1)
    blocks = (ctx_place - jnp.arange(ctx_count, dtype=jnp.int32)) % ctx_count
    places = (blocks[:, None] * row_count + jnp.arange(row_count, dtype=jnp.int32)).reshape(-1)
    passed = places[:, None] >= doc_ends[None, :]
    segment = jnp.sum(passed.astype(jnp.int32), axis=-1)
    doc_start = jnp.sum(jnp.where(passed, lengths[None, :], 0), axis=-1)
    position = places - doc_start
    cosine, sine = rotary_tables(position[:row_count])
    allowed = (segment[:row_count, None] == segment[None, :]) & (
        places[:row_count, None] >= places[None, :]
    )
    return (allowed, cosine, sine)


def normed(resid, gain):
    scale = lax.rsqrt(jnp.mean(resid * resid, axis=-1, keepdims=True) + epsilon)
    return scale, (resid * scale * gain).astype(low_type)


def forward_attn(layer_in, weights, tables, tie):
    attn_gain, mlp_gain, bias, w_attn = weights
    allowed, cosine, sine = tables
    row_count, width = layer_in.shape
    resid = layer_in.astype(wide)
    scale_one, normed_in = normed(resid, attn_gain)
    projected = jnp.dot(normed_in, w_attn[:, :640], preferred_element_type=wide) + bias
    queries = rotate(
        projected[:, :448].reshape(row_count, 7, HD), cosine[:, None, :], sine[:, None, :]
    ).astype(low_type)
    key_own = rotate(projected[:, 448:512], cosine, sine)
    key_value = jnp.concatenate([key_own, projected[:, 512:576]], axis=1).astype(low_type)
    key_value = tie(stack_rows(key_value, turn_ctx(key_value)))
    key_all, value_all = key_value[:, :HD], key_value[:, HD:]
    scores = jnp.einsum("qgd,td->gqt", queries, key_all, preferred_element_type=wide) * 0.125
    scores = jnp.where(allowed[None], scores, masked_score)
    largest = jnp.max(scores, axis=-1, keepdims=True)
    raised = jnp.exp(scores - largest)
    totals = jnp.sum(raised, axis=-1, keepdims=True)
    log_total = largest + jnp.log(totals)
    probs = (raised / totals).astype(low_type)
    mixed = jnp.einsum("gqt,td->qgd", probs, value_all, preferred_element_type=wide)
    mixed = jnp.pad(mixed.reshape(row_count, 448).astype(low_type), ((0, 0), (64, 0)))
    kept = (resid, scale_one, normed_in, queries, key_all, value_all, log_total, mixed)
    return contract(mixed, w_attn[:, 512:], 1, 1), kept


def forward_mid(branch, resid, mlp_gain):
    middle = resid + tensor_sum(branch)
    return middle, *normed(middle, mlp_gain)


def forward_mlp(normed_mid, w_mlp):
    gate_up = jnp.dot(normed_mid, w_mlp[:, : 2 * UNITS], preferred_element_type=wide)
    hidden = (jax.nn.silu(gate_up[:, :UNITS]) * gate_up[:, UNITS:]).astype(low_type)
    return gate_up, hidden


def forward_down(hidden, w_mlp, row_count):
    branch = contract(hidden, w_mlp[:, 2 * UNITS : 3 * UNITS], 1, 1).astype(low_type)
    return list(branch.reshape(-1, row_count, branch.shape[1]))


def backward_mlp(grad_all, kept, w_mlp):
    middle, scale_two, normed_mid, gate_up, hidden = kept
    row_count, width = middle.shape
    grad_hidden = jnp.dot(grad_all, w_mlp[:, 2 * UNITS : 3 * UNITS], preferred_element_type=wide)
    gate = gate_up[:, :UNITS]
    upward = gate_up[:, UNITS:]
    sigmoid = jax.nn.sigmoid(gate)
    grad_gate = grad_hidden * upward * sigmoid * (1.0 + gate * (1.0 - sigmoid))
    grad_upward = grad_hidden * gate * sigmoid
    grad_gate_up = jnp.concatenate([grad_gate, grad_upward], axis=1).astype(low_type)
    branch = contract(grad_gate_up, w_mlp[:, : 2 * UNITS], 1, 1).astype(low_type)
    branch = branch.reshape(-1, row_count, width)
    grad_mlp = jnp.concatenate(
        [
            contract(normed_mid, grad_gate_up, 0, 0).astype(low_type),
            contract(grad_all, hidden, 0, 0).astype(low_type),
        ],
        axis=1,
    )
    return branch, grad_mlp


def backward_mid(branch, grad_out, kept, mlp_gain):
    middle, scale_two = kept[:2]
    grad_normed_mid = tensor_sum(branch)
    grad_mlp_gain, grad_middle = norm_backward(grad_normed_mid, middle, scale_two, mlp_gain)
    return grad_middle + grad_out.astype(wide), grad_mlp_gain


def backward_attn(grad_middle, kept, weights, tables):
    attn_gain, mlp_gain, bias, w_attn = weights
    allowed, cosine, sine = tables
    resid, scale_one, normed_in, queries, key_all, value_all, log_total, mixed = kept
    row_count, width = resid.shape
    grad_branch = grad_middle.astype(low_type)
    grad_mixed = jnp.dot(grad_branch, w_attn[:, 512:], preferred_element_type=wide)
    grad_mixed = grad_mixed[:, 64:].astype(low_type).reshape(queries.shape)
    scores = jnp.einsum("qgd,td->gqt", queries, key_all, preferred_element_type=wide) * 0.125
    probs = jnp.where(allowed[None], jnp.exp(scores - log_total), 0.0)
    grad_probs = jnp.einsum("qgd,td->gqt", grad_mixed, value_all, preferred_element_type=wide)
    grad_value_all = jnp.einsum(
        "gqt,qgd->td", probs.astype(low_type), grad_mixed, preferred_element_type=wide
    )
    row_delta = jnp.sum(grad_probs * probs, axis=-1, keepdims=True)
    grad_scores = (probs * (grad_probs - row_delta)).astype(low_type)
    grad_queries = (
        jnp.einsum("gqt,td->qgd", grad_scores, key_all, preferred_element_type=wide) * 0.125
    )
    grad_key_all = (
        jnp.einsum("gqt,qgd->td", grad_scores, queries, preferred_element_type=wide) * 0.125
    )
    grad_key_value = jnp.concatenate([grad_key_all, grad_value_all], axis=1).astype(low_type)
    grad_key_value = collect(list(grad_key_value.reshape(-1, row_count, 2 * HD)), "ctx")
    grad_projected = jnp.concatenate(
        [
            rotate_back(grad_queries, cosine[:, None, :], sine[:, None, :]).reshape(row_count, 448),
            rotate_back(grad_key_value[:, :HD], cosine, sine),
            grad_key_value[:, HD:],
            jnp.zeros((row_count, HD), wide),
        ],
        axis=1,
    ).astype(low_type)
    return grad_branch, grad_projected


def backward_in(grad_projected, grad_middle, kept, weights):
    attn_gain, mlp_gain, bias, w_attn = weights
    resid, scale_one = kept[:2]
    grad_normed_in = tensor_sum(contract(grad_projected, w_attn[:, :640], 1, 1))
    grad_attn_gain, grad_resid = norm_backward(grad_normed_in, resid, scale_one, attn_gain)
    return (grad_resid + grad_middle).astype(low_type), grad_attn_gain


def attn_weight_grads(grad_branch, grad_projected, kept):
    normed_in, mixed = kept[2], kept[7]
    grad_bias = jnp.sum(grad_projected.astype(wide), axis=0)
    projection = contract(normed_in, grad_projected, 0, 0)
    output = contract(grad_branch, mixed, 0, 0)
    latter = jnp.pad(projection[:, 512:], ((0, 0), (0, 384))) + output
    return jnp.concatenate([projection[:, :512], latter], axis=1).astype(low_type), grad_bias


def row_blocks(blocks, row_place, axis):
    return [pick(blocks, (row_place + steps) % 4, axis) for steps in (0, 1, 3, 2)]


def send_rows(pieces):
    return [turn_y(piece, steps) for steps, piece in zip((1, 3, 2), pieces)]


def add_all(pieces):
    return sum(piece.astype(wide) for piece in pieces).astype(low_type)


def split_columns(blocks, section_place):
    return pick(blocks, section_place, 1), pick(blocks, 1 - section_place, 1)


def halve(kept, sent):
    return (kept.astype(wide) + turn(sent, "section", 1).astype(wide)).astype(low_type)


def to_column(block):
    hops = []
    for row in range(4):
        hops.append((8 + 2 * row, 8 + 2 * row + 1))
        hops.append((2 * row + 1, 2 * row))
    return lax.ppermute(block, ("section", "fsdp"), hops)


def own_layer(block_zero, block_one, section_place, column_place):
    first = section_place == 0
    hops = []
    for row in range(4):
        hops.append((2 * row, 8 + 2 * row))
        hops.append((8 + 2 * row + 1, 2 * row + 1))
    own = jnp.where(first, block_zero, block_one)
    sent = jnp.where(first, block_one, block_zero)
    received = lax.ppermute(sent, ("section", "fsdp"), hops)
    return jnp.where(section_place == column_place, own, received)


def in_order(pieces, ctx_place):
    own, former, latter, opposite = pieces
    pieces = jnp.stack([own, former, opposite, latter])
    return jnp.stack([pick(pieces, (ctx_place - place) % 4, 0) for place in range(4)])


def pack_lines(small):
    grad_attn_gain, grad_mlp_gain, grad_bias = small
    lines = jnp.concatenate(
        [
            jnp.pad(grad_attn_gain.reshape(8, 112), ((0, 0), (0, 16))),
            jnp.pad(grad_mlp_gain.reshape(8, 112), ((0, 0), (0, 16))),
            jnp.pad(grad_bias[:512].reshape(8, 64), ((0, 0), (0, 64))),
            jnp.pad(grad_bias[512:576].reshape(8, 8), ((0, 0), (0, 632))),
        ],
        axis=1,
    ).astype(low_type)
    return jnp.pad(lines[:, None], ((0, 0), (0, 15), (0, 0))).reshape(4, 2, 16, 1024)


def ctx_blocks(blocks, ctx_place):
    return [
        lax.dynamic_slice_in_dim(blocks, (ctx_place - steps) % 4 * 256, 256, 2)
        for steps in (0, 1, 3, 2)
    ]


def send_ctx(pieces):
    return [turn(piece, "ctx", -steps) for steps, piece in zip((1, 3, 2), pieces)]


def per_device(
    layer_input, cotangent, doc_lengths, attn_gain, w_qkv, b_qkv, w_out, mlp_gain, w_gate_up, w_down
):
    section_place = lax.axis_index("section")
    fsdp_place = lax.axis_index("fsdp")
    row_place, column_place = fsdp_place // 2, fsdp_place % 2
    ctx_place = lax.axis_index("ctx")
    places = (section_place, row_place, column_place, ctx_place)
    row_count, width = layer_input.shape[1:]
    units_all = w_down.shape[1]

    line = jnp.concatenate(
        [
            jnp.pad(attn_gain, ((0, 0), (0, 16))),
            jnp.pad(mlp_gain, ((0, 0), (0, 16))),
            jnp.pad(b_qkv[0], ((0, 0), (0, 696))),
        ],
        axis=1,
    )
    attn_block = jnp.concatenate(
        [
            jnp.concatenate([w_qkv[0, :, 0], w_out[0].T], axis=1),
            jnp.pad(line, ((0, 15), (0, 0))),
        ],
        axis=0,
    )
    past = 4 * UNITS - units_all
    mlp_block = jnp.concatenate(
        [
            jnp.pad(w_gate_up[0], ((0, 0), (0, 0), (0, past))),
            jnp.pad(w_down[0].T, ((0, 0), (0, past)))[:, None],
        ],
        axis=1,
    )
    mlp_block = lax.dynamic_slice_in_dim(mlp_block, ctx_place * UNITS, UNITS, 2)
    mlp_block = jnp.pad(mlp_block.reshape(112, 3 * UNITS), ((0, 0), (0, 128)))

    first = section_place == 0
    layer_in = pick(layer_input, section_place, 0)
    grads_last = pick(cotangent, section_place, 0)
    tables = mask_tables(pick(doc_lengths, section_place, 0)[0], ctx_place, row_count, 4)

    half_attn, late_attn = halves_by_layer(attn_block, section_place)
    half_mlp, late_mlp = halves_by_layer(mlp_block, section_place)
    pair_attn = with_column(half_attn, flip_x(half_attn), column_place)
    pair_attn, half_mlp, grads_last = after(pair_attn, half_mlp, grads_last)
    rows_attn = turn_rows(pair_attn)
    pair_mlp = with_column(half_mlp, flip_x(half_mlp), column_place)
    grads_former = turn(grads_last, "ctx", 1)
    pair_attn, pair_mlp, grads_last, grads_former, *rows_attn = after(
        pair_attn, pair_mlp, grads_last, grads_former, *rows_attn
    )
    moved = [pair_mlp, turn_y(pair_mlp, 1), turn_y(pair_mlp, 3)]
    pieces = [pair_attn] + rows_attn
    weights_zero = attn_weights(pieces, swap_all(pieces), places)

    late = [late_attn, late_mlp]
    grads_moved = [grads_last]

    def tie_zero(key_value):
        key_value, late[0], late[1], grads_moved[0], *moved[:] = after(
            key_value, *late, grads_moved[0], *moved
        )
        grads_moved.extend(turn(grads_moved[0], "ctx", steps) for steps in (3, 2))
        moved.append(turn_y(moved[0], 2))
        late[:] = [with_column(half, flip_x(half), column_place) for half in late]
        return key_value

    branch, kept_attn_zero = forward_attn(layer_in, weights_zero, tables, tie_zero)
    branch, pair_attn, pair_mlp, latter, opposite, *pieces = after(
        branch, *late, *grads_moved[1:], *moved
    )
    grads_all = [grads_former, latter, opposite]
    others = swap_all(pieces)
    middle, scale_two, normed_mid = forward_mid(branch, kept_attn_zero[0], weights_zero[1])
    normed_mid, pair_attn, *pieces = after(normed_mid, pair_attn, *pieces, *others)
    rows_attn = [turn_y(pair_attn, 1), turn_y(pair_attn, 3)]
    w_mlp_zero = mlp_weights(pieces[:4], pieces[4:], places)
    normed_mid = stack_rows(normed_mid, turn_ctx(normed_mid))
    normed_mid, pair_attn, pair_mlp, *rows_attn = after(normed_mid, pair_attn, pair_mlp, *rows_attn)
    rows_attn.append(turn_y(pair_attn, 2))
    gate_up, hidden = forward_mlp(normed_mid, w_mlp_zero)
    kept_mlp_zero = (middle, scale_two, normed_mid, gate_up, hidden)
    branch = collect(forward_down(hidden, w_mlp_zero, row_count), "ctx")
    branch, pair_mlp, *pieces = after(branch, pair_mlp, pair_attn, *rows_attn)
    others = swap_all(pieces)
    former, latter = turn_y(pair_mlp, 1), turn_y(pair_mlp, 3)
    out_zero = (middle + tensor_sum(branch)).astype(low_type)
    out_zero, pair_mlp, former, latter, *rest = after(
        out_zero, pair_mlp, former, latter, *pieces, *others
    )
    moved[:] = [pair_mlp, former, latter, turn_y(pair_mlp, 2)]
    weights_one = attn_weights(rest[:4], rest[4:], places)

    branch, kept_attn_one = forward_attn(out_zero, weights_one, tables, lambda key_value: key_value)
    branch, *pieces = after(branch, *moved)
    others = swap_all(pieces)
    middle, scale_two, normed_mid = forward_mid(branch, kept_attn_one[0], weights_one[1])
    normed_mid, *pieces = after(normed_mid, *pieces, *others)
    w_mlp_one = mlp_weights(pieces[:4], pieces[4:], places)
    grads_all = stack_rows(grads_last, grads_all)
    normed_mid = stack_rows(normed_mid, turn_ctx(normed_mid))
    gate_up, hidden = forward_mlp(normed_mid, w_mlp_one)
    kept_mlp_one = (middle, scale_two, normed_mid, gate_up, hidden)

    mlp_shape = (4, 2, 112, 3 * UNITS)
    attn_shape = (4, 2, 112, 1024)
    branch, mlp_one = backward_mlp(grads_all, kept_mlp_one, w_mlp_one)
    branch = collect(list(branch), "ctx")
    down = forward_down(hidden, w_mlp_one, row_count)
    down = [down[steps] for steps in (0, 1, 3, 2)]
    branch, mlp_keep, mlp_sent, *down = after(
        branch, *split_columns(mlp_one.reshape(mlp_shape), section_place), *down
    )
    down_moved = send_ctx(down[1:])
    mlp_pieces = row_blocks(halve(mlp_keep, mlp_sent), row_place, 0)
    middle_one, gain_one = backward_mid(branch, grads_last, kept_mlp_one, weights_one[1])
    middle_one, *pieces = after(middle_one, down[0], *down_moved, *mlp_pieces)
    down, mlp_pieces = sum(piece.astype(wide) for piece in pieces[:4]), pieces[4:]
    mlp_moved = send_rows(mlp_pieces[1:3])
    branch_one, projected_one = backward_attn(middle_one, kept_attn_one, weights_one, tables)
    grads_one, attn_gain_one = backward_in(projected_one, middle_one, kept_attn_one, weights_one)
    attn_one, bias_one = attn_weight_grads(branch_one, projected_one, kept_attn_one)
    grads_one, *mlp_pieces = after(grads_one, mlp_pieces[0], mlp_pieces[3], *mlp_moved)

    mlp_pieces[1] = turn_y(mlp_pieces[1], 2)
    attn_sums = halve(*split_columns(attn_one.reshape(attn_shape), section_place))
    grads_all = stack_rows(grads_one, turn_ctx(grads_one))
    grads_all, attn_sums, down, attn_gain_one, bias_one, *mlp_pieces = after(
        grads_all, attn_sums, down, attn_gain_one, bias_one, *mlp_pieces
    )
    lines_one = pack_lines((attn_gain_one, gain_one, bias_one))
    line_sums = halve(*split_columns(lines_one, section_place))
    mlp_one = add_all(mlp_pieces)
    mlp_one = add_all([mlp_one, to_column(mlp_one)])
    out_one = (kept_mlp_one[0] + tensor_sum(down)).astype(low_type)
    branch, mlp_zero = backward_mlp(grads_all, kept_mlp_zero, w_mlp_zero)
    branch = collect(list(branch), "ctx")
    branch, mlp_keep, mlp_sent, mlp_one, out_one, *attn_pieces = after(
        branch,
        *split_columns(mlp_zero.reshape(mlp_shape), section_place),
        mlp_one,
        out_one,
        *ctx_blocks(jnp.concatenate([attn_sums, line_sums], axis=1), ctx_place),
    )
    mlp_pieces = row_blocks(halve(mlp_keep, mlp_sent), row_place, 0)
    attn_moved = send_ctx(attn_pieces[1:])
    middle_zero, gain_zero = backward_mid(branch, grads_one, kept_mlp_zero, weights_zero[1])
    middle_zero, *pieces = after(middle_zero, attn_pieces[0], *attn_moved, *mlp_pieces)
    attn_one, mlp_pieces = add_all(pieces[:4]), pieces[4:]
    mlp_moved = send_rows(mlp_pieces[1:3])
    branch_zero, projected_zero = backward_attn(middle_zero, kept_attn_zero, weights_zero, tables)
    projected_zero, *pieces = after(projected_zero, mlp_pieces[0], mlp_pieces[3], *mlp_moved)
    mlp_pieces = [pieces[0], pieces[2], pieces[3], turn_y(pieces[1], 2)]
    attn_zero, bias_zero = attn_weight_grads(branch_zero, projected_zero, kept_attn_zero)
    attn_sums = halve(*split_columns(attn_zero.reshape(attn_shape), section_place))
    attn_pieces = ctx_blocks(attn_sums, ctx_place)
    attn_moved = send_ctx(attn_pieces[1:])
    grads_zero, attn_gain_zero = backward_in(
        projected_zero, middle_zero, kept_attn_zero, weights_zero
    )
    attn_gain_zero, *mlp_pieces = after(attn_gain_zero, *mlp_pieces)

    mlp_zero = add_all(mlp_pieces)
    mlp_moved = to_column(mlp_zero)
    lines_zero = pack_lines((attn_gain_zero, gain_zero, bias_zero))
    line_pieces = ctx_blocks(halve(*split_columns(lines_zero, section_place)), ctx_place)
    line_moved = send_ctx(line_pieces[1:])
    attn_zero = jnp.concatenate(
        [add_all([attn_pieces[0]] + attn_moved), add_all([line_pieces[0]] + line_moved)], axis=1
    )
    attn_zero, mlp_zero, mlp_moved = after(attn_zero, mlp_zero, mlp_moved)
    mlp_zero = add_all([mlp_zero, mlp_moved])
    mlp = own_layer(mlp_zero, mlp_one, section_place, column_place)
    attn_pieces = row_blocks(jnp.stack([attn_zero, attn_one]), row_place, 1)
    mlp, *attn_pieces = after(mlp, *attn_pieces)
    mlp_all = turn_ctx(mlp)
    attn_both = add_all(attn_pieces[:1] + send_rows(attn_pieces[1:]))
    attn_both = add_all([attn_both, to_column(attn_both)])
    attn = own_layer(attn_both[0], attn_both[1], section_place, column_place)
    attn, mlp, *mlp_all = after(attn, mlp, *mlp_all)
    attn_all = turn_ctx(attn)
    mlp = in_order([mlp] + mlp_all, ctx_place).reshape(4, 112, 3, UNITS)
    gate_up = mlp[:, :, :2].transpose(1, 2, 0, 3).reshape(112, 2, 4 * UNITS)[:, :, :units_all]
    down = mlp[:, :, 2].transpose(0, 2, 1).reshape(4 * UNITS, 112)[:units_all]
    attn = in_order([attn] + attn_all, ctx_place)
    outputs = [out_zero, out_one]

    def by_layer(values):
        own = jnp.where(first, values[0], values[1])
        other = turn(jnp.where(first, values[1], values[0]), "section", 1)
        return jnp.where(first, jnp.stack([own, other]), jnp.stack([other, own]))[None]

    hidden_states = by_layer(outputs)
    input_grads = by_layer([grads_zero, grads_one])
    attn = attn.transpose(1, 0, 2).reshape(128, 1024).astype(wide)
    lines = attn[112:113]
    return (
        hidden_states,
        input_grads,
        lines[:, :112],
        attn[None, :112, None, :576],
        lines[None, :, 256:320],
        lines[None, :, 384:392],
        attn[:112, 576:].T[None],
        lines[:, 128:240],
        gate_up.astype(wide)[None],
        down.astype(wide)[None],
    )


def solution(mesh):
    return jax.shard_map(
        per_device,
        mesh=mesh,
        in_specs=(
            P(None, ("fsdp", "ctx"), None),
            P(None, ("fsdp", "ctx"), None),
            P(None, "fsdp", None),
            P("section", "fsdp"),
            P("section", "fsdp", "tp", None),
            P("section", "tp", "fsdp"),
            P("section", "tp", "fsdp"),
            P("section", "fsdp"),
            P("section", "fsdp", None, "tp"),
            P("section", "tp", "fsdp"),
        ),
        out_specs=(
            P("section", None, ("fsdp", "ctx"), None),
            P("section", None, ("fsdp", "ctx"), None),
            P("section", "fsdp"),
            P("section", "fsdp", "tp", None),
            P("section", "tp", "fsdp"),
            P("section", "tp", "fsdp"),
            P("section", "tp", "fsdp"),
            P("section", "fsdp"),
            P("section", "fsdp", None, "tp"),
            P("section", "tp", "fsdp"),
        ),
        check_vma=False,
    )
```

```python
import jax
import jax.numpy as jnp
from jax import lax
from jax.experimental import pallas as pl
from jax.experimental.pallas import tpu as pltpu
from jax.sharding import PartitionSpec as P

HD = 64
UNITS = 640

epsilon = 1e-06
rope_base = 1000000.0
masked_score = -1000000000.0
low_type = jnp.bfloat16
wide = jnp.float32


def contract(left, right, left_dim, right_dim):
    return lax.dot_general(
        left, right, (((left_dim,), (right_dim,)), ((), ())), preferred_element_type=wide
    )


def turn(value, axis, steps):
    count = lax.axis_size(axis)
    return lax.ppermute(value, axis, [(place, (place + steps) % count) for place in range(count)])


def turn_y(value, steps):
    count = lax.axis_size("fsdp")
    return lax.ppermute(
        value, "fsdp", [(place, (place + 2 * steps) % count) for place in range(count)]
    )


def flip_x(value):
    count = lax.axis_size("fsdp")
    return lax.ppermute(value, "fsdp", [(place, place ^ 1) for place in range(count)])


def collect(blocks, axis):
    count = lax.axis_size(axis)
    order = [1, count - 1] + list(range(2, count - 1))
    total = blocks[0].astype(wide)
    for steps in order:
        total = total + turn(blocks[steps], axis, -steps).astype(wide)
    return total


def pick(array, place, axis):
    return lax.dynamic_index_in_dim(array, place, axis, keepdims=False)


def turn_ctx(block):
    return [turn(block, "ctx", steps) for steps in (1, 3, 2)]


def stack_rows(own, moved):
    former, latter, opposite = moved
    return jnp.concatenate([own, former, opposite, latter], axis=0)


def tensor_sum(partial_value):
    own = lax.optimization_barrier(partial_value.astype(low_type))
    return own.astype(wide) + turn(own, "tp", 1).astype(wide)


def after(value, *others):
    tied = lax.optimization_barrier((value,) + others)
    return tied[0] if not others else tied


def with_column(half, received, column_place):
    pair = jnp.zeros((2,) + half.shape, half.dtype)
    pair = lax.dynamic_update_slice(pair, half[None], (column_place, 0, 0))
    return lax.dynamic_update_slice(pair, received[None], (1 - column_place, 0, 0))


def turn_rows(pair):
    return [turn_y(pair, steps) for steps in (1, 3, 2)]


def swap_all(pieces):
    return [turn(piece, "section", 1) for piece in pieces]


def place_pieces(lines, row_count, places, *refs):
    pieces, outs = refs[:8], refs[8:]
    columns = pieces[0].shape[2]
    for index, piece in enumerate(pieces):
        row = lax.rem(places[0] + 4 - (0, 1, 3, 2)[index % 4], 4)
        half = places[1] if index < 4 else 1 - places[1]
        start = pl.multiple_of(half * columns, 128)
        for column in range(2):
            where = (row * 2 + column, slice(None), pl.ds(start, columns))
            outs[0][where] = piece[column, pl.ds(0, row_count), :]
            if lines:
                outs[1][where] = piece[column, pl.ds(row_count, lines), :]


def put_together(pieces, others, places, lines):
    rows, columns = pieces[0].shape[1:]
    shapes = [jax.ShapeDtypeStruct((8, rows - lines, 2 * columns), low_type)]
    if lines:
        shapes.append(jax.ShapeDtypeStruct((8, lines, 2 * columns), low_type))
    place = jnp.stack([places[1], places[0]]).astype(jnp.int32)
    size = 8 * rows * 2 * columns * 2
    return pl.pallas_call(
        lambda *refs: place_pieces(lines, rows - lines, *refs),
        out_shape=shapes,
        in_specs=[pl.BlockSpec(memory_space=pltpu.SMEM)] + [pl.BlockSpec(memory_space=pltpu.VMEM)] * 8,
        out_specs=[pl.BlockSpec(memory_space=pltpu.VMEM)] * len(shapes),
        compiler_params=pltpu.CompilerParams(vmem_limit_bytes=20 << 20),
        cost_estimate=pl.CostEstimate(flops=0, bytes_accessed=2 * size, transcendentals=0),
    )(place, *pieces, *others)


def attn_weights(pieces, others, places):
    width = 8 * 112
    w_attn, lines = put_together(pieces, others, places, 16)
    lines = lines[:, 0].astype(wide)
    return (
        lines[:, :112].reshape(width),
        lines[:, 128:240].reshape(width),
        jnp.pad(lines[:, 256:328].reshape(576), (0, 64)),
        w_attn.reshape(width, 1024),
    )


def mlp_weights(pieces, others, places):
    return put_together(pieces, others, places, 0)[0].reshape(8 * 112, 2048)


def halves_by_layer(block, section_place):
    columns = block.shape[1] // 2
    kept = lax.dynamic_slice_in_dim(block, section_place * columns, columns, 1)
    sent = lax.dynamic_slice_in_dim(block, (1 - section_place) * columns, columns, 1)
    received = turn(sent, "section", 1)
    first = section_place == 0
    return jnp.where(first, kept, received), jnp.where(first, received, kept)


def rotary_tables(position):
    inverse = rope_base ** (-jnp.arange(0, HD, 2, dtype=wide) / HD)
    angles = position.astype(wide)[..., None] * inverse
    angles = jnp.concatenate([angles, angles], axis=-1)
    return (jnp.cos(angles), jnp.sin(angles))


def rotate(values, cosine, sine):
    half_width = values.shape[-1] // 2
    turned = jnp.concatenate([-values[..., half_width:], values[..., :half_width]], axis=-1)
    return values * cosine + turned * sine


def rotate_back(grads, cosine, sine):
    half_width = grads.shape[-1] // 2
    scaled = grads * sine
    turned = jnp.concatenate([scaled[..., half_width:], -scaled[..., :half_width]], axis=-1)
    return grads * cosine + turned


def norm_backward(grad_normed, resid, scale, gain):
    grad_gain = jnp.sum(grad_normed * resid * scale, axis=0)
    inner = grad_normed * gain
    grad_resid = scale * inner - resid * (scale * scale * scale) * jnp.mean(
        inner * resid, axis=-1, keepdims=True
    )
    return (grad_gain, grad_resid)


def mask_tables(lengths, ctx_place, row_count, ctx_count):
    doc_ends = jnp.cumsum(lengths, axis=-1)
    blocks = (ctx_place - jnp.arange(ctx_count, dtype=jnp.int32)) % ctx_count
    places = (blocks[:, None] * row_count + jnp.arange(row_count, dtype=jnp.int32)).reshape(-1)
    passed = places[:, None] >= doc_ends[None, :]
    segment = jnp.sum(passed.astype(jnp.int32), axis=-1)
    doc_start = jnp.sum(jnp.where(passed, lengths[None, :], 0), axis=-1)
    position = places - doc_start
    cosine, sine = rotary_tables(position[:row_count])
    allowed = (segment[:row_count, None] == segment[None, :]) & (
        places[:row_count, None] >= places[None, :]
    )
    return (allowed, cosine, sine)


def normed(resid, gain):
    scale = lax.rsqrt(jnp.mean(resid * resid, axis=-1, keepdims=True) + epsilon)
    return scale, (resid * scale * gain).astype(low_type)


def forward_attn(layer_in, weights, tables, tie):
    attn_gain, mlp_gain, bias, w_attn = weights
    allowed, cosine, sine = tables
    row_count, width = layer_in.shape
    resid = layer_in.astype(wide)
    scale_one, normed_in = normed(resid, attn_gain)
    projected = jnp.dot(normed_in, w_attn[:, :640], preferred_element_type=wide) + bias
    queries = rotate(
        projected[:, :448].reshape(row_count, 7, HD), cosine[:, None, :], sine[:, None, :]
    ).astype(low_type)
    key_own = rotate(projected[:, 448:512], cosine, sine)
    key_value = jnp.concatenate([key_own, projected[:, 512:576]], axis=1).astype(low_type)
    key_value = tie(stack_rows(key_value, turn_ctx(key_value)))
    key_all, value_all = key_value[:, :HD], key_value[:, HD:]
    scores = jnp.einsum("qgd,td->gqt", queries, key_all, preferred_element_type=wide) * 0.125
    scores = jnp.where(allowed[None], scores, masked_score)
    largest = jnp.max(scores, axis=-1, keepdims=True)
    raised = jnp.exp(scores - largest)
    totals = jnp.sum(raised, axis=-1, keepdims=True)
    log_total = largest + jnp.log(totals)
    probs = (raised / totals).astype(low_type)
    mixed = jnp.einsum("gqt,td->qgd", probs, value_all, preferred_element_type=wide)
    mixed = jnp.pad(mixed.reshape(row_count, 448).astype(low_type), ((0, 0), (64, 0)))
    kept = (resid, scale_one, normed_in, queries, key_all, value_all, log_total, mixed)
    return contract(mixed, w_attn[:, 512:], 1, 1), kept


def forward_mid(branch, resid, mlp_gain):
    middle = resid + tensor_sum(branch)
    return middle, *normed(middle, mlp_gain)


def forward_mlp(normed_mid, w_mlp):
    gate_up = jnp.dot(normed_mid, w_mlp[:, : 2 * UNITS], preferred_element_type=wide)
    hidden = (jax.nn.silu(gate_up[:, :UNITS]) * gate_up[:, UNITS:]).astype(low_type)
    return gate_up, hidden


def forward_down(hidden, w_mlp, row_count):
    branch = contract(hidden, w_mlp[:, 2 * UNITS : 3 * UNITS], 1, 1).astype(low_type)
    return list(branch.reshape(-1, row_count, branch.shape[1]))


def backward_mlp(grad_all, kept, w_mlp):
    middle, scale_two, normed_mid, gate_up, hidden = kept
    row_count, width = middle.shape
    grad_hidden = jnp.dot(grad_all, w_mlp[:, 2 * UNITS : 3 * UNITS], preferred_element_type=wide)
    gate = gate_up[:, :UNITS]
    upward = gate_up[:, UNITS:]
    sigmoid = jax.nn.sigmoid(gate)
    grad_gate = grad_hidden * upward * sigmoid * (1.0 + gate * (1.0 - sigmoid))
    grad_upward = grad_hidden * gate * sigmoid
    grad_gate_up = jnp.concatenate([grad_gate, grad_upward], axis=1).astype(low_type)
    branch = contract(grad_gate_up, w_mlp[:, : 2 * UNITS], 1, 1).astype(low_type)
    branch = branch.reshape(-1, row_count, width)
    grad_mlp = jnp.concatenate(
        [
            contract(normed_mid, grad_gate_up, 0, 0).astype(low_type),
            contract(grad_all, hidden, 0, 0).astype(low_type),
        ],
        axis=1,
    )
    return branch, grad_mlp


def backward_mid(branch, grad_out, kept, mlp_gain):
    middle, scale_two = kept[:2]
    grad_normed_mid = tensor_sum(branch)
    grad_mlp_gain, grad_middle = norm_backward(grad_normed_mid, middle, scale_two, mlp_gain)
    return grad_middle + grad_out.astype(wide), grad_mlp_gain


def backward_attn(grad_middle, kept, weights, tables):
    attn_gain, mlp_gain, bias, w_attn = weights
    allowed, cosine, sine = tables
    resid, scale_one, normed_in, queries, key_all, value_all, log_total, mixed = kept
    row_count, width = resid.shape
    grad_branch = grad_middle.astype(low_type)
    grad_mixed = jnp.dot(grad_branch, w_attn[:, 512:], preferred_element_type=wide)
    grad_mixed = grad_mixed[:, 64:].astype(low_type).reshape(queries.shape)
    scores = jnp.einsum("qgd,td->gqt", queries, key_all, preferred_element_type=wide) * 0.125
    probs = jnp.where(allowed[None], jnp.exp(scores - log_total), 0.0)
    grad_probs = jnp.einsum("qgd,td->gqt", grad_mixed, value_all, preferred_element_type=wide)
    grad_value_all = jnp.einsum(
        "gqt,qgd->td", probs.astype(low_type), grad_mixed, preferred_element_type=wide
    )
    row_delta = jnp.sum(grad_probs * probs, axis=-1, keepdims=True)
    grad_scores = (probs * (grad_probs - row_delta)).astype(low_type)
    grad_queries = (
        jnp.einsum("gqt,td->qgd", grad_scores, key_all, preferred_element_type=wide) * 0.125
    )
    grad_key_all = (
        jnp.einsum("gqt,qgd->td", grad_scores, queries, preferred_element_type=wide) * 0.125
    )
    grad_key_value = jnp.concatenate([grad_key_all, grad_value_all], axis=1).astype(low_type)
    grad_key_value = collect(list(grad_key_value.reshape(-1, row_count, 2 * HD)), "ctx")
    grad_projected = jnp.concatenate(
        [
            rotate_back(grad_queries, cosine[:, None, :], sine[:, None, :]).reshape(row_count, 448),
            rotate_back(grad_key_value[:, :HD], cosine, sine),
            grad_key_value[:, HD:],
            jnp.zeros((row_count, HD), wide),
        ],
        axis=1,
    ).astype(low_type)
    return grad_branch, grad_projected


def backward_in(grad_projected, grad_middle, kept, weights):
    attn_gain, mlp_gain, bias, w_attn = weights
    resid, scale_one = kept[:2]
    grad_normed_in = tensor_sum(contract(grad_projected, w_attn[:, :640], 1, 1))
    grad_attn_gain, grad_resid = norm_backward(grad_normed_in, resid, scale_one, attn_gain)
    return (grad_resid + grad_middle).astype(low_type), grad_attn_gain


def attn_weight_grads(grad_branch, grad_projected, kept):
    normed_in, mixed = kept[2], kept[7]
    grad_bias = jnp.sum(grad_projected.astype(wide), axis=0)
    projection = contract(normed_in, grad_projected, 0, 0)
    output = contract(grad_branch, mixed, 0, 0)
    latter = jnp.pad(projection[:, 512:], ((0, 0), (0, 384))) + output
    return jnp.concatenate([projection[:, :512], latter], axis=1).astype(low_type), grad_bias


def row_blocks(blocks, row_place, axis):
    return [pick(blocks, (row_place + steps) % 4, axis) for steps in (0, 1, 3, 2)]


def send_rows(pieces):
    return [turn_y(piece, steps) for steps, piece in zip((1, 3, 2), pieces)]


def add_all(pieces):
    return sum(piece.astype(wide) for piece in pieces).astype(low_type)


def split_columns(blocks, section_place):
    return pick(blocks, section_place, 1), pick(blocks, 1 - section_place, 1)


def halve(kept, sent):
    return (kept.astype(wide) + turn(sent, "section", 1).astype(wide)).astype(low_type)


def to_column(block):
    hops = []
    for row in range(4):
        hops.append((8 + 2 * row, 8 + 2 * row + 1))
        hops.append((2 * row + 1, 2 * row))
    return lax.ppermute(block, ("section", "fsdp"), hops)


def own_layer(block_zero, block_one, section_place, column_place):
    first = section_place == 0
    hops = []
    for row in range(4):
        hops.append((2 * row, 8 + 2 * row))
        hops.append((8 + 2 * row + 1, 2 * row + 1))
    own = jnp.where(first, block_zero, block_one)
    sent = jnp.where(first, block_one, block_zero)
    received = lax.ppermute(sent, ("section", "fsdp"), hops)
    return jnp.where(section_place == column_place, own, received)


def in_order(pieces, ctx_place):
    own, former, latter, opposite = pieces
    pieces = jnp.stack([own, former, opposite, latter])
    return jnp.stack([pick(pieces, (ctx_place - place) % 4, 0) for place in range(4)])


def pack_lines(small):
    grad_attn_gain, grad_mlp_gain, grad_bias = small
    lines = jnp.concatenate(
        [
            jnp.pad(grad_attn_gain.reshape(8, 112), ((0, 0), (0, 16))),
            jnp.pad(grad_mlp_gain.reshape(8, 112), ((0, 0), (0, 16))),
            jnp.pad(grad_bias[:512].reshape(8, 64), ((0, 0), (0, 64))),
            jnp.pad(grad_bias[512:576].reshape(8, 8), ((0, 0), (0, 632))),
        ],
        axis=1,
    ).astype(low_type)
    return jnp.pad(lines[:, None], ((0, 0), (0, 15), (0, 0))).reshape(4, 2, 16, 1024)


def ctx_blocks(blocks, ctx_place):
    return [
        lax.dynamic_slice_in_dim(blocks, (ctx_place - steps) % 4 * 256, 256, 2)
        for steps in (0, 1, 3, 2)
    ]


def send_ctx(pieces):
    return [turn(piece, "ctx", -steps) for steps, piece in zip((1, 3, 2), pieces)]


def per_device(
    layer_input, cotangent, doc_lengths, attn_gain, w_qkv, b_qkv, w_out, mlp_gain, w_gate_up, w_down
):
    section_place = lax.axis_index("section")
    fsdp_place = lax.axis_index("fsdp")
    row_place, column_place = fsdp_place // 2, fsdp_place % 2
    ctx_place = lax.axis_index("ctx")
    places = (section_place, row_place, column_place, ctx_place)
    row_count, width = layer_input.shape[1:]
    units_all = w_down.shape[1]

    line = jnp.concatenate(
        [
            jnp.pad(attn_gain, ((0, 0), (0, 16))),
            jnp.pad(mlp_gain, ((0, 0), (0, 16))),
            jnp.pad(b_qkv[0], ((0, 0), (0, 696))),
        ],
        axis=1,
    )
    attn_block = jnp.concatenate(
        [
            jnp.concatenate([w_qkv[0, :, 0], w_out[0].T], axis=1),
            jnp.pad(line, ((0, 15), (0, 0))),
        ],
        axis=0,
    )
    past = 4 * UNITS - units_all
    mlp_block = jnp.concatenate(
        [
            jnp.pad(w_gate_up[0], ((0, 0), (0, 0), (0, past))),
            jnp.pad(w_down[0].T, ((0, 0), (0, past)))[:, None],
        ],
        axis=1,
    )
    mlp_block = lax.dynamic_slice_in_dim(mlp_block, ctx_place * UNITS, UNITS, 2)
    mlp_block = jnp.pad(mlp_block.reshape(112, 3 * UNITS), ((0, 0), (0, 128)))

    first = section_place == 0
    layer_in = pick(layer_input, section_place, 0)
    grads_last = pick(cotangent, section_place, 0)
    tables = mask_tables(pick(doc_lengths, section_place, 0)[0], ctx_place, row_count, 4)

    half_attn, late_attn = halves_by_layer(attn_block, section_place)
    half_mlp, late_mlp = halves_by_layer(mlp_block, section_place)
    pair_attn = with_column(half_attn, flip_x(half_attn), column_place)
    pair_attn, half_mlp, grads_last = after(pair_attn, half_mlp, grads_last)
    rows_attn = turn_rows(pair_attn)
    pair_mlp = with_column(half_mlp, flip_x(half_mlp), column_place)
    grads_former = turn(grads_last, "ctx", 1)
    pair_attn, pair_mlp, grads_last, grads_former, *rows_attn = after(
        pair_attn, pair_mlp, grads_last, grads_former, *rows_attn
    )
    moved = [pair_mlp, turn_y(pair_mlp, 1), turn_y(pair_mlp, 3)]
    pieces = [pair_attn] + rows_attn
    weights_zero = attn_weights(pieces, swap_all(pieces), places)

    late = [late_attn, late_mlp]
    grads_moved = [grads_last]

    def tie_zero(key_value):
        key_value, late[0], late[1], grads_moved[0], *moved[:] = after(
            key_value, *late, grads_moved[0], *moved
        )
        grads_moved.extend(turn(grads_moved[0], "ctx", steps) for steps in (3, 2))
        moved.append(turn_y(moved[0], 2))
        late[:] = [with_column(half, flip_x(half), column_place) for half in late]
        return key_value

    branch, kept_attn_zero = forward_attn(layer_in, weights_zero, tables, tie_zero)
    branch, pair_attn, pair_mlp, latter, opposite, *pieces = after(
        branch, *late, *grads_moved[1:], *moved
    )
    grads_all = [grads_former, latter, opposite]
    others = swap_all(pieces)
    middle, scale_two, normed_mid = forward_mid(branch, kept_attn_zero[0], weights_zero[1])
    normed_mid, pair_attn, *pieces = after(normed_mid, pair_attn, *pieces, *others)
    rows_attn = [turn_y(pair_attn, 1), turn_y(pair_attn, 3)]
    w_mlp_zero = mlp_weights(pieces[:4], pieces[4:], places)
    normed_mid = stack_rows(normed_mid, turn_ctx(normed_mid))
    normed_mid, pair_attn, pair_mlp, *rows_attn = after(normed_mid, pair_attn, pair_mlp, *rows_attn)
    rows_attn.append(turn_y(pair_attn, 2))
    gate_up, hidden = forward_mlp(normed_mid, w_mlp_zero)
    kept_mlp_zero = (middle, scale_two, normed_mid, gate_up, hidden)
    branch = collect(forward_down(hidden, w_mlp_zero, row_count), "ctx")
    branch, pair_mlp, *pieces = after(branch, pair_mlp, pair_attn, *rows_attn)
    others = swap_all(pieces)
    former, latter = turn_y(pair_mlp, 1), turn_y(pair_mlp, 3)
    out_zero = (middle + tensor_sum(branch)).astype(low_type)
    out_zero, pair_mlp, former, latter, *rest = after(
        out_zero, pair_mlp, former, latter, *pieces, *others
    )
    moved[:] = [pair_mlp, former, latter, turn_y(pair_mlp, 2)]
    weights_one = attn_weights(rest[:4], rest[4:], places)

    branch, kept_attn_one = forward_attn(out_zero, weights_one, tables, lambda key_value: key_value)
    branch, *pieces = after(branch, *moved)
    others = swap_all(pieces)
    middle, scale_two, normed_mid = forward_mid(branch, kept_attn_one[0], weights_one[1])
    normed_mid, *pieces = after(normed_mid, *pieces, *others)
    w_mlp_one = mlp_weights(pieces[:4], pieces[4:], places)
    grads_all = stack_rows(grads_last, grads_all)
    normed_mid = stack_rows(normed_mid, turn_ctx(normed_mid))
    gate_up, hidden = forward_mlp(normed_mid, w_mlp_one)
    kept_mlp_one = (middle, scale_two, normed_mid, gate_up, hidden)

    mlp_shape = (4, 2, 112, 3 * UNITS)
    attn_shape = (4, 2, 112, 1024)
    branch, mlp_one = backward_mlp(grads_all, kept_mlp_one, w_mlp_one)
    branch = collect(list(branch), "ctx")
    down = forward_down(hidden, w_mlp_one, row_count)
    down = [down[steps] for steps in (0, 1, 3, 2)]
    branch, mlp_keep, mlp_sent, *down = after(
        branch, *split_columns(mlp_one.reshape(mlp_shape), section_place), *down
    )
    down_moved = send_ctx(down[1:])
    mlp_pieces = row_blocks(halve(mlp_keep, mlp_sent), row_place, 0)
    middle_one, gain_one = backward_mid(branch, grads_last, kept_mlp_one, weights_one[1])
    middle_one, *pieces = after(middle_one, down[0], *down_moved, *mlp_pieces)
    down, mlp_pieces = sum(piece.astype(wide) for piece in pieces[:4]), pieces[4:]
    mlp_moved = send_rows(mlp_pieces[1:3])
    branch_one, projected_one = backward_attn(middle_one, kept_attn_one, weights_one, tables)
    grads_one, attn_gain_one = backward_in(projected_one, middle_one, kept_attn_one, weights_one)
    attn_one, bias_one = attn_weight_grads(branch_one, projected_one, kept_attn_one)
    grads_one, *mlp_pieces = after(grads_one, mlp_pieces[0], mlp_pieces[3], *mlp_moved)

    mlp_pieces[1] = turn_y(mlp_pieces[1], 2)
    attn_sums = halve(*split_columns(attn_one.reshape(attn_shape), section_place))
    grads_all = stack_rows(grads_one, turn_ctx(grads_one))
    grads_all, attn_sums, down, attn_gain_one, bias_one, *mlp_pieces = after(
        grads_all, attn_sums, down, attn_gain_one, bias_one, *mlp_pieces
    )
    lines_one = pack_lines((attn_gain_one, gain_one, bias_one))
    line_sums = halve(*split_columns(lines_one, section_place))
    mlp_one = add_all(mlp_pieces)
    mlp_one = add_all([mlp_one, to_column(mlp_one)])
    out_one = (kept_mlp_one[0] + tensor_sum(down)).astype(low_type)
    branch, mlp_zero = backward_mlp(grads_all, kept_mlp_zero, w_mlp_zero)
    branch = collect(list(branch), "ctx")
    branch, mlp_keep, mlp_sent, mlp_one, out_one, *attn_pieces = after(
        branch,
        *split_columns(mlp_zero.reshape(mlp_shape), section_place),
        mlp_one,
        out_one,
        *ctx_blocks(jnp.concatenate([attn_sums, line_sums], axis=1), ctx_place),
    )
    mlp_pieces = row_blocks(halve(mlp_keep, mlp_sent), row_place, 0)
    attn_moved = send_ctx(attn_pieces[1:])
    middle_zero, gain_zero = backward_mid(branch, grads_one, kept_mlp_zero, weights_zero[1])
    middle_zero, *pieces = after(middle_zero, attn_pieces[0], *attn_moved, *mlp_pieces)
    attn_one, mlp_pieces = add_all(pieces[:4]), pieces[4:]
    mlp_moved = send_rows(mlp_pieces[1:3])
    branch_zero, projected_zero = backward_attn(middle_zero, kept_attn_zero, weights_zero, tables)
    projected_zero, *pieces = after(projected_zero, mlp_pieces[0], mlp_pieces[3], *mlp_moved)
    mlp_pieces = [pieces[0], pieces[2], pieces[3], turn_y(pieces[1], 2)]
    attn_zero, bias_zero = attn_weight_grads(branch_zero, projected_zero, kept_attn_zero)
    attn_sums = halve(*split_columns(attn_zero.reshape(attn_shape), section_place))
    attn_pieces = ctx_blocks(attn_sums, ctx_place)
    attn_moved = send_ctx(attn_pieces[1:])
    grads_zero, attn_gain_zero = backward_in(
        projected_zero, middle_zero, kept_attn_zero, weights_zero
    )
    attn_gain_zero, *mlp_pieces = after(attn_gain_zero, *mlp_pieces)

    mlp_zero = add_all(mlp_pieces)
    mlp_moved = to_column(mlp_zero)
    lines_zero = pack_lines((attn_gain_zero, gain_zero, bias_zero))
    line_pieces = ctx_blocks(halve(*split_columns(lines_zero, section_place)), ctx_place)
    line_moved = send_ctx(line_pieces[1:])
    attn_zero = jnp.concatenate(
        [add_all([attn_pieces[0]] + attn_moved), add_all([line_pieces[0]] + line_moved)], axis=1
    )
    attn_zero, mlp_zero, mlp_moved = after(attn_zero, mlp_zero, mlp_moved)
    mlp_zero = add_all([mlp_zero, mlp_moved])
    mlp = own_layer(mlp_zero, mlp_one, section_place, column_place)
    attn_pieces = row_blocks(jnp.stack([attn_zero, attn_one]), row_place, 1)
    mlp, *attn_pieces = after(mlp, *attn_pieces)
    mlp_all = [turn(mlp, "ctx", 1), turn(mlp, "ctx", 3)]
    attn_both = add_all(attn_pieces[:1] + send_rows(attn_pieces[1:]))
    attn_both, mlp, *mlp_all = after(attn_both, mlp, *mlp_all)
    mlp_all.append(turn(mlp, "ctx", 2))
    attn_both = add_all([attn_both, to_column(attn_both)])
    attn = own_layer(attn_both[0], attn_both[1], section_place, column_place)
    attn, mlp, *mlp_all = after(attn, mlp, *mlp_all)
    attn_all = turn_ctx(attn)
    mlp = in_order([mlp] + mlp_all, ctx_place).reshape(4, 112, 3, UNITS)
    gate_up = mlp[:, :, :2].transpose(1, 2, 0, 3).reshape(112, 2, 4 * UNITS)[:, :, :units_all]
    down = mlp[:, :, 2].transpose(0, 2, 1).reshape(4 * UNITS, 112)[:units_all]
    attn = in_order([attn] + attn_all, ctx_place)
    outputs = [out_zero, out_one]

    def by_layer(values):
        own = jnp.where(first, values[0], values[1])
        other = turn(jnp.where(first, values[1], values[0]), "section", 1)
        return jnp.where(first, jnp.stack([own, other]), jnp.stack([other, own]))[None]

    hidden_states = by_layer(outputs)
    input_grads = by_layer([grads_zero, grads_one])
    attn = attn.transpose(1, 0, 2).reshape(128, 1024).astype(wide)
    lines = attn[112:113]
    return (
        hidden_states,
        input_grads,
        lines[:, :112],
        attn[None, :112, None, :576],
        lines[None, :, 256:320],
        lines[None, :, 384:392],
        attn[:112, 576:].T[None],
        lines[:, 128:240],
        gate_up.astype(wide)[None],
        down.astype(wide)[None],
    )


def solution(mesh):
    return jax.shard_map(
        per_device,
        mesh=mesh,
        in_specs=(
            P(None, ("fsdp", "ctx"), None),
            P(None, ("fsdp", "ctx"), None),
            P(None, "fsdp", None),
            P("section", "fsdp"),
            P("section", "fsdp", "tp", None),
            P("section", "tp", "fsdp"),
            P("section", "tp", "fsdp"),
            P("section", "fsdp"),
            P("section", "fsdp", None, "tp"),
            P("section", "tp", "fsdp"),
        ),
        out_specs=(
            P("section", None, ("fsdp", "ctx"), None),
            P("section", None, ("fsdp", "ctx"), None),
            P("section", "fsdp"),
            P("section", "fsdp", "tp", None),
            P("section", "tp", "fsdp"),
            P("section", "tp", "fsdp"),
            P("section", "tp", "fsdp"),
            P("section", "fsdp"),
            P("section", "fsdp", None, "tp"),
            P("section", "tp", "fsdp"),
        ),
        check_vma=False,
    )
```

```python
import jax
import jax.numpy as jnp
from jax import lax
from jax.experimental import pallas as pl
from jax.experimental.pallas import tpu as pltpu
from jax.sharding import PartitionSpec as P

HD = 64
UNITS = 640

epsilon = 1e-06
rope_base = 1000000.0
masked_score = -1000000000.0
low_type = jnp.bfloat16
wide = jnp.float32


def contract(left, right, left_dim, right_dim):
    return lax.dot_general(
        left, right, (((left_dim,), (right_dim,)), ((), ())), preferred_element_type=wide
    )


def turn(value, axis, steps):
    count = lax.axis_size(axis)
    return lax.ppermute(value, axis, [(place, (place + steps) % count) for place in range(count)])


def turn_y(value, steps):
    count = lax.axis_size("fsdp")
    return lax.ppermute(
        value, "fsdp", [(place, (place + 2 * steps) % count) for place in range(count)]
    )


def flip_x(value):
    count = lax.axis_size("fsdp")
    return lax.ppermute(value, "fsdp", [(place, place ^ 1) for place in range(count)])


def collect(blocks, axis):
    count = lax.axis_size(axis)
    order = [1, count - 1] + list(range(2, count - 1))
    total = blocks[0].astype(wide)
    for steps in order:
        total = total + turn(blocks[steps], axis, -steps).astype(wide)
    return total


def pick(array, place, axis):
    return lax.dynamic_index_in_dim(array, place, axis, keepdims=False)


def turn_ctx(block):
    return [turn(block, "ctx", steps) for steps in (1, 3, 2)]


def stack_rows(own, moved):
    former, latter, opposite = moved
    return jnp.concatenate([own, former, opposite, latter], axis=0)


def tensor_sum(partial_value):
    own = lax.optimization_barrier(partial_value.astype(low_type))
    return own.astype(wide) + turn(own, "tp", 1).astype(wide)


def after(value, *others):
    tied = lax.optimization_barrier((value,) + others)
    return tied[0] if not others else tied


def with_column(half, received, column_place):
    pair = jnp.zeros((2,) + half.shape, half.dtype)
    pair = lax.dynamic_update_slice(pair, half[None], (column_place, 0, 0))
    return lax.dynamic_update_slice(pair, received[None], (1 - column_place, 0, 0))


def turn_rows(pair):
    return [turn_y(pair, steps) for steps in (1, 3, 2)]


def swap_all(pieces):
    return [turn(piece, "section", 1) for piece in pieces]


def place_pieces(lines, row_count, places, *refs):
    pieces, outs = refs[:8], refs[8:]
    columns = pieces[0].shape[2]
    for index, piece in enumerate(pieces):
        row = lax.rem(places[0] + 4 - (0, 1, 3, 2)[index % 4], 4)
        half = places[1] if index < 4 else 1 - places[1]
        start = pl.multiple_of(half * columns, 128)
        for column in range(2):
            where = (row * 2 + column, slice(None), pl.ds(start, columns))
            outs[0][where] = piece[column, pl.ds(0, row_count), :]
            if lines:
                outs[1][where] = piece[column, pl.ds(row_count, lines), :]


def put_together(pieces, others, places, lines):
    rows, columns = pieces[0].shape[1:]
    shapes = [jax.ShapeDtypeStruct((8, rows - lines, 2 * columns), low_type)]
    if lines:
        shapes.append(jax.ShapeDtypeStruct((8, lines, 2 * columns), low_type))
    place = jnp.stack([places[1], places[0]]).astype(jnp.int32)
    size = 8 * rows * 2 * columns * 2
    return pl.pallas_call(
        lambda *refs: place_pieces(lines, rows - lines, *refs),
        out_shape=shapes,
        in_specs=[pl.BlockSpec(memory_space=pltpu.SMEM)] + [pl.BlockSpec(memory_space=pltpu.VMEM)] * 8,
        out_specs=[pl.BlockSpec(memory_space=pltpu.VMEM)] * len(shapes),
        compiler_params=pltpu.CompilerParams(vmem_limit_bytes=20 << 20),
        cost_estimate=pl.CostEstimate(flops=0, bytes_accessed=2 * size, transcendentals=0),
    )(place, *pieces, *others)


def attn_weights(pieces, others, places):
    width = 8 * 112
    w_attn, lines = put_together(pieces, others, places, 16)
    lines = lines[:, 0].astype(wide)
    return (
        lines[:, :112].reshape(width),
        lines[:, 128:240].reshape(width),
        jnp.pad(lines[:, 256:328].reshape(576), (0, 64)),
        w_attn.reshape(width, 1024),
    )


def mlp_weights(pieces, others, places):
    return put_together(pieces, others, places, 0)[0].reshape(8 * 112, 2048)


def halves_by_layer(block, section_place):
    columns = block.shape[1] // 2
    kept = lax.dynamic_slice_in_dim(block, section_place * columns, columns, 1)
    sent = lax.dynamic_slice_in_dim(block, (1 - section_place) * columns, columns, 1)
    received = turn(sent, "section", 1)
    first = section_place == 0
    return jnp.where(first, kept, received), jnp.where(first, received, kept)


def rotary_tables(position):
    inverse = rope_base ** (-jnp.arange(0, HD, 2, dtype=wide) / HD)
    angles = position.astype(wide)[..., None] * inverse
    angles = jnp.concatenate([angles, angles], axis=-1)
    return (jnp.cos(angles), jnp.sin(angles))


def rotate(values, cosine, sine):
    half_width = values.shape[-1] // 2
    turned = jnp.concatenate([-values[..., half_width:], values[..., :half_width]], axis=-1)
    return values * cosine + turned * sine


def rotate_back(grads, cosine, sine):
    half_width = grads.shape[-1] // 2
    scaled = grads * sine
    turned = jnp.concatenate([scaled[..., half_width:], -scaled[..., :half_width]], axis=-1)
    return grads * cosine + turned


def norm_backward(grad_normed, resid, scale, gain):
    grad_gain = jnp.sum(grad_normed * resid * scale, axis=0)
    inner = grad_normed * gain
    grad_resid = scale * inner - resid * (scale * scale * scale) * jnp.mean(
        inner * resid, axis=-1, keepdims=True
    )
    return (grad_gain, grad_resid)


def mask_tables(lengths, ctx_place, row_count, ctx_count):
    doc_ends = jnp.cumsum(lengths, axis=-1)
    blocks = (ctx_place - jnp.arange(ctx_count, dtype=jnp.int32)) % ctx_count
    places = (blocks[:, None] * row_count + jnp.arange(row_count, dtype=jnp.int32)).reshape(-1)
    passed = places[:, None] >= doc_ends[None, :]
    segment = jnp.sum(passed.astype(jnp.int32), axis=-1)
    doc_start = jnp.sum(jnp.where(passed, lengths[None, :], 0), axis=-1)
    position = places - doc_start
    cosine, sine = rotary_tables(position[:row_count])
    allowed = (segment[:row_count, None] == segment[None, :]) & (
        places[:row_count, None] >= places[None, :]
    )
    return (allowed, cosine, sine)


def normed(resid, gain):
    scale = lax.rsqrt(jnp.mean(resid * resid, axis=-1, keepdims=True) + epsilon)
    return scale, (resid * scale * gain).astype(low_type)


def forward_attn(layer_in, weights, tables, tie):
    attn_gain, mlp_gain, bias, w_attn = weights
    allowed, cosine, sine = tables
    row_count, width = layer_in.shape
    resid = layer_in.astype(wide)
    scale_one, normed_in = normed(resid, attn_gain)
    projected = jnp.dot(normed_in, w_attn[:, :640], preferred_element_type=wide) + bias
    queries = rotate(
        projected[:, :448].reshape(row_count, 7, HD), cosine[:, None, :], sine[:, None, :]
    ).astype(low_type)
    key_own = rotate(projected[:, 448:512], cosine, sine)
    key_value = jnp.concatenate([key_own, projected[:, 512:576]], axis=1).astype(low_type)
    key_value = tie(stack_rows(key_value, turn_ctx(key_value)))
    key_all, value_all = key_value[:, :HD], key_value[:, HD:]
    scores = jnp.einsum("qgd,td->gqt", queries, key_all, preferred_element_type=wide) * 0.125
    scores = jnp.where(allowed[None], scores, masked_score)
    largest = jnp.max(scores, axis=-1, keepdims=True)
    raised = jnp.exp(scores - largest)
    totals = jnp.sum(raised, axis=-1, keepdims=True)
    log_total = largest + jnp.log(totals)
    probs = (raised / totals).astype(low_type)
    mixed = jnp.einsum("gqt,td->qgd", probs, value_all, preferred_element_type=wide)
    mixed = jnp.pad(mixed.reshape(row_count, 448).astype(low_type), ((0, 0), (64, 0)))
    kept = (resid, scale_one, normed_in, queries, key_all, value_all, log_total, mixed)
    return contract(mixed, w_attn[:, 512:], 1, 1), kept


def forward_mid(branch, resid, mlp_gain):
    middle = resid + tensor_sum(branch)
    return middle, *normed(middle, mlp_gain)


def forward_mlp(normed_mid, w_mlp):
    gate_up = jnp.dot(normed_mid, w_mlp[:, : 2 * UNITS], preferred_element_type=wide)
    hidden = (jax.nn.silu(gate_up[:, :UNITS]) * gate_up[:, UNITS:]).astype(low_type)
    return gate_up, hidden


def forward_down(hidden, w_mlp, row_count):
    branch = contract(hidden, w_mlp[:, 2 * UNITS : 3 * UNITS], 1, 1).astype(low_type)
    return list(branch.reshape(-1, row_count, branch.shape[1]))


def backward_mlp(grad_all, kept, w_mlp):
    middle, scale_two, normed_mid, gate_up, hidden = kept
    row_count, width = middle.shape
    grad_hidden = jnp.dot(grad_all, w_mlp[:, 2 * UNITS : 3 * UNITS], preferred_element_type=wide)
    gate = gate_up[:, :UNITS]
    upward = gate_up[:, UNITS:]
    sigmoid = jax.nn.sigmoid(gate)
    grad_gate = grad_hidden * upward * sigmoid * (1.0 + gate * (1.0 - sigmoid))
    grad_upward = grad_hidden * gate * sigmoid
    grad_gate_up = jnp.concatenate([grad_gate, grad_upward], axis=1).astype(low_type)
    branch = contract(grad_gate_up, w_mlp[:, : 2 * UNITS], 1, 1).astype(low_type)
    branch = branch.reshape(-1, row_count, width)
    grad_mlp = jnp.concatenate(
        [
            contract(normed_mid, grad_gate_up, 0, 0).astype(low_type),
            contract(grad_all, hidden, 0, 0).astype(low_type),
        ],
        axis=1,
    )
    return branch, grad_mlp


def backward_mid(branch, grad_out, kept, mlp_gain):
    middle, scale_two = kept[:2]
    grad_normed_mid = tensor_sum(branch)
    grad_mlp_gain, grad_middle = norm_backward(grad_normed_mid, middle, scale_two, mlp_gain)
    return grad_middle + grad_out.astype(wide), grad_mlp_gain


def backward_attn(grad_middle, kept, weights, tables):
    attn_gain, mlp_gain, bias, w_attn = weights
    allowed, cosine, sine = tables
    resid, scale_one, normed_in, queries, key_all, value_all, log_total, mixed = kept
    row_count, width = resid.shape
    grad_branch = grad_middle.astype(low_type)
    grad_mixed = jnp.dot(grad_branch, w_attn[:, 512:], preferred_element_type=wide)
    grad_mixed = grad_mixed[:, 64:].astype(low_type).reshape(queries.shape)
    scores = jnp.einsum("qgd,td->gqt", queries, key_all, preferred_element_type=wide) * 0.125
    probs = jnp.where(allowed[None], jnp.exp(scores - log_total), 0.0)
    grad_probs = jnp.einsum("qgd,td->gqt", grad_mixed, value_all, preferred_element_type=wide)
    grad_value_all = jnp.einsum(
        "gqt,qgd->td", probs.astype(low_type), grad_mixed, preferred_element_type=wide
    )
    row_delta = jnp.sum(grad_probs * probs, axis=-1, keepdims=True)
    grad_scores = (probs * (grad_probs - row_delta)).astype(low_type)
    grad_queries = (
        jnp.einsum("gqt,td->qgd", grad_scores, key_all, preferred_element_type=wide) * 0.125
    )
    grad_key_all = (
        jnp.einsum("gqt,qgd->td", grad_scores, queries, preferred_element_type=wide) * 0.125
    )
    grad_key_value = jnp.concatenate([grad_key_all, grad_value_all], axis=1).astype(low_type)
    grad_key_value = collect(list(grad_key_value.reshape(-1, row_count, 2 * HD)), "ctx")
    grad_projected = jnp.concatenate(
        [
            rotate_back(grad_queries, cosine[:, None, :], sine[:, None, :]).reshape(row_count, 448),
            rotate_back(grad_key_value[:, :HD], cosine, sine),
            grad_key_value[:, HD:],
            jnp.zeros((row_count, HD), wide),
        ],
        axis=1,
    ).astype(low_type)
    return grad_branch, grad_projected


def backward_in(grad_projected, grad_middle, kept, weights):
    attn_gain, mlp_gain, bias, w_attn = weights
    resid, scale_one = kept[:2]
    grad_normed_in = tensor_sum(contract(grad_projected, w_attn[:, :640], 1, 1))
    grad_attn_gain, grad_resid = norm_backward(grad_normed_in, resid, scale_one, attn_gain)
    return (grad_resid + grad_middle).astype(low_type), grad_attn_gain


def attn_weight_grads(grad_branch, grad_projected, kept):
    normed_in, mixed = kept[2], kept[7]
    grad_bias = jnp.sum(grad_projected.astype(wide), axis=0)
    projection = contract(normed_in, grad_projected, 0, 0)
    output = contract(grad_branch, mixed, 0, 0)
    latter = jnp.pad(projection[:, 512:], ((0, 0), (0, 384))) + output
    return jnp.concatenate([projection[:, :512], latter], axis=1).astype(low_type), grad_bias


def row_blocks(blocks, row_place, axis):
    return [pick(blocks, (row_place + steps) % 4, axis) for steps in (0, 1, 3, 2)]


def send_rows(pieces):
    return [turn_y(piece, steps) for steps, piece in zip((1, 3, 2), pieces)]


def add_all(pieces):
    return sum(piece.astype(wide) for piece in pieces).astype(low_type)


def split_columns(blocks, section_place):
    return pick(blocks, section_place, 1), pick(blocks, 1 - section_place, 1)


def halve(kept, sent):
    return (kept.astype(wide) + turn(sent, "section", 1).astype(wide)).astype(low_type)


def to_column(block):
    hops = []
    for row in range(4):
        hops.append((8 + 2 * row, 8 + 2 * row + 1))
        hops.append((2 * row + 1, 2 * row))
    return lax.ppermute(block, ("section", "fsdp"), hops)


def own_layer(block_zero, block_one, section_place, column_place):
    first = section_place == 0
    hops = []
    for row in range(4):
        hops.append((2 * row, 8 + 2 * row))
        hops.append((8 + 2 * row + 1, 2 * row + 1))
    own = jnp.where(first, block_zero, block_one)
    sent = jnp.where(first, block_one, block_zero)
    received = lax.ppermute(sent, ("section", "fsdp"), hops)
    return jnp.where(section_place == column_place, own, received)


def in_order(pieces, ctx_place):
    own, former, latter, opposite = pieces
    pieces = jnp.stack([own, former, opposite, latter])
    return jnp.stack([pick(pieces, (ctx_place - place) % 4, 0) for place in range(4)])


def pack_lines(small):
    grad_attn_gain, grad_mlp_gain, grad_bias = small
    lines = jnp.concatenate(
        [
            jnp.pad(grad_attn_gain.reshape(8, 112), ((0, 0), (0, 16))),
            jnp.pad(grad_mlp_gain.reshape(8, 112), ((0, 0), (0, 16))),
            jnp.pad(grad_bias[:512].reshape(8, 64), ((0, 0), (0, 64))),
            jnp.pad(grad_bias[512:576].reshape(8, 8), ((0, 0), (0, 632))),
        ],
        axis=1,
    ).astype(low_type)
    return jnp.pad(lines[:, None], ((0, 0), (0, 15), (0, 0))).reshape(4, 2, 16, 1024)


def ctx_blocks(blocks, ctx_place):
    return [
        lax.dynamic_slice_in_dim(blocks, (ctx_place - steps) % 4 * 256, 256, 2)
        for steps in (0, 1, 3, 2)
    ]


def send_ctx(pieces):
    return [turn(piece, "ctx", -steps) for steps, piece in zip((1, 3, 2), pieces)]


def per_device(
    layer_input, cotangent, doc_lengths, attn_gain, w_qkv, b_qkv, w_out, mlp_gain, w_gate_up, w_down
):
    section_place = lax.axis_index("section")
    fsdp_place = lax.axis_index("fsdp")
    row_place, column_place = fsdp_place // 2, fsdp_place % 2
    ctx_place = lax.axis_index("ctx")
    places = (section_place, row_place, column_place, ctx_place)
    row_count, width = layer_input.shape[1:]
    units_all = w_down.shape[1]

    line = jnp.concatenate(
        [
            jnp.pad(attn_gain, ((0, 0), (0, 16))),
            jnp.pad(mlp_gain, ((0, 0), (0, 16))),
            jnp.pad(b_qkv[0], ((0, 0), (0, 696))),
        ],
        axis=1,
    )
    attn_block = jnp.concatenate(
        [
            jnp.concatenate([w_qkv[0, :, 0], w_out[0].T], axis=1),
            jnp.pad(line, ((0, 15), (0, 0))),
        ],
        axis=0,
    )
    past = 4 * UNITS - units_all
    mlp_block = jnp.concatenate(
        [
            jnp.pad(w_gate_up[0], ((0, 0), (0, 0), (0, past))),
            jnp.pad(w_down[0].T, ((0, 0), (0, past)))[:, None],
        ],
        axis=1,
    )
    mlp_block = lax.dynamic_slice_in_dim(mlp_block, ctx_place * UNITS, UNITS, 2)
    mlp_block = jnp.pad(mlp_block.reshape(112, 3 * UNITS), ((0, 0), (0, 128)))

    first = section_place == 0
    layer_in = pick(layer_input, section_place, 0)
    grads_last = pick(cotangent, section_place, 0)
    tables = mask_tables(pick(doc_lengths, section_place, 0)[0], ctx_place, row_count, 4)

    half_attn, late_attn = halves_by_layer(attn_block, section_place)
    half_mlp, late_mlp = halves_by_layer(mlp_block, section_place)
    pair_attn = with_column(half_attn, flip_x(half_attn), column_place)
    pair_attn, half_mlp, grads_last = after(pair_attn, half_mlp, grads_last)
    rows_attn = turn_rows(pair_attn)
    pair_mlp = with_column(half_mlp, flip_x(half_mlp), column_place)
    grads_former = turn(grads_last, "ctx", 1)
    pair_attn, pair_mlp, grads_last, grads_former, *rows_attn = after(
        pair_attn, pair_mlp, grads_last, grads_former, *rows_attn
    )
    moved = [pair_mlp, turn_y(pair_mlp, 1), turn_y(pair_mlp, 3)]
    pieces = [pair_attn] + rows_attn
    weights_zero = attn_weights(pieces, swap_all(pieces), places)

    late = [late_attn, late_mlp]
    grads_moved = [grads_last]

    def tie_zero(key_value):
        key_value, late[0], late[1], grads_moved[0], *moved[:] = after(
            key_value, *late, grads_moved[0], *moved
        )
        grads_moved.extend(turn(grads_moved[0], "ctx", steps) for steps in (3, 2))
        moved.append(turn_y(moved[0], 2))
        late[:] = [with_column(half, flip_x(half), column_place) for half in late]
        return key_value

    branch, kept_attn_zero = forward_attn(layer_in, weights_zero, tables, tie_zero)
    branch, pair_attn, pair_mlp, latter, opposite, *pieces = after(
        branch, *late, *grads_moved[1:], *moved
    )
    grads_all = [grads_former, latter, opposite]
    others = swap_all(pieces)
    middle, scale_two, normed_mid = forward_mid(branch, kept_attn_zero[0], weights_zero[1])
    normed_mid, pair_attn, *pieces = after(normed_mid, pair_attn, *pieces, *others)
    rows_attn = [turn_y(pair_attn, 1), turn_y(pair_attn, 3)]
    w_mlp_zero = mlp_weights(pieces[:4], pieces[4:], places)
    normed_mid = stack_rows(normed_mid, turn_ctx(normed_mid))
    normed_mid, pair_attn, pair_mlp, *rows_attn = after(normed_mid, pair_attn, pair_mlp, *rows_attn)
    rows_attn.append(turn_y(pair_attn, 2))
    gate_up, hidden = forward_mlp(normed_mid, w_mlp_zero)
    kept_mlp_zero = (middle, scale_two, normed_mid, gate_up, hidden)
    branch = collect(forward_down(hidden, w_mlp_zero, row_count), "ctx")
    branch, pair_mlp, *pieces = after(branch, pair_mlp, pair_attn, *rows_attn)
    others = swap_all(pieces)
    former, latter = turn_y(pair_mlp, 1), turn_y(pair_mlp, 3)
    out_zero = (middle + tensor_sum(branch)).astype(low_type)
    out_zero, pair_mlp, former, latter, *rest = after(
        out_zero, pair_mlp, former, latter, *pieces, *others
    )
    moved[:] = [pair_mlp, former, latter, turn_y(pair_mlp, 2)]
    weights_one = attn_weights(rest[:4], rest[4:], places)

    branch, kept_attn_one = forward_attn(out_zero, weights_one, tables, lambda key_value: key_value)
    branch, *pieces = after(branch, *moved)
    others = swap_all(pieces)
    middle, scale_two, normed_mid = forward_mid(branch, kept_attn_one[0], weights_one[1])
    normed_mid, *pieces = after(normed_mid, *pieces, *others)
    w_mlp_one = mlp_weights(pieces[:4], pieces[4:], places)
    grads_all = stack_rows(grads_last, grads_all)
    normed_mid = stack_rows(normed_mid, turn_ctx(normed_mid))
    gate_up, hidden = forward_mlp(normed_mid, w_mlp_one)
    kept_mlp_one = (middle, scale_two, normed_mid, gate_up, hidden)

    mlp_shape = (4, 2, 112, 3 * UNITS)
    attn_shape = (4, 2, 112, 1024)
    branch, mlp_one = backward_mlp(grads_all, kept_mlp_one, w_mlp_one)
    branch = collect(list(branch), "ctx")
    down = forward_down(hidden, w_mlp_one, row_count)
    down = [down[steps] for steps in (0, 1, 3, 2)]
    branch, mlp_keep, mlp_sent, *down = after(
        branch, *split_columns(mlp_one.reshape(mlp_shape), section_place), *down
    )
    down_moved = send_ctx(down[1:])
    mlp_pieces = row_blocks(halve(mlp_keep, mlp_sent), row_place, 0)
    middle_one, gain_one = backward_mid(branch, grads_last, kept_mlp_one, weights_one[1])
    middle_one, *pieces = after(middle_one, down[0], *down_moved, *mlp_pieces)
    down, mlp_pieces = sum(piece.astype(wide) for piece in pieces[:4]), pieces[4:]
    mlp_moved = send_rows(mlp_pieces[1:3])
    branch_one, projected_one = backward_attn(middle_one, kept_attn_one, weights_one, tables)
    grads_one, attn_gain_one = backward_in(projected_one, middle_one, kept_attn_one, weights_one)
    attn_one, bias_one = attn_weight_grads(branch_one, projected_one, kept_attn_one)
    grads_one, *mlp_pieces = after(grads_one, mlp_pieces[0], mlp_pieces[3], *mlp_moved)

    mlp_pieces[1] = turn_y(mlp_pieces[1], 2)
    attn_sums = halve(*split_columns(attn_one.reshape(attn_shape), section_place))
    grads_all = stack_rows(grads_one, turn_ctx(grads_one))
    grads_all, attn_sums, down, attn_gain_one, bias_one, *mlp_pieces = after(
        grads_all, attn_sums, down, attn_gain_one, bias_one, *mlp_pieces
    )
    lines_one = pack_lines((attn_gain_one, gain_one, bias_one))
    line_sums = halve(*split_columns(lines_one, section_place))
    mlp_one = add_all(mlp_pieces)
    mlp_one = add_all([mlp_one, to_column(mlp_one)])
    out_one = (kept_mlp_one[0] + tensor_sum(down)).astype(low_type)
    branch, mlp_zero = backward_mlp(grads_all, kept_mlp_zero, w_mlp_zero)
    branch = collect(list(branch), "ctx")
    branch, mlp_keep, mlp_sent, mlp_one, out_one, *attn_pieces = after(
        branch,
        *split_columns(mlp_zero.reshape(mlp_shape), section_place),
        mlp_one,
        out_one,
        *ctx_blocks(jnp.concatenate([attn_sums, line_sums], axis=1), ctx_place),
    )
    mlp_pieces = row_blocks(halve(mlp_keep, mlp_sent), row_place, 0)
    attn_moved = send_ctx(attn_pieces[1:])
    middle_zero, gain_zero = backward_mid(branch, grads_one, kept_mlp_zero, weights_zero[1])
    middle_zero, *pieces = after(middle_zero, attn_pieces[0], *attn_moved, *mlp_pieces)
    attn_one, mlp_pieces = add_all(pieces[:4]), pieces[4:]
    mlp_moved = send_rows(mlp_pieces[1:3])
    branch_zero, projected_zero = backward_attn(middle_zero, kept_attn_zero, weights_zero, tables)
    projected_zero, *pieces = after(projected_zero, mlp_pieces[0], mlp_pieces[3], *mlp_moved)
    mlp_pieces = [pieces[0], pieces[2], pieces[3], turn_y(pieces[1], 2)]
    attn_zero, bias_zero = attn_weight_grads(branch_zero, projected_zero, kept_attn_zero)
    attn_sums = halve(*split_columns(attn_zero.reshape(attn_shape), section_place))
    attn_pieces = ctx_blocks(attn_sums, ctx_place)
    attn_moved = send_ctx(attn_pieces[1:])
    grads_zero, attn_gain_zero = backward_in(
        projected_zero, middle_zero, kept_attn_zero, weights_zero
    )
    attn_gain_zero, *mlp_pieces = after(attn_gain_zero, *mlp_pieces)

    mlp_zero = add_all(mlp_pieces)
    mlp_moved = to_column(mlp_zero)
    lines_zero = pack_lines((attn_gain_zero, gain_zero, bias_zero))
    line_pieces = ctx_blocks(halve(*split_columns(lines_zero, section_place)), ctx_place)
    line_moved = send_ctx(line_pieces[1:])
    attn_zero = jnp.concatenate(
        [add_all([attn_pieces[0]] + attn_moved), add_all([line_pieces[0]] + line_moved)], axis=1
    )
    attn_zero, mlp_zero, mlp_moved = after(attn_zero, mlp_zero, mlp_moved)
    mlp_zero = add_all([mlp_zero, mlp_moved])
    mlp = own_layer(mlp_zero, mlp_one, section_place, column_place)
    attn_pieces = row_blocks(jnp.stack([attn_zero, attn_one]), row_place, 1)
    mlp, *attn_pieces = after(mlp, *attn_pieces)
    mlp_all = [turn(mlp, "ctx", 1), turn(mlp, "ctx", 3)]
    attn_both = add_all(attn_pieces[:1] + send_rows(attn_pieces[1:]))
    attn_both, mlp, *mlp_all = after(attn_both, mlp, *mlp_all)
    mlp_all.append(turn(mlp, "ctx", 2))
    attn_both = add_all([attn_both, to_column(attn_both)])
    attn = own_layer(attn_both[0], attn_both[1], section_place, column_place)
    attn_all = [turn(attn, "ctx", 1), turn(attn, "ctx", 3)]
    attn, mlp, *rest = after(attn, mlp, *mlp_all, *attn_all)
    mlp_all, attn_all = rest[:3], rest[3:] + [turn(attn, "ctx", 2)]
    mlp = in_order([mlp] + mlp_all, ctx_place).reshape(4, 112, 3, UNITS)
    gate_up = mlp[:, :, :2].transpose(1, 2, 0, 3).reshape(112, 2, 4 * UNITS)[:, :, :units_all]
    down = mlp[:, :, 2].transpose(0, 2, 1).reshape(4 * UNITS, 112)[:units_all]
    attn = in_order([attn] + attn_all, ctx_place)
    outputs = [out_zero, out_one]

    def by_layer(values):
        own = jnp.where(first, values[0], values[1])
        other = turn(jnp.where(first, values[1], values[0]), "section", 1)
        return jnp.where(first, jnp.stack([own, other]), jnp.stack([other, own]))[None]

    hidden_states = by_layer(outputs)
    input_grads = by_layer([grads_zero, grads_one])
    attn = attn.transpose(1, 0, 2).reshape(128, 1024).astype(wide)
    lines = attn[112:113]
    return (
        hidden_states,
        input_grads,
        lines[:, :112],
        attn[None, :112, None, :576],
        lines[None, :, 256:320],
        lines[None, :, 384:392],
        attn[:112, 576:].T[None],
        lines[:, 128:240],
        gate_up.astype(wide)[None],
        down.astype(wide)[None],
    )


def solution(mesh):
    return jax.shard_map(
        per_device,
        mesh=mesh,
        in_specs=(
            P(None, ("fsdp", "ctx"), None),
            P(None, ("fsdp", "ctx"), None),
            P(None, "fsdp", None),
            P("section", "fsdp"),
            P("section", "fsdp", "tp", None),
            P("section", "tp", "fsdp"),
            P("section", "tp", "fsdp"),
            P("section", "fsdp"),
            P("section", "fsdp", None, "tp"),
            P("section", "tp", "fsdp"),
        ),
        out_specs=(
            P("section", None, ("fsdp", "ctx"), None),
            P("section", None, ("fsdp", "ctx"), None),
            P("section", "fsdp"),
            P("section", "fsdp", "tp", None),
            P("section", "tp", "fsdp"),
            P("section", "tp", "fsdp"),
            P("section", "tp", "fsdp"),
            P("section", "fsdp"),
            P("section", "fsdp", None, "tp"),
            P("section", "tp", "fsdp"),
        ),
        check_vma=False,
    )
```
